32 devices in a mesh: chaos: 8 (over y, x, core), slab: 4 (over z).
Axes of the slice: x: 2, y: 2, z: 4, core: 2. Of those that a mesh axis runs over, the one named last changes fastest.
Arguments:
- displacement: float32 [288, 3, 3072], P('chaos', None, 'slab'), may hold values from -1.5 to 1.5
- load: float32 [288, 3, 3072], P('chaos', None, 'slab'), may hold values from -12 to 12
- mean_modulus: float32 [3072], P('slab'), may hold values from 0.5 to 2
- modes: float32 [10, 3072], P(None, 'slab'), may hold values from -0.6 to 0.6
- owner: int32 [288], replicated, may hold values from 0 to 287, each once
Outputs:
- solution: float32 [288, 3, 3072], P('chaos', None, 'slab')
- residual: float32 [288, 3, 3072], P('chaos', None, 'slab')
The draws below stay inside these ranges and needn't reach their ends.
Inputs may be any that keep to these rules, and one draw needn't show every extreme that they name: `owner`: each value appears exactly once. Slot s lies on device s // 36 of the chaos axis; values of 286 or more mark empty slots.
All inputs are finite; a program needn't handle non-finite values.
Results may differ from the reference program's by a relative error of at most 0.0003.
Values sent between devices are 32-bit elements; how exact they have to be, the bound alone decides.
No kernel may reach another device: no remote copies, remote signals or barrier semaphores. Data moves between devices by JAX's collectives and lax.ppermute only.
A program may use at most 128 MiB of HBM per device.

```python
import math
import jax
import jax.numpy as jnp
import numpy as np

NX = 24
NY = 32
KL = 10
DEG = 3
SWEEPS = 4
ITERS = 2
NZ = 4
SLOTS = 288


def level_of(stream_key, shape, cuts, smallest, high):
    def one(axis_at, shards_of):
        draws = jax.random.uniform(jax.random.fold_in(jax.random.fold_in(stream_key, 6), axis_at), (shards_of,), jnp.float32, smallest / len(cuts), high / len(cuts))
        return jnp.repeat(jnp.exp(draws), shape[axis_at] // shards_of).reshape((-1,) + (1,) * (len(shape) - axis_at - 1))

    factor_of = one(*cuts[0])
    for cut in cuts[1:]:
        factor_of = factor_of * one(*cut)
    return factor_of


def centred(own_key, shape, scale, reach, cuts=(), held_as=jnp.bfloat16):
    drawn = scale * jax.random.normal(own_key, shape, jnp.float32)
    if cuts:
        drawn = drawn * level_of(own_key, shape, cuts, -0.22, 0.18)
    return jnp.clip(drawn, -reach, reach).astype(held_as)


def setup_inputs(seed: int = 0) -> dict:
    seeds = jax.random.split(jax.random.key(seed), 6)
    return {
        "displacement": centred(seeds[0], (SLOTS, 3, NZ * NX * NY), 0.25, 1.5, ((0, 8), (2, 4)), jnp.float32),
        "load": centred(seeds[1], (SLOTS, 3, NZ * NX * NY), 2.0, 12.0, ((0, 8), (2, 4)), jnp.float32),
        "mean_modulus": jnp.clip(jnp.exp(math.log(2.0) - 1.3862944 * jax.random.uniform(seeds[2], (NZ * NX * NY,), jnp.float32) ** level_of(seeds[2], (NZ * NX * NY,), ((0, 4),), -0.2, 0.2)), 0.5, 2.0),
        "modes": centred(seeds[3], (KL, NZ * NX * NY), 0.15, 0.6, ((1, 4),), jnp.float32),
        "owner": jax.random.permutation(seeds[4], SLOTS).astype(jnp.int32),
    }


bound_high = 50.0
bound_low = 2.5

def multi_indices():
    listing = [[]]
    for variable in range(KL):
        extended_list = []
        for prefix in listing:
            for degree in range(DEG + 1 - sum(prefix)):
                extended_list.append(prefix + [degree])
        listing = extended_list
    return listing

def chaos_tables():
    listing = multi_indices()
    lookup = {tuple(multi_entry): number for number, multi_entry in enumerate(listing)}
    number_all = len(listing)
    up_index = np.full((number_all, KL), number_all, np.int32)
    up_weight = np.zeros((number_all, KL), np.float32)
    down_index = np.full((number_all, KL), number_all, np.int32)
    down_weight = np.zeros((number_all, KL), np.float32)
    for number, multi_entry in enumerate(listing):
        for variable in range(KL):
            raised = list(multi_entry)
            raised[variable] += 1
            if tuple(raised) in lookup:
                up_index[number, variable] = lookup[tuple(raised)]
                up_weight[number, variable] = math.sqrt(multi_entry[variable] + 1)
            if multi_entry[variable] > 0:
                lowered = list(multi_entry)
                lowered[variable] -= 1
                down_index[number, variable] = lookup[tuple(lowered)]
                down_weight[number, variable] = math.sqrt(multi_entry[variable])
    return (up_index, up_weight, down_index, down_weight)

def slot_neighbours(owner):
    up_index, up_weight, down_index, down_weight = chaos_tables()
    number_all = up_index.shape[0]
    live_slots = owner < number_all
    clipped = jnp.minimum(owner, number_all - 1)
    inverse = jnp.argsort(owner).astype(jnp.int32)

    def to_slots(index_table, weight_table):
        targets = jnp.asarray(index_table)[clipped]
        present = (targets < number_all) & live_slots[:, None]
        slots_of = inverse[jnp.minimum(targets, number_all - 1)]
        weights = jnp.where(present, jnp.asarray(weight_table)[clipped], 0.0)
        return (jnp.where(present, slots_of, 0).astype(jnp.int32), weights.astype(jnp.float32))
    return (to_slots(up_index, up_weight), to_slots(down_index, down_weight), live_slots)

def plane_masks(length):
    position = jnp.arange(length, dtype=jnp.int32)
    return (position // NY % NX, position % NY)

def forward_flat(values, step_size, keep):
    shifted = jnp.concatenate([values[..., step_size:], jnp.zeros_like(values[..., :step_size])], axis=-1)
    return jnp.where(keep, shifted, 0.0) - values

def backward_flat(values, step_size, keep):
    shifted = jnp.concatenate([jnp.zeros_like(values[..., :step_size]), values[..., :-step_size]], axis=-1)
    return values - jnp.where(keep, shifted, 0.0)

def stiffness_flat(fields, modulus):
    plane_size = NX * NY
    lowered = [field_one[..., :-plane_size] for field_one in fields]
    raised = [field_one[..., plane_size:] for field_one in fields]
    across_x, along_y = plane_masks(lowered[0].shape[-1])
    inner_x, inner_y = plane_masks(lowered[0].shape[-1] - plane_size)

    def slope_of(component, direction):
        if direction == 2:
            return raised[component] - lowered[component]
        if direction == 0:
            return forward_flat(lowered[component], NY, across_x != NX - 1)
        return forward_flat(lowered[component], 1, along_y != NY - 1)
    spread = slope_of(0, 0) + slope_of(1, 1) + slope_of(2, 2)
    results = []
    for component in range(3):
        summed = 0.0
        for direction in range(3):
            gradient = slope_of(component, direction)
            if direction == component:
                gradient = gradient + spread
            flux_term = modulus * gradient
            if direction == 2:
                summed = summed + (flux_term[..., plane_size:] - flux_term[..., :-plane_size])
            elif direction == 0:
                summed = summed + backward_flat(flux_term[..., plane_size:], NY, inner_x != 0)
            else:
                summed = summed + backward_flat(flux_term[..., plane_size:], 1, inner_y != 0)
        results.append(-summed)
    return results

def chebyshev(residual_in, apply_mean):
    center_value = 0.5 * (bound_high + bound_low)
    half_width = 0.5 * (bound_high - bound_low)
    ratio_value = center_value / half_width
    update = residual_in / center_value
    increment = update
    rho_prev = 1.0 / ratio_value
    for sweep_turn in range(SWEEPS):
        rho_next = 1.0 / (2.0 * ratio_value - rho_prev)
        increment = rho_next * rho_prev * increment + 2.0 * rho_next / half_width * (residual_in - apply_mean(update))
        update = update + increment
        rho_prev = rho_next
    return update

def reference(displacement, load, mean_modulus, modes, owner):
    plane_size = NX * NY
    (slot_up, weight_up), (slot_down, weight_down), live_slots = slot_neighbours(owner)
    keep_mask = live_slots[:, None, None]
    solution = jnp.where(keep_mask, displacement, 0.0)
    target = jnp.where(keep_mask, load, 0.0)
    moduli = jnp.concatenate([mean_modulus[None], modes], axis=0)
    moduli_ext = jnp.concatenate([jnp.zeros_like(moduli[:, :plane_size]), moduli], axis=1)

    def stiffness_global(field_in, modulus_ext):
        padded = jnp.pad(field_in, ((0, 0), (0, 0), (plane_size, plane_size)))
        return jnp.stack(stiffness_flat([padded[:, component] for component in range(3)], modulus_ext), axis=1)

    def operator(field_in):
        summed = stiffness_global(jnp.where(live_slots[:, None, None], field_in, 0.0), moduli_ext[0])
        for term_index in range(KL):
            mixed_terms = weight_up[:, term_index][:, None, None] * field_in[slot_up[:, term_index]]
            mixed_terms = mixed_terms + weight_down[:, term_index][:, None, None] * field_in[slot_down[:, term_index]]
            summed = summed + stiffness_global(mixed_terms, moduli_ext[term_index + 1])
        return summed

    def apply_mean(field_in):
        return stiffness_global(field_in, moduli_ext[0])
    residual = target
    for iteration in range(ITERS):
        residual = target - operator(solution)
        solution = solution + chebyshev(residual, apply_mean)
    return (solution, residual)
```

```python
import functools
import math

import jax
import jax.numpy as jnp
import numpy as np
from jax import lax
from jax.experimental import pallas as pl
from jax.experimental.pallas import tpu as pltpu
from jax.sharding import PartitionSpec as P

NX = 24
NY = 32
KL = 10
DEG = 3
SWEEPS = 4
PLANE = NX * NY
FIELDS = KL + 1

bound_high = 50.0
bound_low = 2.5
VMEM_LIMIT = 60 * 1024 * 1024
F32 = jnp.float32
BF16 = jnp.bfloat16


def up8(count):
    return -(-count // 8) * 8


def multi_indices():
    listing = [[]]
    for variable in range(KL):
        extended_list = []
        for prefix in listing:
            for degree in range(DEG + 1 - sum(prefix)):
                extended_list.append(prefix + [degree])
        listing = extended_list
    return listing


def edge_tables():
    listing = multi_indices()
    lookup = {tuple(entry): number for number, entry in enumerate(listing)}
    low, raised, level = [], [], []
    for number, entry in enumerate(listing):
        if sum(entry) == DEG:
            continue
        low.append(number)
        for variable in range(KL):
            other = list(entry)
            other[variable] += 1
            raised.append(lookup[tuple(other)])
            level.append(entry[variable])
    return len(listing), np.array(low, np.int32), np.array(raised, np.int32), np.array(level, np.int32)


class Plan:
    def __init__(self, chaos, slab, slots_dev):
        self.chaos, self.slab, self.slots_dev = chaos, slab, slots_dev
        self.n = chaos * slab
        self.nz = slab
        self.sp = -(-slots_dev // slab)
        self.hs = up8(self.sp)
        self.ls = self.nz * NY
        best = None
        for tx in range(1, 7):
            for ty in range(1, NY + 1):
                if NX % tx or NY % ty or (NX // tx) * (NY // ty) > self.n:
                    continue
                lanes = -(-3 * self.nz * (ty + 2) // 128) * 128
                rows = up8((self.sp - 1) * (tx + 2) + 8)
                key = (-(NX // tx) * (NY // ty), rows * lanes)
                if best is None or key < best[0]:
                    best = (key, tx, ty, lanes, rows)
        _, self.tx, self.ty, self.lanes, self.rows_in = best
        self.rx = self.tx + 2
        self.ry = self.ty + 2
        self.nxb, self.nyb = NX // self.tx, NY // self.ty
        self.rows_out = up8(self.sp * self.tx)
        self.rows_start = up8(6 * self.sp + 16)
        self.rows_end = up8(6 * self.sp)
        self.positions = self.n * self.sp

    def pack_table(self):
        table = np.zeros((3 * self.ls, self.nyb * self.lanes), np.float32)
        for c in range(3):
            for z in range(self.nz):
                for yb in range(self.nyb):
                    for k in range(self.ry):
                        y = yb * self.ty - 1 + k
                        if 0 <= y < NY:
                            table[
                                c * self.ls + z * NY + y,
                                yb * self.lanes + (c * self.nz + z) * self.ry + k,
                            ] = 1
        return table

    def unpack_table(self):
        table = np.zeros((self.nyb * self.lanes, 3 * self.ls), np.float32)
        for c in range(3):
            for z in range(self.nz):
                for y in range(NY):
                    yb, k = y // self.ty, y % self.ty + 1
                    table[
                        yb * self.lanes + (c * self.nz + z) * self.ry + k, c * self.ls + z * NY + y
                    ] = 1
        return table

    def modulus_table(self):
        table = np.zeros((self.nyb, self.ls, self.lanes), np.float32)
        for yb in range(self.nyb):
            for z in range(self.nz):
                for k in range(self.ry):
                    y = yb * self.ty - 1 + k
                    if 0 <= y < NY:
                        for c in range(3):
                            table[yb, z * NY + y, (c * self.nz + z) * self.ry + k] = 1
        return table


def picked(values, table):
    high = values.astype(BF16)
    rest = values - high.astype(F32)
    middle = rest.astype(BF16)
    low = (rest - middle.astype(F32)).astype(BF16)
    return (
        jnp.dot(high, table, preferred_element_type=F32)
        + jnp.dot(middle, table, preferred_element_type=F32)
        + jnp.dot(low, table, preferred_element_type=F32)
    )


def pick_into(out_ref, values_ref, table_ref):
    width = table_ref.shape[1]
    chunk = width if width <= 1024 else 512
    for first in range(0, width, chunk):
        out_ref[:, first : first + chunk] = picked(values_ref[...], table_ref[:, first : first + chunk])


def swap_quarters(parts):
    quarter = lax.broadcasted_iota(jnp.int32, parts[0].shape, 1) // NY
    swapped = []
    for j in range(4):
        total = parts[j]
        for i in range(4):
            if i != j:
                turned = pltpu.roll(parts[i], (i - j) % 4 * NY, 1)
                total = jnp.where(quarter == i, turned, total)
        swapped.append(total)
    return swapped


def strided(start, size, step):
    return pl.ds(start, size) if size == 1 or step == 1 else pl.ds(start, size, stride=step)


def store_message(plan, rows_ref, msg_ref):
    blank = jnp.zeros((8, plan.lanes), F32)
    for tile in range(plan.n):
        if tile >= plan.nxb * plan.nyb:
            msg_ref[tile] = jnp.zeros((plan.rows_in, plan.lanes), F32)
            continue
        xb, yb = divmod(tile, plan.nyb)
        msg_ref[tile, plan.rows_in - 8 :, :] = blank
        for k in range(plan.rx):
            x = xb * plan.tx - 1 + k
            if 0 <= x < NX:
                rows = rows_ref[
                    x * plan.hs : x * plan.hs + plan.sp, yb * plan.lanes : (yb + 1) * plan.lanes
                ]
            else:
                rows = jnp.zeros((plan.sp, plan.lanes), F32)
            msg_ref[tile, strided(k, plan.sp, plan.rx), :] = rows


def start_kernel(plan, tile_ref, in_ref, pack_ref, mtab_ref, msg_ref, load_ref, mean_ref, mods_ref, lhs, rows, fields):
    fields[0] = jnp.zeros((16, plan.ls), F32)
    fields[NX + 1] = jnp.zeros((16, plan.ls), F32)

    def slabs_of(first, count, a):
        out = [[] for _ in range(4)]
        for t in range(plan.nz // 4):
            parts = [in_ref[4 * t + i, first : first + count, a * 128 : (a + 1) * 128] for i in range(4)]
            for b, piece in enumerate(swap_quarters(parts)):
                out[b].append(piece)
        return [piece[0] if len(piece) == 1 else jnp.concatenate(piece, axis=1) for piece in out]

    for a in range(PLANE // 128):
        for c in range(3):
            for b, piece in enumerate(slabs_of(c * plan.sp, plan.hs, a)):
                x = 4 * a + b
                lhs[x * plan.hs : (x + 1) * plan.hs, c * plan.ls : (c + 1) * plan.ls] = piece
            for b, piece in enumerate(slabs_of((3 + c) * plan.sp, plan.hs, a)):
                load_ref[4 * a + b, c] = piece
        for b, piece in enumerate(slabs_of(6 * plan.sp, 16, a)):
            fields[4 * a + b + 1] = piece
            mean_ref[4 * a + b : 4 * a + b + 1, :] = piece[0:1]
    pick_into(rows, lhs, pack_ref)
    store_message(plan, rows, msg_ref)
    tile = jnp.minimum(tile_ref[0], plan.nxb * plan.nyb - 1)
    xb, yb = tile // plan.nyb, tile % plan.nyb
    table = mtab_ref[yb]
    mods_ref[...] = jnp.zeros(mods_ref.shape, F32)
    for k in range(plan.rx):
        here = picked(fields[xb * plan.tx + k], table)
        for v in range(FIELDS):
            mods_ref[v, k : k + 1, :] = here[v : v + 1]


def mix_kernel(plan, low_count, nodes_ref, level_ref, msg_ref, mods_ref, out_ref, grad, flux, scaled):
    sp, rx, ry, nz, lanes = plan.sp, plan.rx, plan.ry, plan.nz, plan.lanes
    segment = nz * ry
    lane = lax.broadcasted_iota(jnp.int32, (8, lanes), 1)
    part, height = lane // segment, lane % segment // ry
    not_top, not_bottom = height != nz - 1, height != 0
    is_x, is_y, is_z = part == 0, part == 1, part == 2
    for level in range(DEG):
        for v in range(KL):
            scaled[level * KL + v] = mods_ref[v + 1] * math.sqrt(level + 1)
    mean = mods_ref[0]

    def gradients(source, carry):
        for s in range(sp):
            own = msg_ref[source, s * rx : s * rx + 8, :]
            slope_x = pltpu.roll(own, 7, 0) - own
            slope_y = pltpu.roll(own, lanes - 1, 1) - own
            slope_z = jnp.where(not_top, pltpu.roll(own, lanes - ry, 1), 0.0) - own
            spread = slope_x + pltpu.roll(slope_y, lanes - segment, 1) + pltpu.roll(slope_z, lanes - 2 * segment, 1)
            full_x = slope_x + jnp.where(is_x, spread, 0.0)
            full_y = slope_y + jnp.where(is_y, pltpu.roll(spread, segment, 1), 0.0)
            full_z = slope_z + jnp.where(is_z, pltpu.roll(spread, 2 * segment, 1), 0.0)
            at = source * sp + s
            for d, full in enumerate((full_x, full_y, full_z)):
                grad[at, d] = full
                flux[at, d] = mean * full
        return carry

    lax.fori_loop(0, plan.n, gradients, 0)

    def edges(number, carry):
        base = nodes_ref[number]
        own = [grad[base, d] for d in range(3)]
        total = [flux[base, d] for d in range(3)]
        for group in range(0, KL, 5):
            at = [nodes_ref[low_count + number * KL + v] for v in range(group, group + 5)]
            field = [scaled[level_ref[number * KL + v] * KL + v] for v in range(group, group + 5)]
            fresh = [
                [flux[spot, d] + weight * own[d] for d in range(3)] for spot, weight in zip(at, field)
            ]
            for spot, weight in zip(at, field):
                total = [total[d] + weight * grad[spot, d] for d in range(3)]
            for spot, values in zip(at, fresh):
                for d in range(3):
                    flux[spot, d] = values[d]
        for d in range(3):
            flux[base, d] = total[d]
        return carry

    lax.fori_loop(0, low_count, edges, 0)

    def divergences(source, carry):
        for s in range(sp):
            at = source * sp + s
            flux_x, flux_y, flux_z = (flux[at, d] for d in range(3))
            total = flux_x - pltpu.roll(flux_x, 1, 0)
            total = total + (flux_y - pltpu.roll(flux_y, 1, 1))
            total = total + (flux_z - jnp.where(not_bottom, pltpu.roll(flux_z, ry, 1), 0.0))
            out_ref[source, s * plan.tx : (s + 1) * plan.tx, :] = total[1 : 1 + plan.tx]
        return carry

    lax.fori_loop(0, plan.n, divergences, 0)


def unpack_image(plan, image_ref, unpack_ref, lhs, rows):
    for xb in range(plan.nxb):
        for k in range(plan.tx):
            x = xb * plan.tx + k
            for yb in range(plan.nyb):
                lhs[x * plan.hs : x * plan.hs + plan.sp, yb * plan.lanes : (yb + 1) * plan.lanes] = image_ref[
                    xb * plan.nyb + yb, strided(k, plan.sp, plan.tx), :
                ]
    pick_into(rows, lhs, unpack_ref)


def smooth(plan, base_ref, live_ref, mean_ref, rows, residual_ref, update, step):
    hs, ls = plan.hs, plan.ls
    live = live_ref[...] != 0.0
    center_value = 0.5 * (bound_high + bound_low)
    half_width = 0.5 * (bound_high - bound_low)
    ratio_value = center_value / half_width
    lane = lax.broadcasted_iota(jnp.int32, (hs, ls), 1)
    at_y, at_z = lane % NY, lane // NY
    not_y_end, not_y_start = at_y != NY - 1, at_y != 0
    not_z_end, not_z_start = at_z != plan.nz - 1, at_z != 0

    def first(x, carry):
        for c in range(3):
            image = rows[pl.ds(pl.multiple_of(x * hs, hs), hs), c * ls : (c + 1) * ls]
            value = jnp.where(live, base_ref[x, c] + image, 0.0)
            residual_ref[x, c] = value
            scaled = value * (1.0 / center_value)
            update[x, c] = scaled
            step[x, c] = scaled
        return carry

    lax.fori_loop(0, NX, first, 0)
    for c in range(3):
        update[NX, c] = jnp.zeros((hs, ls), F32)

    rho_prev = 1.0 / ratio_value
    for sweep in range(SWEEPS):
        rho_next = 1.0 / (2.0 * ratio_value - rho_prev)
        keep, gain = rho_next * rho_prev, 2.0 * rho_next / half_width

        def slab_of(x, carry, keep=keep, gain=gain):
            behind, own = carry[:3], carry[3:]
            modulus = jnp.broadcast_to(mean_ref[pl.ds(x, 1), :], (hs, ls))
            ahead = [update[x + 1, c] for c in range(3)]
            slope_x = [ahead[c] - own[c] for c in range(3)]
            slope_y = [jnp.where(not_y_end, pltpu.roll(own[c], ls - 1, 1), 0.0) - own[c] for c in range(3)]
            slope_z = [jnp.where(not_z_end, pltpu.roll(own[c], ls - NY, 1), 0.0) - own[c] for c in range(3)]
            spread = slope_x[0] + slope_y[1] + slope_z[2]
            slope_x[0] = slope_x[0] + spread
            slope_y[1] = slope_y[1] + spread
            slope_z[2] = slope_z[2] + spread
            through = []
            for c in range(3):
                flux_x, flux_y, flux_z = (modulus * slope[c] for slope in (slope_x, slope_y, slope_z))
                through.append(flux_x)
                total = flux_x - behind[c]
                total = total + (flux_y - jnp.where(not_y_start, pltpu.roll(flux_y, 1, 1), 0.0))
                total = total + (flux_z - jnp.where(not_z_start, pltpu.roll(flux_z, NY, 1), 0.0))
                moved = keep * step[x, c] + gain * (residual_ref[x, c] + total)
                step[x, c] = moved
                update[x, c] = own[c] + moved
            return (*through, *ahead)

        zero = jnp.zeros((hs, ls), F32)
        lax.fori_loop(0, NX, slab_of, (zero, zero, zero, *(update[0, c] for c in range(3))), unroll=2)
        rho_prev = rho_next


def middle_kernel(plan, image_ref, base_ref, live_ref, mean_ref, unpack_ref, pack_ref, msg_ref, residual_ref, update_ref, wide, narrow, step):
    unpack_image(plan, image_ref, unpack_ref, wide, narrow)
    smooth(plan, base_ref, live_ref, mean_ref, narrow, residual_ref, update_ref, step)
    for x in range(NX):
        for c in range(3):
            narrow[x * plan.hs : (x + 1) * plan.hs, c * plan.ls : (c + 1) * plan.ls] = update_ref[x, c]
    pick_into(wide, narrow, pack_ref)
    store_message(plan, wide, msg_ref)


def end_kernel(plan, image_ref, base_ref, live_ref, mean_ref, unpack_ref, before_ref, out_ref, lhs_in, rows_in, residual, update, step):
    unpack_image(plan, image_ref, unpack_ref, lhs_in, rows_in)
    smooth(plan, base_ref, live_ref, mean_ref, rows_in, residual, update, step)
    sp = plan.sp

    def spread_out(values, first, a):
        for t in range(plan.nz // 4):
            parts = [value[:, t * 128 : (t + 1) * 128] for value in values]
            for i, piece in enumerate(swap_quarters(parts)):
                out_ref[4 * t + i, first : first + sp, a * 128 : (a + 1) * 128] = piece[:sp]

    for a in range(PLANE // 128):
        for c in range(3):
            spread_out([update[4 * a + b, c] + before_ref[4 * a + b, c] for b in range(4)], c * sp, a)
            spread_out([residual[4 * a + b, c] for b in range(4)], (3 + c) * sp, a)


def per_device(displacement, load, mean_modulus, modes, owner):
    chaos, slab = lax.axis_size("chaos"), lax.axis_size("slab")
    slots_dev, slots_all = displacement.shape[0], owner.shape[0]
    plan = Plan(chaos, slab, slots_dev)
    n, sp, hs, ls, lanes = plan.n, plan.sp, plan.hs, plan.ls, plan.lanes
    count, low, raised, level = edge_tables()
    at_chaos, at_slab = lax.axis_index("chaos"), lax.axis_index("slab")

    slots = np.arange(slots_all)
    places = (slots // slots_dev) * (slab * sp) + slots % slots_dev
    wanted = np.concatenate([low, raised])
    nodes = jnp.sum(
        jnp.where(wanted[:, None] == owner[None, :], jnp.asarray(places, jnp.int32)[None, :], 0), axis=1
    ).astype(jnp.int32)
    live_all = owner < count
    live_own = lax.dynamic_slice_in_dim(live_all, at_chaos * slots_dev, slots_dev, 0)
    live_here = jnp.pad(live_own.astype(F32), (0, slab * sp - slots_dev))
    live_here = lax.dynamic_slice_in_dim(live_here, at_slab * sp, sp, 0)
    live_here = jnp.broadcast_to(jnp.pad(live_here, (0, hs - sp))[:, None], (hs, ls))

    pack = jnp.asarray(plan.pack_table(), BF16)
    unpack = jnp.asarray(plan.unpack_table(), BF16)
    mtab = jnp.asarray(plan.modulus_table(), BF16)
    tile = (at_chaos * slab + at_slab).astype(jnp.int32).reshape(1)

    def by_slab(values):
        values = jnp.pad(values, ((0, slab * sp - slots_dev), (0, 0), (0, 0)))
        return jnp.transpose(values.reshape(slab, sp, 3, PLANE), (0, 2, 1, 3)).reshape(slab, 3 * sp, PLANE)

    moduli = jnp.concatenate([mean_modulus[None], modes], axis=0)
    outgoing = jnp.concatenate(
        [by_slab(displacement), by_slab(load), jnp.broadcast_to(moduli[None], (slab, FIELDS, PLANE))], axis=1
    )
    outgoing = jnp.pad(outgoing, ((0, 0), (0, plan.rows_start - outgoing.shape[1]), (0, 0)))
    incoming = lax.all_to_all(outgoing, "slab", 0, 0, tiled=True)

    smem = pl.BlockSpec(memory_space=pltpu.SMEM)
    vmem = pl.BlockSpec(memory_space=pltpu.VMEM)
    params = pltpu.CompilerParams(vmem_limit_bytes=VMEM_LIMIT)
    message = jax.ShapeDtypeStruct((n, plan.rows_in, lanes), F32)
    image = jax.ShapeDtypeStruct((n, plan.rows_out, lanes), F32)
    grid_field = jax.ShapeDtypeStruct((NX, 3, hs, ls), F32)
    grid_more = jax.ShapeDtypeStruct((NX + 1, 3, hs, ls), F32)
    wide = pltpu.VMEM((NX * hs, plan.nyb * lanes), F32)
    narrow = pltpu.VMEM((NX * hs, 3 * ls), F32)

    def everyone(values):
        return lax.all_to_all(values, ("chaos", "slab"), 0, 0, tiled=True)

    msg, load_s, mean_s, mods = pl.pallas_call(
        functools.partial(start_kernel, plan),
        out_shape=(
            message,
            grid_field,
            jax.ShapeDtypeStruct((NX, ls), F32),
            jax.ShapeDtypeStruct((FIELDS, 8, lanes), F32),
        ),
        in_specs=[smem, vmem, vmem, vmem],
        out_specs=(vmem,) * 4,
        scratch_shapes=[narrow, wide, pltpu.VMEM((NX + 2, 16, ls), F32)],
        compiler_params=params,
        name="start",
    )(tile, incoming, pack, mtab)

    def mixed(values):
        return pl.pallas_call(
            functools.partial(mix_kernel, plan, len(low)),
            out_shape=image,
            in_specs=[smem, smem, vmem, vmem],
            out_specs=vmem,
            scratch_shapes=[
                pltpu.VMEM((plan.positions, 3, 8, lanes), F32),
                pltpu.VMEM((plan.positions, 3, 8, lanes), F32),
                pltpu.VMEM((DEG * KL, 8, lanes), F32),
            ],
            compiler_params=params,
            name="mix",
        )(nodes, jnp.asarray(level, jnp.int32), values, mods)

    first_image = everyone(mixed(everyone(msg)))
    msg, residual_s, update_s = pl.pallas_call(
        functools.partial(middle_kernel, plan),
        out_shape=(message, grid_field, grid_more),
        in_specs=[vmem] * 6,
        out_specs=(vmem,) * 3,
        scratch_shapes=[wide, narrow, pltpu.VMEM((NX, 3, hs, ls), F32)],
        compiler_params=params,
        name="middle",
    )(first_image, load_s, live_here, mean_s, unpack, pack)

    second_image = everyone(mixed(everyone(msg)))
    ending = pl.pallas_call(
        functools.partial(end_kernel, plan),
        out_shape=jax.ShapeDtypeStruct((slab, plan.rows_end, PLANE), F32),
        in_specs=[vmem] * 6,
        out_specs=vmem,
        scratch_shapes=[
            wide,
            narrow,
            pltpu.VMEM((NX, 3, hs, ls), F32),
            pltpu.VMEM((NX + 1, 3, hs, ls), F32),
            pltpu.VMEM((NX, 3, hs, ls), F32),
        ],
        compiler_params=params,
        name="end",
    )(second_image, residual_s, live_here, mean_s, unpack, update_s)
    final = lax.all_to_all(ending, "slab", 0, 0, tiled=True)

    def by_slot(values):
        values = jnp.transpose(values.reshape(slab, 3, sp, PLANE), (0, 2, 1, 3))
        return values.reshape(slab * sp, 3, PLANE)[:slots_dev]

    start = jnp.where(live_own[:, None, None], displacement, 0.0)
    return (start + by_slot(final[:, : 3 * sp]), by_slot(final[:, 3 * sp : 6 * sp]))


def solution(mesh):
    in_specs = (P("chaos", None, "slab"), P("chaos", None, "slab"), P("slab"), P(None, "slab"), P())
    out_specs = (P("chaos", None, "slab"), P("chaos", None, "slab"))
    return jax.shard_map(
        per_device, mesh=mesh, in_specs=in_specs, out_specs=out_specs, check_vma=False
    )
```

```python
import functools
import math

import jax
import jax.numpy as jnp
import numpy as np
from jax import lax
from jax.experimental import pallas as pl
from jax.experimental.pallas import tpu as pltpu
from jax.sharding import PartitionSpec as P

NX = 24
NY = 32
KL = 10
DEG = 3
SWEEPS = 4
PLANE = NX * NY
FIELDS = KL + 1

bound_high = 50.0
bound_low = 2.5
MIB = 1024 * 1024
F32 = jnp.float32
BF16 = jnp.bfloat16


def up8(count):
    return -(-count // 8) * 8


def multi_indices():
    listing = [[]]
    for variable in range(KL):
        extended_list = []
        for prefix in listing:
            for degree in range(DEG + 1 - sum(prefix)):
                extended_list.append(prefix + [degree])
        listing = extended_list
    return listing


def edge_tables():
    listing = multi_indices()
    lookup = {tuple(entry): number for number, entry in enumerate(listing)}
    low, raised, level = [], [], []
    for number, entry in enumerate(listing):
        if sum(entry) == DEG:
            continue
        low.append(number)
        for variable in range(KL):
            other = list(entry)
            other[variable] += 1
            raised.append(lookup[tuple(other)])
            level.append(entry[variable])
    return len(listing), np.array(low, np.int32), np.array(raised, np.int32), np.array(level, np.int32)


class Plan:
    def __init__(self, chaos, slab, slots_dev):
        self.chaos, self.slab, self.slots_dev = chaos, slab, slots_dev
        self.n = chaos * slab
        self.nz = slab
        self.sp = -(-slots_dev // slab)
        self.hs = up8(self.sp)
        self.ls = self.nz * NY
        best = None
        for tx in range(1, 7):
            for ty in range(1, NY + 1):
                if NX % tx or NY % ty or (NX // tx) * (NY // ty) > self.n:
                    continue
                lanes = -(-3 * self.nz * (ty + 2) // 128) * 128
                rows = up8((self.sp - 1) * (tx + 2) + 8)
                key = (-(NX // tx) * (NY // ty), rows * lanes)
                if best is None or key < best[0]:
                    best = (key, tx, ty, lanes, rows)
        _, self.tx, self.ty, self.lanes, self.rows_in = best
        self.rx = self.tx + 2
        self.ry = self.ty + 2
        self.nxb, self.nyb = NX // self.tx, NY // self.ty
        self.rows_out = up8(self.sp * self.tx)
        self.rows_flat = up8(3 * self.sp)
        self.positions = self.n * self.sp

    def pack_table(self):
        table = np.zeros((3 * self.ls, self.nyb * self.lanes), np.float32)
        for c in range(3):
            for z in range(self.nz):
                for yb in range(self.nyb):
                    for k in range(self.ry):
                        y = yb * self.ty - 1 + k
                        if 0 <= y < NY:
                            table[
                                c * self.ls + z * NY + y,
                                yb * self.lanes + (c * self.nz + z) * self.ry + k,
                            ] = 1
        return table

    def unpack_table(self):
        table = np.zeros((self.nyb * self.lanes, 3 * self.ls), np.float32)
        for c in range(3):
            for z in range(self.nz):
                for y in range(NY):
                    yb, k = y // self.ty, y % self.ty + 1
                    table[
                        yb * self.lanes + (c * self.nz + z) * self.ry + k, c * self.ls + z * NY + y
                    ] = 1
        return table

    def modulus_table(self):
        table = np.zeros((self.nyb, self.ls, self.lanes), np.float32)
        for yb in range(self.nyb):
            for z in range(self.nz):
                for k in range(self.ry):
                    y = yb * self.ty - 1 + k
                    if 0 <= y < NY:
                        for c in range(3):
                            table[yb, z * NY + y, (c * self.nz + z) * self.ry + k] = 1
        return table


def picked(values, table):
    high = values.astype(BF16)
    rest = values - high.astype(F32)
    middle = rest.astype(BF16)
    low = (rest - middle.astype(F32)).astype(BF16)
    return (
        jnp.dot(high, table, preferred_element_type=F32)
        + jnp.dot(middle, table, preferred_element_type=F32)
        + jnp.dot(low, table, preferred_element_type=F32)
    )


def pick_into(out_ref, values_ref, table_ref):
    width = table_ref.shape[1]
    chunk = width if width <= 1024 else 512
    for first in range(0, width, chunk):
        out_ref[:, first : first + chunk] = picked(values_ref[...], table_ref[:, first : first + chunk])


def swap_quarters(parts):
    quarter = lax.broadcasted_iota(jnp.int32, parts[0].shape, 1) // NY
    swapped = []
    for j in range(4):
        total = parts[j]
        for i in range(4):
            if i != j:
                turned = pltpu.roll(parts[i], (i - j) % 4 * NY, 1)
                total = jnp.where(quarter == i, turned, total)
        swapped.append(total)
    return swapped


def strided(start, size, step):
    return pl.ds(start, size) if size == 1 or step == 1 else pl.ds(start, size, stride=step)


def store_message(plan, rows_ref, msg_ref):
    blank = jnp.zeros((8, plan.lanes), F32)
    for tile in range(plan.n):
        if tile >= plan.nxb * plan.nyb:
            msg_ref[tile] = jnp.zeros((plan.rows_in, plan.lanes), F32)
            continue
        xb, yb = divmod(tile, plan.nyb)
        msg_ref[tile, plan.rows_in - 8 :, :] = blank
        for k in range(plan.rx):
            x = xb * plan.tx - 1 + k
            if 0 <= x < NX:
                rows = rows_ref[
                    x * plan.hs : x * plan.hs + plan.sp, yb * plan.lanes : (yb + 1) * plan.lanes
                ]
            else:
                rows = jnp.zeros((plan.sp, plan.lanes), F32)
            msg_ref[tile, strided(k, plan.sp, plan.rx), :] = rows


def rows_at(piece_of):
    return [jnp.concatenate(pieces, axis=1) if len(pieces) > 1 else pieces[0] for pieces in zip(*piece_of)]


def start_kernel(plan, in_ref, pack_ref, msg_ref, lhs, rows):
    for a in range(PLANE // 128):
        for c in range(3):
            pieces = rows_at(
                swap_quarters(
                    [
                        in_ref[c, (4 * t + i) * plan.sp : (4 * t + i + 1) * plan.sp, a * 128 : (a + 1) * 128]
                        for i in range(4)
                    ]
                )
                for t in range(plan.slab // 4)
            )
            for b, piece in enumerate(pieces):
                x = 4 * a + b
                lhs[x * plan.hs : x * plan.hs + plan.sp, c * plan.ls : (c + 1) * plan.ls] = piece
    pick_into(rows, lhs, pack_ref)
    store_message(plan, rows, msg_ref)


def split_kernel(plan, in_ref, out_ref):
    for group in range(plan.slab):
        for c in range(3):
            out_ref[group, c * plan.sp : (c + 1) * plan.sp, :] = in_ref[
                c, group * plan.sp : (group + 1) * plan.sp, :
            ]


def load_kernel(plan, in_ref, out_ref):
    for a in range(PLANE // 128):
        for c in range(3):
            pieces = rows_at(
                swap_quarters(
                    [in_ref[4 * t + i, c * plan.sp : (c + 1) * plan.sp, a * 128 : (a + 1) * 128] for i in range(4)]
                )
                for t in range(plan.nz // 4)
            )
            for b, piece in enumerate(pieces):
                out_ref[4 * a + b, c, 0 : plan.sp, :] = piece


def join_kernel(plan, in_ref, out_ref):
    for group in range(plan.slab):
        for c in range(3):
            out_ref[c, group * plan.sp : (group + 1) * plan.sp, :] = in_ref[
                group, c * plan.sp : (c + 1) * plan.sp, :
            ]


def add_kernel(plan, in_ref, live_ref, start_ref, out_ref):
    for group in range(plan.slab):
        here = slice(group * plan.sp, (group + 1) * plan.sp)
        live = jnp.broadcast_to(live_ref[here, :], (plan.sp, PLANE)) != 0.0
        for c in range(3):
            out_ref[c, here, :] = jnp.where(live, start_ref[c, here, :], 0.0) + in_ref[
                group, c * plan.sp : (c + 1) * plan.sp, :
            ]


def moduli_kernel(plan, tile_ref, in_ref, mtab_ref, mean_ref, mods_ref, fields):
    fields[0] = jnp.zeros((16, plan.ls), F32)
    fields[NX + 1] = jnp.zeros((16, plan.ls), F32)
    for a in range(PLANE // 128):
        pieces = rows_at(
            swap_quarters([in_ref[4 * t + i, :, a * 128 : (a + 1) * 128] for i in range(4)])
            for t in range(plan.nz // 4)
        )
        for b, piece in enumerate(pieces):
            fields[4 * a + b + 1] = piece
            mean_ref[4 * a + b : 4 * a + b + 1, :] = piece[0:1]
    tile = jnp.minimum(tile_ref[0], plan.nxb * plan.nyb - 1)
    xb, yb = tile // plan.nyb, tile % plan.nyb
    table = mtab_ref[yb]
    mods_ref[...] = jnp.zeros(mods_ref.shape, F32)
    for k in range(plan.rx):
        here = picked(fields[xb * plan.tx + k], table)
        for v in range(FIELDS):
            mods_ref[v, k : k + 1, :] = here[v : v + 1]


def regrouped(plan, msg_ref, out_ref):
    lane = lax.broadcasted_iota(jnp.int32, (plan.rows_in, plan.lanes), 1)
    height = lane % (plan.nz * plan.ry) // plan.ry

    def one(row, carry):
        parts = [msg_ref[row * plan.slab + z] for z in range(plan.nz)]
        for group in range(plan.slab):
            total = parts[group]
            for z in range(plan.nz):
                if z != group:
                    turned = pltpu.roll(parts[z], (z - group) * plan.ry % plan.lanes, 1)
                    total = jnp.where(height == z, turned, total)
            out_ref[row * plan.slab + group] = total
        return carry

    lax.fori_loop(0, plan.chaos, one, 0)


def first_mix_kernel(plan, low_count, nodes_ref, level_ref, msg_ref, mods_ref, out_ref, grad, flux, scaled, regroup):
    regrouped(plan, msg_ref, regroup)
    mix_kernel(plan, low_count, nodes_ref, level_ref, regroup, mods_ref, out_ref, grad, flux, scaled)


def mix_kernel(plan, low_count, nodes_ref, level_ref, msg_ref, mods_ref, out_ref, grad, flux, scaled):
    sp, rx, ry, nz, lanes = plan.sp, plan.rx, plan.ry, plan.nz, plan.lanes
    segment = nz * ry
    lane = lax.broadcasted_iota(jnp.int32, (8, lanes), 1)
    part, height = lane // segment, lane % segment // ry
    not_top, not_bottom = height != nz - 1, height != 0
    is_x, is_y, is_z = part == 0, part == 1, part == 2
    for level in range(DEG):
        for v in range(KL):
            scaled[level * KL + v] = mods_ref[v + 1] * math.sqrt(level + 1)
    mean = mods_ref[0]

    def gradients(source, carry):
        for s in range(sp):
            own = msg_ref[source, s * rx : s * rx + 8, :]
            slope_x = pltpu.roll(own, 7, 0) - own
            slope_y = pltpu.roll(own, lanes - 1, 1) - own
            slope_z = jnp.where(not_top, pltpu.roll(own, lanes - ry, 1), 0.0) - own
            spread = slope_x + pltpu.roll(slope_y, lanes - segment, 1) + pltpu.roll(slope_z, lanes - 2 * segment, 1)
            full_x = slope_x + jnp.where(is_x, spread, 0.0)
            full_y = slope_y + jnp.where(is_y, pltpu.roll(spread, segment, 1), 0.0)
            full_z = slope_z + jnp.where(is_z, pltpu.roll(spread, 2 * segment, 1), 0.0)
            at = source * sp + s
            for d, full in enumerate((full_x, full_y, full_z)):
                grad[at, d] = full
                flux[at, d] = mean * full
        return carry

    lax.fori_loop(0, plan.n, gradients, 0)

    def edges(number, carry):
        base = nodes_ref[number]
        own = [grad[base, d] for d in range(3)]
        total = [flux[base, d] for d in range(3)]
        for group in range(0, KL, 5):
            at = [nodes_ref[low_count + number * KL + v] for v in range(group, group + 5)]
            field = [scaled[level_ref[number * KL + v] * KL + v] for v in range(group, group + 5)]
            fresh = [
                [flux[spot, d] + weight * own[d] for d in range(3)] for spot, weight in zip(at, field)
            ]
            for spot, weight in zip(at, field):
                total = [total[d] + weight * grad[spot, d] for d in range(3)]
            for spot, values in zip(at, fresh):
                for d in range(3):
                    flux[spot, d] = values[d]
        for d in range(3):
            flux[base, d] = total[d]
        return carry

    lax.fori_loop(0, low_count, edges, 0)

    def divergences(source, carry):
        for s in range(sp):
            at = source * sp + s
            flux_x, flux_y, flux_z = (flux[at, d] for d in range(3))
            total = flux_x - pltpu.roll(flux_x, 1, 0)
            total = total + (flux_y - pltpu.roll(flux_y, 1, 1))
            total = total + (flux_z - jnp.where(not_bottom, pltpu.roll(flux_z, ry, 1), 0.0))
            out_ref[source, s * plan.tx : (s + 1) * plan.tx, :] = total[1 : 1 + plan.tx]
        return carry

    lax.fori_loop(0, plan.n, divergences, 0)


def unpack_image(plan, image_ref, unpack_ref, lhs, rows):
    for xb in range(plan.nxb):
        for k in range(plan.tx):
            x = xb * plan.tx + k
            for yb in range(plan.nyb):
                lhs[x * plan.hs : x * plan.hs + plan.sp, yb * plan.lanes : (yb + 1) * plan.lanes] = image_ref[
                    xb * plan.nyb + yb, strided(k, plan.sp, plan.tx), :
                ]
    pick_into(rows, lhs, unpack_ref)


def add_image(plan, base_ref, live_ref, rows, residual_ref):
    live = live_ref[...] != 0.0

    def one(x, carry):
        for c in range(3):
            image = rows[pl.ds(pl.multiple_of(x * plan.hs, plan.hs), plan.hs), c * plan.ls : (c + 1) * plan.ls]
            residual_ref[x, c] = jnp.where(live, base_ref[x, c] + image, 0.0)
        return carry

    lax.fori_loop(0, NX, one, 0)


def smooth(plan, mean_ref, residual_ref, update, step):
    hs, ls = plan.hs, plan.ls
    center_value = 0.5 * (bound_high + bound_low)
    half_width = 0.5 * (bound_high - bound_low)
    ratio_value = center_value / half_width
    lane = lax.broadcasted_iota(jnp.int32, (hs, ls), 1)
    at_y, at_z = lane % NY, lane // NY
    not_y_end, not_y_start = at_y != NY - 1, at_y != 0
    not_z_end, not_z_start = at_z != plan.nz - 1, at_z != 0

    def first(x, carry):
        for c in range(3):
            scaled = residual_ref[x, c] * (1.0 / center_value)
            update[x, c] = scaled
            step[x, c] = scaled
        return carry

    lax.fori_loop(0, NX, first, 0)
    for c in range(3):
        update[NX, c] = jnp.zeros((hs, ls), F32)

    rho_prev = 1.0 / ratio_value
    for sweep in range(SWEEPS):
        rho_next = 1.0 / (2.0 * ratio_value - rho_prev)
        keep, gain = rho_next * rho_prev, 2.0 * rho_next / half_width

        def slab_of(x, carry, keep=keep, gain=gain):
            behind, own = carry[:3], carry[3:]
            modulus = jnp.broadcast_to(mean_ref[pl.ds(x, 1), :], (hs, ls))
            ahead = [update[x + 1, c] for c in range(3)]
            slope_x = [ahead[c] - own[c] for c in range(3)]
            slope_y = [jnp.where(not_y_end, pltpu.roll(own[c], ls - 1, 1), 0.0) - own[c] for c in range(3)]
            slope_z = [jnp.where(not_z_end, pltpu.roll(own[c], ls - NY, 1), 0.0) - own[c] for c in range(3)]
            spread = slope_x[0] + slope_y[1] + slope_z[2]
            slope_x[0] = slope_x[0] + spread
            slope_y[1] = slope_y[1] + spread
            slope_z[2] = slope_z[2] + spread
            through = []
            for c in range(3):
                flux_x, flux_y, flux_z = (modulus * slope[c] for slope in (slope_x, slope_y, slope_z))
                through.append(flux_x)
                total = flux_x - behind[c]
                total = total + (flux_y - jnp.where(not_y_start, pltpu.roll(flux_y, 1, 1), 0.0))
                total = total + (flux_z - jnp.where(not_z_start, pltpu.roll(flux_z, NY, 1), 0.0))
                moved = keep * step[x, c] + gain * (residual_ref[x, c] + total)
                step[x, c] = moved
                update[x, c] = own[c] + moved
            return (*through, *ahead)

        zero = jnp.zeros((hs, ls), F32)
        lax.fori_loop(0, NX, slab_of, (zero, zero, zero, *(update[0, c] for c in range(3))), unroll=2)
        rho_prev = rho_next


def middle_kernel(plan, image_ref, base_ref, live_ref, mean_ref, unpack_ref, pack_ref, msg_ref, residual_ref, update_ref, wide, narrow, step):
    unpack_image(plan, image_ref, unpack_ref, wide, narrow)
    add_image(plan, base_ref, live_ref, narrow, residual_ref)
    smooth(plan, mean_ref, residual_ref, update_ref, step)
    for x in range(NX):
        for c in range(3):
            narrow[x * plan.hs : (x + 1) * plan.hs, c * plan.ls : (c + 1) * plan.ls] = update_ref[x, c]
    pick_into(wide, narrow, pack_ref)
    store_message(plan, wide, msg_ref)


def flat_rows(plan, values, out_ref, c, a):
    for t in range(plan.nz // 4):
        parts = [value[:, t * 128 : (t + 1) * 128] for value in values]
        for i, piece in enumerate(swap_quarters(parts)):
            out_ref[4 * t + i, c * plan.sp : (c + 1) * plan.sp, a * 128 : (a + 1) * 128] = piece[: plan.sp]


def residual_kernel(plan, image_ref, base_ref, live_ref, unpack_ref, residual_ref, out_ref, wide, narrow):
    unpack_image(plan, image_ref, unpack_ref, wide, narrow)
    add_image(plan, base_ref, live_ref, narrow, residual_ref)
    for a in range(PLANE // 128):
        for c in range(3):
            flat_rows(plan, [residual_ref[4 * a + b, c] for b in range(4)], out_ref, c, a)


def end_kernel(plan, residual_ref, mean_ref, before_ref, out_ref, update, step):
    smooth(plan, mean_ref, residual_ref, update, step)
    for a in range(PLANE // 128):
        for c in range(3):
            flat_rows(plan, [update[4 * a + b, c] + before_ref[4 * a + b, c] for b in range(4)], out_ref, c, a)


def per_device(displacement, load, mean_modulus, modes, owner):
    chaos, slab = lax.axis_size("chaos"), lax.axis_size("slab")
    slots_dev, slots_all = displacement.shape[0], owner.shape[0]
    plan = Plan(chaos, slab, slots_dev)
    n, sp, hs, ls, lanes = plan.n, plan.sp, plan.hs, plan.ls, plan.lanes
    count, low, raised, level = edge_tables()
    at_chaos, at_slab = lax.axis_index("chaos"), lax.axis_index("slab")

    slots = np.arange(slots_all)
    places = (slots // slots_dev) * (slab * sp) + slots % slots_dev
    wanted = np.concatenate([low, raised])
    nodes = jnp.sum(
        jnp.where(wanted[:, None] == owner[None, :], jnp.asarray(places, jnp.int32)[None, :], 0), axis=1
    ).astype(jnp.int32)
    live_all = owner < count
    live_own = lax.dynamic_slice_in_dim(live_all, at_chaos * slots_dev, slots_dev, 0)
    live_here = jnp.pad(live_own.astype(F32), (0, slab * sp - slots_dev))
    live_here = lax.dynamic_slice_in_dim(live_here, at_slab * sp, sp, 0)
    live_here = jnp.broadcast_to(jnp.pad(live_here, (0, hs - sp))[:, None], (hs, ls))

    pack = jnp.asarray(plan.pack_table(), BF16)
    unpack = jnp.asarray(plan.unpack_table(), BF16)
    mtab = jnp.asarray(plan.modulus_table(), BF16)
    tile = (at_chaos * slab + at_slab).astype(jnp.int32).reshape(1)

    slots_pad = slab * sp

    def by_component(values):
        return jnp.pad(jnp.transpose(values, (1, 0, 2)), ((0, 0), (0, slots_pad - slots_dev), (0, 0)))

    def everyone(values):
        return lax.all_to_all(values, ("chaos", "slab"), 0, 0, tiled=True)

    def column(values):
        return lax.all_to_all(values, "slab", 0, 0, tiled=True)

    smem = pl.BlockSpec(memory_space=pltpu.SMEM)
    vmem = pl.BlockSpec(memory_space=pltpu.VMEM)

    def call(kernel, name, in_specs, out_shape, scratch_shapes):
        return pl.pallas_call(
            kernel,
            out_shape=out_shape,
            in_specs=in_specs,
            out_specs=jax.tree.map(lambda _: vmem, out_shape),
            scratch_shapes=scratch_shapes,
            compiler_params=pltpu.CompilerParams(vmem_limit_bytes=(16 if plan.positions <= 512 and n <= 64 else 60) * MIB),
            name=name,
        )

    def array(*shape):
        return jax.ShapeDtypeStruct(shape, F32)

    message, image = array(n, plan.rows_in, lanes), array(n, plan.rows_out, lanes)
    grid_field, grid_more = array(NX, 3, hs, ls), array(NX + 1, 3, hs, ls)
    wide = pltpu.VMEM((NX * hs, plan.nyb * lanes), F32)
    narrow = pltpu.VMEM((NX * hs, 3 * ls), F32)
    field_scratch, more_scratch = pltpu.VMEM(grid_field.shape, F32), pltpu.VMEM(grid_more.shape, F32)

    moduli = jnp.concatenate([mean_modulus[None], modes], axis=0)
    moduli = lax.all_gather(jnp.pad(moduli, ((0, 16 - FIELDS), (0, 0))), "slab", axis=0)
    mean_s, mods = call(
        functools.partial(moduli_kernel, plan),
        "moduli",
        [smem, vmem, vmem],
        (array(NX, ls), array(FIELDS, 8, lanes)),
        [pltpu.VMEM((NX + 2, 16, ls), F32)],
    )(tile, moduli, mtab)

    msg = call(functools.partial(start_kernel, plan), "start", [vmem, vmem], message, [narrow, wide])(
        by_component(displacement), pack
    )

    def mixed(values, first):
        scratch = [
            pltpu.VMEM((plan.positions, 3, 8, lanes), F32),
            pltpu.VMEM((plan.positions, 3, 8, lanes), F32),
            pltpu.VMEM((DEG * KL, 8, lanes), F32),
        ]
        kernel = mix_kernel
        if first:
            kernel = first_mix_kernel
            scratch.append(pltpu.VMEM((n, plan.rows_in, lanes), F32))
        return call(
            functools.partial(kernel, plan, len(low)), "mix", [smem, smem, vmem, vmem], image, scratch
        )(nodes, jnp.asarray(level, jnp.int32), values, mods)

    arrived = everyone(msg)
    flat, parts = array(slab, plan.rows_flat, PLANE), array(3, slots_pad, PLANE)
    load_flat = call(functools.partial(split_kernel, plan), "split", [vmem], flat, [])(by_component(load))
    load_flat, nodes, mean_s, mods = lax.optimization_barrier((load_flat, nodes, mean_s, mods))
    load_flat, arrived = lax.optimization_barrier((load_flat, arrived))
    load_s = call(functools.partial(load_kernel, plan), "load", [vmem], grid_field, [])(column(load_flat))
    first_image = everyone(mixed(arrived, True))
    msg, residual_s, update_s = call(
        functools.partial(middle_kernel, plan),
        "middle",
        [vmem] * 6,
        (message, grid_field, grid_more),
        [wide, narrow, field_scratch],
    )(first_image, load_s, live_here, mean_s, unpack, pack)

    second_image = everyone(mixed(everyone(msg), False))
    residual_s, residual_flat = call(
        functools.partial(residual_kernel, plan), "residual", [vmem] * 4, (grid_field, flat), [wide, narrow]
    )(second_image, residual_s, live_here, unpack)
    residual = column(residual_flat)
    update_flat = call(
        functools.partial(end_kernel, plan), "end", [vmem] * 3, flat, [more_scratch, field_scratch]
    )(residual_s, mean_s, update_s)
    residual = call(functools.partial(join_kernel, plan), "join", [vmem], parts, [])(residual)
    live_pad = jnp.pad(live_own.astype(F32), (0, slots_pad - slots_dev))
    total = call(functools.partial(add_kernel, plan), "add", [vmem] * 3, parts, [])(
        column(update_flat), jnp.broadcast_to(live_pad[:, None], (slots_pad, 128))[:, :1], by_component(displacement)
    )
    return tuple(jnp.transpose(values, (1, 0, 2))[:slots_dev] for values in (total, residual))


def solution(mesh):
    in_specs = (P("chaos", None, "slab"), P("chaos", None, "slab"), P("slab"), P(None, "slab"), P())
    out_specs = (P("chaos", None, "slab"), P("chaos", None, "slab"))
    return jax.shard_map(
        per_device, mesh=mesh, in_specs=in_specs, out_specs=out_specs, check_vma=False
    )
```

```python
import functools
import math

import jax
import jax.numpy as jnp
import numpy as np
from jax import lax
from jax.experimental import pallas as pl
from jax.experimental.pallas import tpu as pltpu
from jax.sharding import PartitionSpec as P

NX = 24
NY = 32
KL = 10
DEG = 3
SWEEPS = 4
PLANE = NX * NY
FIELDS = KL + 1

bound_high = 50.0
bound_low = 2.5
MIB = 1024 * 1024
F32 = jnp.float32
BF16 = jnp.bfloat16


def up8(count):
    return -(-count // 8) * 8


def multi_indices():
    listing = [[]]
    for variable in range(KL):
        extended_list = []
        for prefix in listing:
            for degree in range(DEG + 1 - sum(prefix)):
                extended_list.append(prefix + [degree])
        listing = extended_list
    return listing


def edge_tables():
    listing = multi_indices()
    lookup = {tuple(entry): number for number, entry in enumerate(listing)}
    low, raised, level = [], [], []
    for number, entry in enumerate(listing):
        if sum(entry) == DEG:
            continue
        low.append(number)
        for variable in range(KL):
            other = list(entry)
            other[variable] += 1
            raised.append(lookup[tuple(other)])
            level.append(entry[variable])
    return len(listing), np.array(low, np.int32), np.array(raised, np.int32), np.array(level, np.int32)


class Plan:
    def __init__(self, chaos, slab, slots_dev):
        self.chaos, self.slab, self.slots_dev = chaos, slab, slots_dev
        self.n = chaos * slab
        self.nz = slab
        self.sp = -(-slots_dev // slab)
        self.hs = up8(self.sp)
        self.ls = self.nz * NY
        best = None
        for tx in range(1, 7):
            for ty in range(1, NY + 1):
                if NX % tx or NY % ty or (NX // tx) * (NY // ty) > self.n:
                    continue
                lanes = -(-3 * self.nz * (ty + 2) // 128) * 128
                rows = up8((self.sp - 1) * (tx + 2) + 8)
                key = (-(NX // tx) * (NY // ty), rows * lanes)
                if best is None or key < best[0]:
                    best = (key, tx, ty, lanes, rows)
        _, self.tx, self.ty, self.lanes, self.rows_in = best
        self.rx = self.tx + 2
        self.ry = self.ty + 2
        self.nxb, self.nyb = NX // self.tx, NY // self.ty
        self.rows_out = up8(self.sp * self.tx)
        self.rows_flat = up8(3 * self.sp)
        self.positions = self.n * self.sp

    def pack_table(self):
        table = np.zeros((3 * self.ls, self.nyb * self.lanes), np.float32)
        for c in range(3):
            for z in range(self.nz):
                for yb in range(self.nyb):
                    for k in range(self.ry):
                        y = yb * self.ty - 1 + k
                        if 0 <= y < NY:
                            table[
                                c * self.ls + z * NY + y,
                                yb * self.lanes + (c * self.nz + z) * self.ry + k,
                            ] = 1
        return table

    def unpack_table(self):
        table = np.zeros((self.nyb * self.lanes, 3 * self.ls), np.float32)
        for c in range(3):
            for z in range(self.nz):
                for y in range(NY):
                    yb, k = y // self.ty, y % self.ty + 1
                    table[
                        yb * self.lanes + (c * self.nz + z) * self.ry + k, c * self.ls + z * NY + y
                    ] = 1
        return table

    def modulus_table(self):
        table = np.zeros((self.nyb, self.ls, self.lanes), np.float32)
        for yb in range(self.nyb):
            for z in range(self.nz):
                for k in range(self.ry):
                    y = yb * self.ty - 1 + k
                    if 0 <= y < NY:
                        for c in range(3):
                            table[yb, z * NY + y, (c * self.nz + z) * self.ry + k] = 1
        return table


def picked(values, table):
    high = values.astype(BF16)
    rest = values - high.astype(F32)
    middle = rest.astype(BF16)
    low = (rest - middle.astype(F32)).astype(BF16)
    return (
        jnp.dot(high, table, preferred_element_type=F32)
        + jnp.dot(middle, table, preferred_element_type=F32)
        + jnp.dot(low, table, preferred_element_type=F32)
    )


def pick_into(out_ref, values_ref, table_ref):
    width = table_ref.shape[1]
    chunk = width if width <= 1024 else 512
    for first in range(0, width, chunk):
        out_ref[:, first : first + chunk] = picked(values_ref[...], table_ref[:, first : first + chunk])


def swap_quarters(parts):
    quarter = lax.broadcasted_iota(jnp.int32, parts[0].shape, 1) // NY
    swapped = []
    for j in range(4):
        total = parts[j]
        for i in range(4):
            if i != j:
                turned = pltpu.roll(parts[i], (i - j) % 4 * NY, 1)
                total = jnp.where(quarter == i, turned, total)
        swapped.append(total)
    return swapped


def strided(start, size, step):
    return pl.ds(start, size) if size == 1 or step == 1 else pl.ds(start, size, stride=step)


def store_message(plan, rows_ref, msg_ref):
    blank = jnp.zeros((8, plan.lanes), F32)
    for tile in range(plan.n):
        if tile >= plan.nxb * plan.nyb:
            msg_ref[tile] = jnp.zeros((plan.rows_in, plan.lanes), F32)
            continue
        xb, yb = divmod(tile, plan.nyb)
        msg_ref[tile, plan.rows_in - 8 :, :] = blank
        for k in range(plan.rx):
            x = xb * plan.tx - 1 + k
            if 0 <= x < NX:
                rows = rows_ref[
                    x * plan.hs : x * plan.hs + plan.sp, yb * plan.lanes : (yb + 1) * plan.lanes
                ]
            else:
                rows = jnp.zeros((plan.sp, plan.lanes), F32)
            msg_ref[tile, strided(k, plan.sp, plan.rx), :] = rows


def rows_at(piece_of):
    return [jnp.concatenate(pieces, axis=1) if len(pieces) > 1 else pieces[0] for pieces in zip(*piece_of)]


def start_kernel(plan, in_ref, pack_ref, msg_ref, lhs, rows):
    for a in range(PLANE // 128):
        for c in range(3):
            pieces = rows_at(
                swap_quarters(
                    [
                        in_ref[c, (4 * t + i) * plan.sp : (4 * t + i + 1) * plan.sp, a * 128 : (a + 1) * 128]
                        for i in range(4)
                    ]
                )
                for t in range(plan.slab // 4)
            )
            for b, piece in enumerate(pieces):
                x = 4 * a + b
                lhs[x * plan.hs : x * plan.hs + plan.sp, c * plan.ls : (c + 1) * plan.ls] = piece
    pick_into(rows, lhs, pack_ref)
    store_message(plan, rows, msg_ref)


def split_kernel(plan, in_ref, out_ref):
    for group in range(plan.slab):
        for c in range(3):
            out_ref[group, c * plan.sp : (c + 1) * plan.sp, :] = in_ref[
                c, group * plan.sp : (group + 1) * plan.sp, :
            ]


def load_kernel(plan, in_ref, out_ref):
    for a in range(PLANE // 128):
        for c in range(3):
            pieces = rows_at(
                swap_quarters(
                    [in_ref[4 * t + i, c * plan.sp : (c + 1) * plan.sp, a * 128 : (a + 1) * 128] for i in range(4)]
                )
                for t in range(plan.nz // 4)
            )
            for b, piece in enumerate(pieces):
                out_ref[4 * a + b, c, 0 : plan.sp, :] = piece


def join_kernel(plan, in_ref, out_ref):
    for group in range(plan.slab):
        for c in range(3):
            out_ref[c, group * plan.sp : (group + 1) * plan.sp, :] = in_ref[
                group, c * plan.sp : (c + 1) * plan.sp, :
            ]


def add_kernel(plan, in_ref, live_ref, start_ref, out_ref):
    for group in range(plan.slab):
        here = slice(group * plan.sp, (group + 1) * plan.sp)
        live = jnp.broadcast_to(live_ref[here, :], (plan.sp, PLANE)) != 0.0
        for c in range(3):
            out_ref[c, here, :] = jnp.where(live, start_ref[c, here, :], 0.0) + in_ref[
                group, c * plan.sp : (c + 1) * plan.sp, :
            ]


def moduli_kernel(plan, tile_ref, in_ref, mtab_ref, mean_ref, mods_ref, fields):
    from_plane = [lax.rem(tile_ref[1] + (plan.nz - z), plan.nz) for z in range(plan.nz)]
    fields[0] = jnp.zeros((16, plan.ls), F32)
    fields[NX + 1] = jnp.zeros((16, plan.ls), F32)
    for a in range(PLANE // 128):
        pieces = rows_at(
            swap_quarters([in_ref[from_plane[4 * t + i], :, a * 128 : (a + 1) * 128] for i in range(4)])
            for t in range(plan.nz // 4)
        )
        for b, piece in enumerate(pieces):
            fields[4 * a + b + 1] = piece
            mean_ref[4 * a + b : 4 * a + b + 1, :] = piece[0:1]
    tile = jnp.minimum(tile_ref[0], plan.nxb * plan.nyb - 1)
    xb, yb = tile // plan.nyb, tile % plan.nyb
    table = mtab_ref[yb]
    mods_ref[...] = jnp.zeros(mods_ref.shape, F32)
    for k in range(plan.rx):
        here = picked(fields[xb * plan.tx + k], table)
        for v in range(FIELDS):
            mods_ref[v, k : k + 1, :] = here[v : v + 1]


def regrouped(plan, msg_ref, out_ref):
    lane = lax.broadcasted_iota(jnp.int32, (plan.rows_in, plan.lanes), 1)
    height = lane % (plan.nz * plan.ry) // plan.ry

    def one(row, carry):
        parts = [msg_ref[row * plan.slab + z] for z in range(plan.nz)]
        for group in range(plan.slab):
            total = parts[group]
            for z in range(plan.nz):
                if z != group:
                    turned = pltpu.roll(parts[z], (z - group) * plan.ry % plan.lanes, 1)
                    total = jnp.where(height == z, turned, total)
            out_ref[row * plan.slab + group] = total
        return carry

    lax.fori_loop(0, plan.chaos, one, 0, unroll=4)


def first_mix_kernel(plan, low_count, nodes_ref, level_ref, msg_ref, mods_ref, out_ref, grad, flux, scaled, regroup):
    regrouped(plan, msg_ref, regroup)
    mix_kernel(plan, low_count, nodes_ref, level_ref, regroup, mods_ref, out_ref, grad, flux, scaled)


def mix_kernel(plan, low_count, nodes_ref, level_ref, msg_ref, mods_ref, out_ref, grad, flux, scaled):
    sp, rx, ry, nz, lanes = plan.sp, plan.rx, plan.ry, plan.nz, plan.lanes
    segment = nz * ry
    lane = lax.broadcasted_iota(jnp.int32, (8, lanes), 1)
    part, height = lane // segment, lane % segment // ry
    not_top, not_bottom = height != nz - 1, height != 0
    is_x, is_y, is_z = part == 0, part == 1, part == 2
    for level in range(DEG):
        for v in range(KL):
            scaled[level * KL + v] = mods_ref[v + 1] * math.sqrt(level + 1)
    mean = mods_ref[0]

    def gradients(source, carry):
        own = jnp.stack([msg_ref[source, s * rx : s * rx + 8, :] for s in range(sp)])
        slope_x = pltpu.roll(own, 7, 1) - own
        slope_y = pltpu.roll(own, lanes - 1, 2) - own
        slope_z = jnp.where(not_top, pltpu.roll(own, lanes - ry, 2), 0.0) - own
        spread = slope_x + pltpu.roll(slope_y, lanes - segment, 2) + pltpu.roll(slope_z, lanes - 2 * segment, 2)
        full_x = slope_x + jnp.where(is_x, spread, 0.0)
        full_y = slope_y + jnp.where(is_y, pltpu.roll(spread, segment, 2), 0.0)
        full_z = slope_z + jnp.where(is_z, pltpu.roll(spread, 2 * segment, 2), 0.0)
        here = pl.ds(source * sp, sp)
        for d, full in enumerate((full_x, full_y, full_z)):
            grad[here, d] = full
            flux[here, d] = mean * full
        return carry

    lax.fori_loop(0, plan.n, gradients, 0, unroll=4)

    def edges(number, carry):
        base = nodes_ref[number]
        own = [grad[base, d] for d in range(3)]
        total = [flux[base, d] for d in range(3)]
        for group in range(0, KL, 5):
            at = [nodes_ref[low_count + number * KL + v] for v in range(group, group + 5)]
            field = [scaled[level_ref[number * KL + v] * KL + v] for v in range(group, group + 5)]
            fresh = [
                [flux[spot, d] + weight * own[d] for d in range(3)] for spot, weight in zip(at, field)
            ]
            for spot, weight in zip(at, field):
                total = [total[d] + weight * grad[spot, d] for d in range(3)]
            for spot, values in zip(at, fresh):
                for d in range(3):
                    flux[spot, d] = values[d]
        for d in range(3):
            flux[base, d] = total[d]
        return carry

    lax.fori_loop(0, low_count, edges, 0, unroll=2)

    def divergences(source, carry):
        here = pl.ds(source * sp, sp)
        flux_x, flux_y, flux_z = (flux[here, d] for d in range(3))
        total = flux_x - pltpu.roll(flux_x, 1, 1)
        total = total + (flux_y - pltpu.roll(flux_y, 1, 2))
        total = total + (flux_z - jnp.where(not_bottom, pltpu.roll(flux_z, ry, 2), 0.0))
        for s in range(sp):
            out_ref[source, s * plan.tx : (s + 1) * plan.tx, :] = total[s, 1 : 1 + plan.tx]
        return carry

    lax.fori_loop(0, plan.n, divergences, 0, unroll=2)


def unpack_image(plan, image_ref, unpack_ref, lhs, rows):
    for xb in range(plan.nxb):
        for k in range(plan.tx):
            x = xb * plan.tx + k
            for yb in range(plan.nyb):
                lhs[x * plan.hs : x * plan.hs + plan.sp, yb * plan.lanes : (yb + 1) * plan.lanes] = image_ref[
                    xb * plan.nyb + yb, strided(k, plan.sp, plan.tx), :
                ]
    pick_into(rows, lhs, unpack_ref)


def add_image(plan, base_ref, live_ref, rows, residual_ref):
    live = live_ref[...] != 0.0

    def one(x, carry):
        for c in range(3):
            image = rows[pl.ds(pl.multiple_of(x * plan.hs, plan.hs), plan.hs), c * plan.ls : (c + 1) * plan.ls]
            residual_ref[x, c] = jnp.where(live, base_ref[x, c] + image, 0.0)
        return carry

    lax.fori_loop(0, NX, one, 0, unroll=6)


def smooth(plan, mean_ref, residual_ref, update, step):
    hs, ls = plan.hs, plan.ls
    center_value = 0.5 * (bound_high + bound_low)
    half_width = 0.5 * (bound_high - bound_low)
    ratio_value = center_value / half_width
    lane = lax.broadcasted_iota(jnp.int32, (hs, ls), 1)
    at_y, at_z = lane % NY, lane // NY
    not_y_end, not_y_start = at_y != NY - 1, at_y != 0
    not_z_end, not_z_start = at_z != plan.nz - 1, at_z != 0

    def first(x, carry):
        for c in range(3):
            scaled = residual_ref[x, c] * (1.0 / center_value)
            update[x, c] = scaled
            step[x, c] = scaled
        return carry

    lax.fori_loop(0, NX, first, 0, unroll=6)
    for c in range(3):
        update[NX, c] = jnp.zeros((hs, ls), F32)

    rho_prev = 1.0 / ratio_value
    for sweep in range(SWEEPS):
        rho_next = 1.0 / (2.0 * ratio_value - rho_prev)
        keep, gain = rho_next * rho_prev, 2.0 * rho_next / half_width

        def slab_of(x, carry, keep=keep, gain=gain):
            behind, own = carry[:3], carry[3:]
            modulus = jnp.broadcast_to(mean_ref[pl.ds(x, 1), :], (hs, ls))
            ahead = [update[x + 1, c] for c in range(3)]
            slope_x = [ahead[c] - own[c] for c in range(3)]
            slope_y = [jnp.where(not_y_end, pltpu.roll(own[c], ls - 1, 1), 0.0) - own[c] for c in range(3)]
            slope_z = [jnp.where(not_z_end, pltpu.roll(own[c], ls - NY, 1), 0.0) - own[c] for c in range(3)]
            spread = slope_x[0] + slope_y[1] + slope_z[2]
            slope_x[0] = slope_x[0] + spread
            slope_y[1] = slope_y[1] + spread
            slope_z[2] = slope_z[2] + spread
            through = []
            for c in range(3):
                flux_x, flux_y, flux_z = (modulus * slope[c] for slope in (slope_x, slope_y, slope_z))
                through.append(flux_x)
                total = flux_x - behind[c]
                total = total + (flux_y - jnp.where(not_y_start, pltpu.roll(flux_y, 1, 1), 0.0))
                total = total + (flux_z - jnp.where(not_z_start, pltpu.roll(flux_z, NY, 1), 0.0))
                moved = keep * step[x, c] + gain * (residual_ref[x, c] + total)
                step[x, c] = moved
                update[x, c] = own[c] + moved
            return (*through, *ahead)

        zero = jnp.zeros((hs, ls), F32)
        lax.fori_loop(0, NX, slab_of, (zero, zero, zero, *(update[0, c] for c in range(3))), unroll=6)
        rho_prev = rho_next


def middle_kernel(plan, image_ref, base_ref, live_ref, mean_ref, unpack_ref, pack_ref, msg_ref, residual_ref, update_ref, wide, narrow, step):
    unpack_image(plan, image_ref, unpack_ref, wide, narrow)
    add_image(plan, base_ref, live_ref, narrow, residual_ref)
    smooth(plan, mean_ref, residual_ref, update_ref, step)
    for x in range(NX):
        for c in range(3):
            narrow[x * plan.hs : (x + 1) * plan.hs, c * plan.ls : (c + 1) * plan.ls] = update_ref[x, c]
    pick_into(wide, narrow, pack_ref)
    store_message(plan, wide, msg_ref)


def flat_rows(plan, values, out_ref, c, a):
    for t in range(plan.nz // 4):
        parts = [value[:, t * 128 : (t + 1) * 128] for value in values]
        for i, piece in enumerate(swap_quarters(parts)):
            out_ref[4 * t + i, c * plan.sp : (c + 1) * plan.sp, a * 128 : (a + 1) * 128] = piece[: plan.sp]


def residual_kernel(plan, image_ref, base_ref, live_ref, unpack_ref, residual_ref, out_ref, wide, narrow):
    unpack_image(plan, image_ref, unpack_ref, wide, narrow)
    add_image(plan, base_ref, live_ref, narrow, residual_ref)
    for a in range(PLANE // 128):
        for c in range(3):
            flat_rows(plan, [residual_ref[4 * a + b, c] for b in range(4)], out_ref, c, a)


def end_kernel(plan, residual_ref, mean_ref, before_ref, out_ref, update, step):
    smooth(plan, mean_ref, residual_ref, update, step)
    for a in range(PLANE // 128):
        for c in range(3):
            flat_rows(plan, [update[4 * a + b, c] + before_ref[4 * a + b, c] for b in range(4)], out_ref, c, a)


def per_device(displacement, load, mean_modulus, modes, owner):
    chaos, slab = lax.axis_size("chaos"), lax.axis_size("slab")
    slots_dev, slots_all = displacement.shape[0], owner.shape[0]
    plan = Plan(chaos, slab, slots_dev)
    n, sp, hs, ls, lanes = plan.n, plan.sp, plan.hs, plan.ls, plan.lanes
    count, low, raised, level = edge_tables()
    at_chaos, at_slab = lax.axis_index("chaos"), lax.axis_index("slab")

    slots = np.arange(slots_all)
    places = (slots // slots_dev) * (slab * sp) + slots % slots_dev
    wanted = np.concatenate([low, raised])
    nodes = jnp.sum(
        jnp.where(wanted[:, None] == owner[None, :], jnp.asarray(places, jnp.int32)[None, :], 0), axis=1
    ).astype(jnp.int32)
    live_all = owner < count
    live_own = lax.dynamic_slice_in_dim(live_all, at_chaos * slots_dev, slots_dev, 0)
    live_here = jnp.pad(live_own.astype(F32), (0, slab * sp - slots_dev))
    live_here = lax.dynamic_slice_in_dim(live_here, at_slab * sp, sp, 0)
    live_here = jnp.broadcast_to(jnp.pad(live_here, (0, hs - sp))[:, None], (hs, ls))

    pack = jnp.asarray(plan.pack_table(), BF16)
    unpack = jnp.asarray(plan.unpack_table(), BF16)
    mtab = jnp.asarray(plan.modulus_table(), BF16)
    tile = jnp.stack([at_chaos * slab + at_slab, at_slab]).astype(jnp.int32)

    slots_pad = slab * sp

    def by_component(values):
        return jnp.pad(jnp.transpose(values, (1, 0, 2)), ((0, 0), (0, slots_pad - slots_dev), (0, 0)))

    def everyone(values):
        return lax.all_to_all(values, ("chaos", "slab"), 0, 0, tiled=True)

    def column(values):
        return lax.all_to_all(values, "slab", 0, 0, tiled=True)

    smem = pl.BlockSpec(memory_space=pltpu.SMEM)
    vmem = pl.BlockSpec(memory_space=pltpu.VMEM)

    def call(kernel, name, in_specs, out_shape, scratch_shapes):
        return pl.pallas_call(
            kernel,
            out_shape=out_shape,
            in_specs=in_specs,
            out_specs=jax.tree.map(lambda _: vmem, out_shape),
            scratch_shapes=scratch_shapes,
            compiler_params=pltpu.CompilerParams(vmem_limit_bytes=(16 if plan.positions <= 512 and n <= 64 else 60) * MIB),
            name=name,
        )

    def array(*shape):
        return jax.ShapeDtypeStruct(shape, F32)

    message, image = array(n, plan.rows_in, lanes), array(n, plan.rows_out, lanes)
    grid_field, grid_more = array(NX, 3, hs, ls), array(NX + 1, 3, hs, ls)
    wide = pltpu.VMEM((NX * hs, plan.nyb * lanes), F32)
    narrow = pltpu.VMEM((NX * hs, 3 * ls), F32)
    field_scratch, more_scratch = pltpu.VMEM(grid_field.shape, F32), pltpu.VMEM(grid_more.shape, F32)

    moduli = jnp.concatenate([mean_modulus[None], modes], axis=0)
    moduli = jnp.pad(moduli, ((0, 16 - FIELDS), (0, 0)))
    moduli = jnp.stack(
        [moduli] + [lax.ppermute(moduli, "slab", [(z, (z + step) % slab) for z in range(slab)]) for step in range(1, slab)]
    )
    mean_s, mods = call(
        functools.partial(moduli_kernel, plan),
        "moduli",
        [smem, vmem, vmem],
        (array(NX, ls), array(FIELDS, 8, lanes)),
        [pltpu.VMEM((NX + 2, 16, ls), F32)],
    )(tile, moduli, mtab)

    msg = call(functools.partial(start_kernel, plan), "start", [vmem, vmem], message, [narrow, wide])(
        by_component(displacement), pack
    )

    def mixed(values, first):
        scratch = [
            pltpu.VMEM((plan.positions, 3, 8, lanes), F32),
            pltpu.VMEM((plan.positions, 3, 8, lanes), F32),
            pltpu.VMEM((DEG * KL, 8, lanes), F32),
        ]
        kernel = mix_kernel
        if first:
            kernel = first_mix_kernel
            scratch.append(pltpu.VMEM((n, plan.rows_in, lanes), F32))
        return call(
            functools.partial(kernel, plan, len(low)), "mix", [smem, smem, vmem, vmem], image, scratch
        )(nodes, jnp.asarray(level, jnp.int32), values, mods)

    arrived = everyone(msg)
    flat, parts = array(slab, plan.rows_flat, PLANE), array(3, slots_pad, PLANE)
    load_flat = call(functools.partial(split_kernel, plan), "split", [vmem], flat, [])(by_component(load))
    load_flat, nodes, mean_s, mods = lax.optimization_barrier((load_flat, nodes, mean_s, mods))
    load_flat, arrived = lax.optimization_barrier((load_flat, arrived))
    load_s = call(functools.partial(load_kernel, plan), "load", [vmem], grid_field, [])(column(load_flat))
    first_image = everyone(mixed(arrived, True))
    msg, residual_s, update_s = call(
        functools.partial(middle_kernel, plan),
        "middle",
        [vmem] * 6,
        (message, grid_field, grid_more),
        [wide, narrow, field_scratch],
    )(first_image, load_s, live_here, mean_s, unpack, pack)

    second_image = everyone(mixed(everyone(msg), False))
    residual_s, residual_flat = call(
        functools.partial(residual_kernel, plan), "residual", [vmem] * 4, (grid_field, flat), [wide, narrow]
    )(second_image, residual_s, live_here, unpack)
    residual = column(residual_flat)
    update_flat = call(
        functools.partial(end_kernel, plan), "end", [vmem] * 3, flat, [more_scratch, field_scratch]
    )(residual_s, mean_s, update_s)
    residual = call(functools.partial(join_kernel, plan), "join", [vmem], parts, [])(residual)
    live_pad = jnp.pad(live_own.astype(F32), (0, slots_pad - slots_dev))
    total = call(functools.partial(add_kernel, plan), "add", [vmem] * 3, parts, [])(
        column(update_flat), jnp.broadcast_to(live_pad[:, None], (slots_pad, 128))[:, :1], by_component(displacement)
    )
    return tuple(jnp.transpose(values, (1, 0, 2))[:slots_dev] for values in (total, residual))


def solution(mesh):
    in_specs = (P("chaos", None, "slab"), P("chaos", None, "slab"), P("slab"), P(None, "slab"), P())
    out_specs = (P("chaos", None, "slab"), P("chaos", None, "slab"))
    return jax.shard_map(
        per_device, mesh=mesh, in_specs=in_specs, out_specs=out_specs, check_vma=False
    )
```

```python
import functools
import math

import jax
import jax.numpy as jnp
import numpy as np
from jax import lax
from jax.experimental import pallas as pl
from jax.experimental.pallas import tpu as pltpu
from jax.sharding import PartitionSpec as P

NX = 24
NY = 32
KL = 10
DEG = 3
SWEEPS = 4
PLANE = NX * NY
FIELDS = KL + 1

bound_high = 50.0
bound_low = 2.5
MIB = 1024 * 1024
F32 = jnp.float32
BF16 = jnp.bfloat16


def up8(count):
    return -(-count // 8) * 8


def multi_indices():
    listing = [[]]
    for variable in range(KL):
        extended_list = []
        for prefix in listing:
            for degree in range(DEG + 1 - sum(prefix)):
                extended_list.append(prefix + [degree])
        listing = extended_list
    return listing


def edge_tables():
    listing = multi_indices()
    lookup = {tuple(entry): number for number, entry in enumerate(listing)}
    low, raised, level = [], [], []
    for number, entry in enumerate(listing):
        if sum(entry) == DEG:
            continue
        low.append(number)
        for variable in range(KL):
            other = list(entry)
            other[variable] += 1
            raised.append(lookup[tuple(other)])
            level.append(entry[variable])
    return len(listing), np.array(low, np.int32), np.array(raised, np.int32), np.array(level, np.int32)


class Plan:
    def __init__(self, chaos, slab, slots_dev):
        self.chaos, self.slab, self.slots_dev = chaos, slab, slots_dev
        self.n = chaos * slab
        self.nz = slab
        self.sp = -(-slots_dev // slab)
        self.hs = up8(self.sp)
        self.ls = self.nz * NY
        best = None
        for tx in range(1, 7):
            for ty in range(1, NY + 1):
                if NX % tx or NY % ty or (NX // tx) * (NY // ty) > self.n:
                    continue
                lanes = -(-3 * self.nz * (ty + 2) // 128) * 128
                rows = up8((self.sp - 1) * (tx + 2) + 8)
                key = (-(NX // tx) * (NY // ty), rows * lanes)
                if best is None or key < best[0]:
                    best = (key, tx, ty, lanes, rows)
        _, self.tx, self.ty, self.lanes, self.rows_in = best
        self.rx = self.tx + 2
        self.ry = self.ty + 2
        self.nxb, self.nyb = NX // self.tx, NY // self.ty
        self.rows_out = up8(self.sp * self.tx)
        self.rows_flat = up8(3 * self.sp + 1)
        self.rows_end = up8(6 * self.sp)
        self.shares = -(-FIELDS // min(chaos, 16))
        self.per_share = 16 // self.shares
        self.positions = self.n * self.sp

    def pack_table(self):
        table = np.zeros((3 * self.ls, self.nyb * self.lanes), np.float32)
        for c in range(3):
            for z in range(self.nz):
                for yb in range(self.nyb):
                    for k in range(self.ry):
                        y = yb * self.ty - 1 + k
                        if 0 <= y < NY:
                            table[
                                c * self.ls + z * NY + y,
                                yb * self.lanes + (c * self.nz + z) * self.ry + k,
                            ] = 1
        return table

    def unpack_table(self):
        table = np.zeros((self.nyb * self.lanes, 3 * self.ls), np.float32)
        for c in range(3):
            for z in range(self.nz):
                for y in range(NY):
                    yb, k = y // self.ty, y % self.ty + 1
                    table[
                        yb * self.lanes + (c * self.nz + z) * self.ry + k, c * self.ls + z * NY + y
                    ] = 1
        return table

    def modulus_table(self):
        table = np.zeros((self.nyb, self.ls, self.lanes), np.float32)
        for yb in range(self.nyb):
            for z in range(self.nz):
                for k in range(self.ry):
                    y = yb * self.ty - 1 + k
                    if 0 <= y < NY:
                        for c in range(3):
                            table[yb, z * NY + y, (c * self.nz + z) * self.ry + k] = 1
        return table


def picked(values, table):
    high = values.astype(BF16)
    rest = values - high.astype(F32)
    middle = rest.astype(BF16)
    low = (rest - middle.astype(F32)).astype(BF16)
    return (
        jnp.dot(high, table, preferred_element_type=F32)
        + jnp.dot(middle, table, preferred_element_type=F32)
        + jnp.dot(low, table, preferred_element_type=F32)
    )


def pick_into(out_ref, values_ref, table_ref):
    width = table_ref.shape[1]
    chunk = width if width <= 1024 else 512
    for first in range(0, width, chunk):
        out_ref[:, first : first + chunk] = picked(values_ref[...], table_ref[:, first : first + chunk])


def swap_quarters(parts):
    quarter = lax.broadcasted_iota(jnp.int32, parts[0].shape, 1) // NY
    swapped = []
    for j in range(4):
        total = parts[j]
        for i in range(4):
            if i != j:
                turned = pltpu.roll(parts[i], (i - j) % 4 * NY, 1)
                total = jnp.where(quarter == i, turned, total)
        swapped.append(total)
    return swapped


def strided(start, size, step):
    return pl.ds(start, size) if size == 1 or step == 1 else pl.ds(start, size, stride=step)


def store_moduli(plan, chaos_at, moduli_ref, msg_ref):
    quarter = lax.broadcasted_iota(jnp.int32, (1, 128), 1) // NY
    own = [moduli_ref[pl.ds(share * plan.per_share + chaos_at, 1), :] for share in range(plan.shares)]
    count, first = plan.shares * plan.rx, plan.sp * plan.rx
    for xb in range(plan.nxb):
        for start in range(0, count, 4):
            line = jnp.zeros((1, 128), F32)
            for number in range(start, min(count, start + 4)):
                share, k = divmod(number, plan.rx)
                x = xb * plan.tx - 1 + k
                if 0 <= x < NX:
                    piece = own[share][:, x // 4 * 128 : (x // 4 + 1) * 128]
                    turned = pltpu.roll(piece, (number - x) % 4 * NY, 1)
                    line = jnp.where(quarter == number % 4, turned, line)
            row, column = divmod(start // 4, plan.lanes // 128)
            for yb in range(plan.nyb):
                tile = xb * plan.nyb + yb
                msg_ref[tile, first + row : first + row + 1, column * 128 : (column + 1) * 128] = line


def gather_moduli(plan, tile_at, msg_ref, mtab_ref, mods_ref):
    quarter = lax.broadcasted_iota(jnp.int32, (plan.per_share, 128), 1) // NY
    first, rows = plan.sp * plan.rx, plan.rows_in
    table = mtab_ref[lax.rem(tile_at, plan.nyb)]
    mods_ref[...] = jnp.zeros(mods_ref.shape, F32)
    for share in range(plan.shares):
        lines = []
        for k in range(plan.rx):
            number = share * plan.rx + k
            row, column = divmod(number // 4, plan.lanes // 128)
            parts = []
            for t in range(plan.nz // 4):
                total = jnp.zeros((plan.per_share, 128), F32)
                for i in range(4):
                    at, columns = (4 * t + i) * rows + first + row, slice(column * 128, (column + 1) * 128)
                    if plan.lanes == 128:
                        piece = msg_ref[pl.ds(at, plan.per_share, stride=plan.slab * rows), columns]
                    else:
                        lone = [at + j * plan.slab * rows for j in range(plan.per_share)]
                        piece = jnp.concatenate([msg_ref[j : j + 1, columns] for j in lone], axis=0)
                    total = jnp.where(quarter == i, pltpu.roll(piece, (i - number) % 4 * NY, 1), total)
                parts.append(total)
            lines.append(parts[0] if len(parts) == 1 else jnp.concatenate(parts, axis=1))
        here = picked(jnp.concatenate(lines, axis=0), table)
        for k in range(plan.rx):
            for v in range(min(plan.per_share, FIELDS - share * plan.per_share)):
                at = k * plan.per_share + v
                mods_ref[share * plan.per_share + v, k : k + 1, :] = here[at : at + 1]


def store_message(plan, rows_ref, msg_ref):
    blank = jnp.zeros((8, plan.lanes), F32)
    for tile in range(plan.n):
        if tile >= plan.nxb * plan.nyb:
            msg_ref[tile] = jnp.zeros((plan.rows_in, plan.lanes), F32)
            continue
        xb, yb = divmod(tile, plan.nyb)
        msg_ref[tile, plan.rows_in - 8 :, :] = blank
        for k in range(plan.rx):
            x = xb * plan.tx - 1 + k
            if 0 <= x < NX:
                rows = rows_ref[
                    x * plan.hs : x * plan.hs + plan.sp, yb * plan.lanes : (yb + 1) * plan.lanes
                ]
            else:
                rows = jnp.zeros((plan.sp, plan.lanes), F32)
            msg_ref[tile, strided(k, plan.sp, plan.rx), :] = rows


def rows_at(piece_of):
    return [jnp.concatenate(pieces, axis=1) if len(pieces) > 1 else pieces[0] for pieces in zip(*piece_of)]


def start_kernel(plan, place_ref, in_ref, mean_ref, modes_ref, pack_ref, msg_ref, lhs, rows, moduli):
    moduli[...] = jnp.zeros(moduli.shape, F32)
    moduli[0:1] = mean_ref[...]
    moduli[1:FIELDS] = modes_ref[...]
    for a in range(PLANE // 128):
        for c in range(3):
            pieces = rows_at(
                swap_quarters(
                    [
                        in_ref[c, (4 * t + i) * plan.sp : (4 * t + i + 1) * plan.sp, a * 128 : (a + 1) * 128]
                        for i in range(4)
                    ]
                )
                for t in range(plan.slab // 4)
            )
            for b, piece in enumerate(pieces):
                x = 4 * a + b
                lhs[x * plan.hs : x * plan.hs + plan.sp, c * plan.ls : (c + 1) * plan.ls] = piece
    pick_into(rows, lhs, pack_ref)
    store_message(plan, rows, msg_ref)
    store_moduli(plan, jnp.minimum(place_ref[0], plan.per_share - 1), moduli, msg_ref)


def split_kernel(plan, in_ref, mean_ref, out_ref):
    for group in range(plan.slab):
        out_ref[group, 3 * plan.sp : 3 * plan.sp + 1, :] = mean_ref[...]
        for c in range(3):
            out_ref[group, c * plan.sp : (c + 1) * plan.sp, :] = in_ref[
                c, group * plan.sp : (group + 1) * plan.sp, :
            ]


def load_kernel(plan, in_ref, out_ref, mean_ref):
    for a in range(PLANE // 128):
        pieces = rows_at(
            swap_quarters(
                [in_ref[4 * t + i, 3 * plan.sp : 3 * plan.sp + 1, a * 128 : (a + 1) * 128] for i in range(4)]
            )
            for t in range(plan.nz // 4)
        )
        for b, piece in enumerate(pieces):
            mean_ref[4 * a + b : 4 * a + b + 1, :] = piece
        for c in range(3):
            pieces = rows_at(
                swap_quarters(
                    [in_ref[4 * t + i, c * plan.sp : (c + 1) * plan.sp, a * 128 : (a + 1) * 128] for i in range(4)]
                )
                for t in range(plan.nz // 4)
            )
            for b, piece in enumerate(pieces):
                out_ref[4 * a + b, c, 0 : plan.sp, :] = piece


def finish_kernel(plan, in_ref, live_ref, start_ref, total_ref, residual_ref):
    for group in range(plan.slab):
        here = slice(group * plan.sp, (group + 1) * plan.sp)
        live = jnp.broadcast_to(live_ref[here, :], (plan.sp, PLANE)) != 0.0
        for c in range(3):
            total_ref[c, here, :] = jnp.where(live, start_ref[c, here, :], 0.0) + in_ref[
                group, c * plan.sp : (c + 1) * plan.sp, :
            ]
            residual_ref[c, here, :] = in_ref[group, (3 + c) * plan.sp : (4 + c) * plan.sp, :]


def regrouped(plan, msg_ref, out_ref):
    lane = lax.broadcasted_iota(jnp.int32, (plan.rows_in, plan.lanes), 1)
    height = lane % (plan.nz * plan.ry) // plan.ry

    def one(row, carry):
        parts = [
            msg_ref[pl.ds(pl.multiple_of((row * plan.slab + z) * plan.rows_in, 8), plan.rows_in), :] for z in range(plan.nz)
        ]
        for group in range(plan.slab):
            total = parts[group]
            for z in range(plan.nz):
                if z != group:
                    turned = pltpu.roll(parts[z], (z - group) * plan.ry % plan.lanes, 1)
                    total = jnp.where(height == z, turned, total)
            out_ref[row * plan.slab + group] = total
        return carry

    lax.fori_loop(0, plan.chaos, one, 0, unroll=4)


def first_mix_kernel(plan, low_count, place_ref, nodes_ref, level_ref, msg_ref, mtab_ref, out_ref, mods_ref, grad, flux, scaled, regroup):
    gather_moduli(plan, place_ref[0] * plan.slab + place_ref[1], msg_ref, mtab_ref, mods_ref)
    regrouped(plan, msg_ref, regroup)
    mix_kernel(plan, low_count, nodes_ref, level_ref, regroup, mods_ref, out_ref, grad, flux, scaled)


def mix_kernel(plan, low_count, nodes_ref, level_ref, msg_ref, mods_ref, out_ref, grad, flux, scaled):
    sp, rx, ry, nz, lanes = plan.sp, plan.rx, plan.ry, plan.nz, plan.lanes
    segment = nz * ry
    lane = lax.broadcasted_iota(jnp.int32, (8, lanes), 1)
    part, height = lane // segment, lane % segment // ry
    not_top, not_bottom = height != nz - 1, height != 0
    is_x, is_y, is_z = part == 0, part == 1, part == 2
    for level in range(DEG):
        for v in range(KL):
            scaled[level * KL + v] = mods_ref[v + 1] * math.sqrt(level + 1)
    mean = mods_ref[0]

    def gradients(source, carry):
        own = jnp.stack([msg_ref[source, s * rx : s * rx + 8, :] for s in range(sp)])
        slope_x = pltpu.roll(own, 7, 1) - own
        slope_y = pltpu.roll(own, lanes - 1, 2) - own
        slope_z = jnp.where(not_top, pltpu.roll(own, lanes - ry, 2), 0.0) - own
        spread = slope_x + pltpu.roll(slope_y, lanes - segment, 2) + pltpu.roll(slope_z, lanes - 2 * segment, 2)
        full_x = slope_x + jnp.where(is_x, spread, 0.0)
        full_y = slope_y + jnp.where(is_y, pltpu.roll(spread, segment, 2), 0.0)
        full_z = slope_z + jnp.where(is_z, pltpu.roll(spread, 2 * segment, 2), 0.0)
        here = pl.ds(source * sp, sp)
        for d, full in enumerate((full_x, full_y, full_z)):
            grad[here, d] = full
            flux[here, d] = mean * full
        return carry

    lax.fori_loop(0, plan.n, gradients, 0, unroll=4)

    def edges(number, carry):
        base = nodes_ref[number]
        own = [grad[base, d] for d in range(3)]
        total = [flux[base, d] for d in range(3)]
        for group in range(0, KL, 5):
            at = [nodes_ref[low_count + number * KL + v] for v in range(group, group + 5)]
            field = [scaled[level_ref[number * KL + v] * KL + v] for v in range(group, group + 5)]
            fresh = [
                [flux[spot, d] + weight * own[d] for d in range(3)] for spot, weight in zip(at, field)
            ]
            for spot, weight in zip(at, field):
                total = [total[d] + weight * grad[spot, d] for d in range(3)]
            for spot, values in zip(at, fresh):
                for d in range(3):
                    flux[spot, d] = values[d]
        for d in range(3):
            flux[base, d] = total[d]
        return carry

    lax.fori_loop(0, low_count, edges, 0, unroll=2)

    def divergences(source, carry):
        here = pl.ds(source * sp, sp)
        flux_x, flux_y, flux_z = (flux[here, d] for d in range(3))
        total = flux_x - pltpu.roll(flux_x, 1, 1)
        total = total + (flux_y - pltpu.roll(flux_y, 1, 2))
        total = total + (flux_z - jnp.where(not_bottom, pltpu.roll(flux_z, ry, 2), 0.0))
        for s in range(sp):
            out_ref[source, s * plan.tx : (s + 1) * plan.tx, :] = total[s, 1 : 1 + plan.tx]
        return carry

    lax.fori_loop(0, plan.n, divergences, 0, unroll=2)


def unpack_image(plan, image_ref, unpack_ref, lhs, rows):
    for xb in range(plan.nxb):
        for k in range(plan.tx):
            x = xb * plan.tx + k
            for yb in range(plan.nyb):
                lhs[x * plan.hs : x * plan.hs + plan.sp, yb * plan.lanes : (yb + 1) * plan.lanes] = image_ref[
                    xb * plan.nyb + yb, strided(k, plan.sp, plan.tx), :
                ]
    pick_into(rows, lhs, unpack_ref)


def add_image(plan, base_ref, live_ref, rows, residual_ref):
    live = live_ref[...] != 0.0

    def one(x, carry):
        for c in range(3):
            image = rows[pl.ds(pl.multiple_of(x * plan.hs, plan.hs), plan.hs), c * plan.ls : (c + 1) * plan.ls]
            residual_ref[x, c] = jnp.where(live, base_ref[x, c] + image, 0.0)
        return carry

    lax.fori_loop(0, NX, one, 0, unroll=6)


def smooth(plan, mean_ref, residual_ref, update, step):
    hs, ls = plan.hs, plan.ls
    center_value = 0.5 * (bound_high + bound_low)
    half_width = 0.5 * (bound_high - bound_low)
    ratio_value = center_value / half_width
    lane = lax.broadcasted_iota(jnp.int32, (hs, ls), 1)
    at_y, at_z = lane % NY, lane // NY
    not_y_end, not_y_start = at_y != NY - 1, at_y != 0
    not_z_end, not_z_start = at_z != plan.nz - 1, at_z != 0

    def first(x, carry):
        for c in range(3):
            scaled = residual_ref[x, c] * (1.0 / center_value)
            update[x, c] = scaled
            step[x, c] = scaled
        return carry

    lax.fori_loop(0, NX, first, 0, unroll=6)
    for c in range(3):
        update[NX, c] = jnp.zeros((hs, ls), F32)

    rho_prev = 1.0 / ratio_value
    for sweep in range(SWEEPS):
        rho_next = 1.0 / (2.0 * ratio_value - rho_prev)
        keep, gain = rho_next * rho_prev, 2.0 * rho_next / half_width

        def slab_of(x, carry, keep=keep, gain=gain):
            behind, own = carry[:3], carry[3:]
            modulus = jnp.broadcast_to(mean_ref[pl.ds(x, 1), :], (hs, ls))
            ahead = [update[x + 1, c] for c in range(3)]
            slope_x = [ahead[c] - own[c] for c in range(3)]
            slope_y = [jnp.where(not_y_end, pltpu.roll(own[c], ls - 1, 1), 0.0) - own[c] for c in range(3)]
            slope_z = [jnp.where(not_z_end, pltpu.roll(own[c], ls - NY, 1), 0.0) - own[c] for c in range(3)]
            spread = slope_x[0] + slope_y[1] + slope_z[2]
            slope_x[0] = slope_x[0] + spread
            slope_y[1] = slope_y[1] + spread
            slope_z[2] = slope_z[2] + spread
            through = []
            for c in range(3):
                flux_x, flux_y, flux_z = (modulus * slope[c] for slope in (slope_x, slope_y, slope_z))
                through.append(flux_x)
                total = flux_x - behind[c]
                total = total + (flux_y - jnp.where(not_y_start, pltpu.roll(flux_y, 1, 1), 0.0))
                total = total + (flux_z - jnp.where(not_z_start, pltpu.roll(flux_z, NY, 1), 0.0))
                moved = keep * step[x, c] + gain * (residual_ref[x, c] + total)
                step[x, c] = moved
                update[x, c] = own[c] + moved
            return (*through, *ahead)

        zero = jnp.zeros((hs, ls), F32)
        lax.fori_loop(0, NX, slab_of, (zero, zero, zero, *(update[0, c] for c in range(3))), unroll=6)
        rho_prev = rho_next


def middle_kernel(plan, image_ref, base_ref, live_ref, mean_ref, unpack_ref, pack_ref, msg_ref, residual_ref, update_ref, wide, narrow, step):
    unpack_image(plan, image_ref, unpack_ref, wide, narrow)
    add_image(plan, base_ref, live_ref, narrow, residual_ref)
    smooth(plan, mean_ref, residual_ref, update_ref, step)
    for x in range(NX):
        for c in range(3):
            narrow[x * plan.hs : (x + 1) * plan.hs, c * plan.ls : (c + 1) * plan.ls] = update_ref[x, c]
    pick_into(wide, narrow, pack_ref)
    store_message(plan, wide, msg_ref)


def flat_rows(plan, values, out_ref, first, a):
    for t in range(plan.nz // 4):
        parts = [value[:, t * 128 : (t + 1) * 128] for value in values]
        for i, piece in enumerate(swap_quarters(parts)):
            out_ref[4 * t + i, first : first + plan.sp, a * 128 : (a + 1) * 128] = piece[: plan.sp]


def end_kernel(plan, image_ref, base_ref, live_ref, mean_ref, unpack_ref, before_ref, out_ref, wide, narrow, residual, update, step):
    unpack_image(plan, image_ref, unpack_ref, wide, narrow)
    add_image(plan, base_ref, live_ref, narrow, residual)
    smooth(plan, mean_ref, residual, update, step)
    for a in range(PLANE // 128):
        for c in range(3):
            flat_rows(plan, [update[4 * a + b, c] + before_ref[4 * a + b, c] for b in range(4)], out_ref, c * plan.sp, a)
            flat_rows(plan, [residual[4 * a + b, c] for b in range(4)], out_ref, (3 + c) * plan.sp, a)


def per_device(displacement, load, mean_modulus, modes, owner):
    chaos, slab = lax.axis_size("chaos"), lax.axis_size("slab")
    slots_dev, slots_all = displacement.shape[0], owner.shape[0]
    plan = Plan(chaos, slab, slots_dev)
    n, sp, hs, ls, lanes = plan.n, plan.sp, plan.hs, plan.ls, plan.lanes
    count, low, raised, level = edge_tables()
    at_chaos, at_slab = lax.axis_index("chaos"), lax.axis_index("slab")

    slots = np.arange(slots_all)
    places = (slots // slots_dev) * (slab * sp) + slots % slots_dev
    wanted = np.concatenate([low, raised])
    nodes = jnp.sum(
        jnp.where(wanted[:, None] == owner[None, :], jnp.asarray(places, jnp.int32)[None, :], 0), axis=1
    ).astype(jnp.int32)
    live_all = owner < count
    live_own = lax.dynamic_slice_in_dim(live_all, at_chaos * slots_dev, slots_dev, 0)
    live_here = jnp.pad(live_own.astype(F32), (0, slab * sp - slots_dev))
    live_here = lax.dynamic_slice_in_dim(live_here, at_slab * sp, sp, 0)
    live_here = jnp.broadcast_to(jnp.pad(live_here, (0, hs - sp))[:, None], (hs, ls))

    pack = jnp.asarray(plan.pack_table(), BF16)
    unpack = jnp.asarray(plan.unpack_table(), BF16)
    mtab = jnp.asarray(plan.modulus_table(), BF16)
    place = jnp.stack([at_chaos, at_slab]).astype(jnp.int32)

    slots_pad = slab * sp

    def by_component(values):
        return jnp.pad(jnp.transpose(values, (1, 0, 2)), ((0, 0), (0, slots_pad - slots_dev), (0, 0)))

    def everyone(values):
        return lax.all_to_all(values, ("chaos", "slab"), 0, 0, tiled=True)

    def column(values):
        return lax.all_to_all(values, "slab", 0, 0, tiled=True)

    smem = pl.BlockSpec(memory_space=pltpu.SMEM)
    vmem = pl.BlockSpec(memory_space=pltpu.VMEM)

    def call(kernel, name, in_specs, out_shape, scratch_shapes):
        return pl.pallas_call(
            kernel,
            out_shape=out_shape,
            in_specs=in_specs,
            out_specs=jax.tree.map(lambda _: vmem, out_shape),
            scratch_shapes=scratch_shapes,
            compiler_params=pltpu.CompilerParams(vmem_limit_bytes=(16 if plan.positions <= 512 and n <= 64 else 60) * MIB),
            name=name,
        )

    def array(*shape):
        return jax.ShapeDtypeStruct(shape, F32)

    message, image = array(n, plan.rows_in, lanes), array(n, plan.rows_out, lanes)
    grid_field, grid_more = array(NX, 3, hs, ls), array(NX + 1, 3, hs, ls)
    wide = pltpu.VMEM((NX * hs, plan.nyb * lanes), F32)
    narrow = pltpu.VMEM((NX * hs, 3 * ls), F32)
    field_scratch, more_scratch = pltpu.VMEM(grid_field.shape, F32), pltpu.VMEM(grid_more.shape, F32)

    mean_row = mean_modulus.reshape(1, PLANE)
    msg = call(
        functools.partial(start_kernel, plan),
        "start",
        [smem, vmem, vmem, vmem, vmem],
        message,
        [narrow, wide, pltpu.VMEM((16, PLANE), F32)],
    )(place, by_component(displacement), mean_row, modes, pack)
    levels = jnp.asarray(level, jnp.int32)
    mix_scratch = [
        pltpu.VMEM((plan.positions, 3, 8, lanes), F32),
        pltpu.VMEM((plan.positions, 3, 8, lanes), F32),
        pltpu.VMEM((DEG * KL, 8, lanes), F32),
    ]

    arrived = everyone(msg)
    flat, parts = array(slab, plan.rows_flat, PLANE), array(3, slots_pad, PLANE)
    load_flat = call(functools.partial(split_kernel, plan), "split", [vmem, vmem], flat, [])(
        by_component(load), mean_row
    )
    load_flat, nodes, place = lax.optimization_barrier((load_flat, nodes, place))
    load_flat, arrived = lax.optimization_barrier((load_flat, arrived))
    load_s, mean_s = call(functools.partial(load_kernel, plan), "load", [vmem], (grid_field, array(NX, ls)), [])(
        column(load_flat)
    )
    first_image, mods = call(
        functools.partial(first_mix_kernel, plan, len(low)),
        "mix",
        [smem, smem, smem, vmem, vmem],
        (image, array(FIELDS, 8, lanes)),
        mix_scratch + [pltpu.VMEM((n, plan.rows_in, lanes), F32)],
    )(place, nodes, levels, arrived.reshape(n * plan.rows_in, lanes), mtab)
    msg, residual_s, update_s = call(
        functools.partial(middle_kernel, plan),
        "middle",
        [vmem] * 6,
        (message, grid_field, grid_more),
        [wide, narrow, field_scratch],
    )(everyone(first_image), load_s, live_here, mean_s, unpack, pack)

    second_image = call(
        functools.partial(mix_kernel, plan, len(low)), "mix", [smem, smem, vmem, vmem], image, mix_scratch
    )(nodes, levels, everyone(msg), mods)
    ending = call(
        functools.partial(end_kernel, plan),
        "end",
        [vmem] * 6,
        array(slab, plan.rows_end, PLANE),
        [wide, narrow, field_scratch, more_scratch, field_scratch],
    )(everyone(second_image), residual_s, live_here, mean_s, unpack, update_s)
    live_pad = jnp.pad(live_own.astype(F32), (0, slots_pad - slots_dev))
    outs = call(functools.partial(finish_kernel, plan), "finish", [vmem] * 3, (parts, parts), [])(
        column(ending), live_pad[:, None], by_component(displacement)
    )
    return tuple(jnp.transpose(values, (1, 0, 2))[:slots_dev] for values in outs)


def solution(mesh):
    in_specs = (P("chaos", None, "slab"), P("chaos", None, "slab"), P("slab"), P(None, "slab"), P())
    out_specs = (P("chaos", None, "slab"), P("chaos", None, "slab"))
    return jax.shard_map(
        per_device, mesh=mesh, in_specs=in_specs, out_specs=out_specs, check_vma=False
    )
```

```python
import functools
import math

import jax
import jax.numpy as jnp
import numpy as np
from jax import lax
from jax.experimental import pallas as pl
from jax.experimental.pallas import tpu as pltpu
from jax.sharding import PartitionSpec as P

NX = 24
NY = 32
KL = 10
DEG = 3
SWEEPS = 4
PLANE = NX * NY
FIELDS = KL + 1

bound_high = 50.0
bound_low = 2.5
MIB = 1024 * 1024
F32 = jnp.float32
BF16 = jnp.bfloat16


def up8(count):
    return -(-count // 8) * 8


def multi_indices():
    listing = [[]]
    for variable in range(KL):
        extended_list = []
        for prefix in listing:
            for degree in range(DEG + 1 - sum(prefix)):
                extended_list.append(prefix + [degree])
        listing = extended_list
    return listing


def edge_tables():
    listing = multi_indices()
    lookup = {tuple(entry): number for number, entry in enumerate(listing)}
    low, raised, level = [], [], []
    for number, entry in enumerate(listing):
        if sum(entry) == DEG:
            continue
        low.append(number)
        for variable in range(KL):
            other = list(entry)
            other[variable] += 1
            raised.append(lookup[tuple(other)])
            level.append(entry[variable])
    return len(listing), np.array(low, np.int32), np.array(raised, np.int32), np.array(level, np.int32)


class Plan:
    def __init__(self, chaos, slab, slots_dev):
        self.chaos, self.slab, self.slots_dev = chaos, slab, slots_dev
        self.n = chaos * slab
        self.nz = slab
        self.sp = -(-slots_dev // slab)
        self.hs = up8(self.sp)
        self.ls = self.nz * NY
        best = None
        for tx in range(1, 7):
            for ty in range(1, NY + 1):
                if NX % tx or NY % ty or (NX // tx) * (NY // ty) > self.n:
                    continue
                lanes = -(-3 * self.nz * (ty + 2) // 128) * 128
                rows = up8((self.sp - 1) * (tx + 2) + 8)
                key = (-(NX // tx) * (NY // ty), rows * lanes)
                if best is None or key < best[0]:
                    best = (key, tx, ty, lanes, rows)
        _, self.tx, self.ty, self.lanes, self.rows_in = best
        self.rx = self.tx + 2
        self.ry = self.ty + 2
        self.nxb, self.nyb = NX // self.tx, NY // self.ty
        self.lanes_out = -(-3 * self.nz * self.ty // 128) * 128
        self.segment = self.nz * self.ty
        self.moved = self.sp // 4 if self.lanes_out >= 4 * self.segment else 0
        self.kept = self.sp - self.moved
        self.rows_out = up8(self.kept * self.tx)
        self.image_width = (4 if self.moved else 3) * self.ls
        self.rows_flat = up8(3 * self.sp + 1)
        self.rows_end = up8(6 * self.sp)
        self.shares = -(-FIELDS // min(chaos, 16))
        self.per_share = 16 // self.shares
        self.positions = self.n * self.sp

    def pack_table(self):
        table = np.zeros((3 * self.ls, self.nyb * self.lanes), np.float32)
        for c in range(3):
            for z in range(self.nz):
                for yb in range(self.nyb):
                    for k in range(self.ry):
                        y = yb * self.ty - 1 + k
                        if 0 <= y < NY:
                            table[
                                c * self.ls + z * NY + y,
                                yb * self.lanes + (c * self.nz + z) * self.ry + k,
                            ] = 1
        return table

    def unpack_table(self):
        table = np.zeros((self.nyb * self.lanes_out, self.image_width), np.float32)
        for c in range(self.image_width // self.ls):
            for z in range(self.nz):
                for y in range(NY):
                    yb, k = divmod(y, self.ty)
                    table[
                        yb * self.lanes_out + (c * self.nz + z) * self.ty + k, c * self.ls + z * NY + y
                    ] = 1
        return table

    def tile_lane(self, c, z, y):
        return (c * self.nz + z) * self.ry + y

    def gradient_table(self):
        table = np.zeros((2 * self.lanes, 3 * self.lanes), np.float32)
        at, wide = self.tile_lane, self.lanes

        def add(column, c, d, z, y, sign=1):
            if d == 0:
                table[wide + at(c, z, y), column] += 1
                return
            table[at(c, z, y), column] -= 1
            if d == 1 and y + 1 < self.ry:
                table[at(c, z, y + 1), column] += 1
            if d == 2 and z + 1 < self.nz:
                table[at(c, z + 1, y), column] += 1

        for z in range(self.nz):
            for y in range(self.ry):
                for c in range(3):
                    for d in range(3):
                        add(d * wide + at(c, z, y), c, d, z, y)
                        add(c * wide + at(c, z, y), d, d, z, y)
        return table

    def divergence_table(self):
        table = np.zeros((3 * self.lanes, self.lanes_out), np.float32)
        at, wide = self.tile_lane, self.lanes
        for c in range(3):
            for z in range(self.nz):
                for y in range(self.ty):
                    column = (c * self.nz + z) * self.ty + y
                    table[at(c, z, y + 1), column] = 1
                    table[wide + at(c, z, y + 1), column] = 1
                    table[wide + at(c, z, y), column] = -1
                    table[2 * wide + at(c, z, y + 1), column] = 1
                    if z:
                        table[2 * wide + at(c, z - 1, y + 1), column] = -1
        return table

    def slope_table(self):
        table = np.zeros((self.ls, 2 * self.ls), np.float32)
        for z in range(self.nz):
            for y in range(NY):
                j = z * NY + y
                table[j, j] = table[j, self.ls + j] = -1
                if y + 1 < NY:
                    table[j + 1, j] = 1
                if z + 1 < self.nz:
                    table[j + NY, self.ls + j] = 1
        return table

    def modulus_table(self):
        table = np.zeros((self.nyb, self.ls, self.lanes), np.float32)
        for yb in range(self.nyb):
            for z in range(self.nz):
                for k in range(self.ry):
                    y = yb * self.ty - 1 + k
                    if 0 <= y < NY:
                        for c in range(3):
                            table[yb, z * NY + y, (c * self.nz + z) * self.ry + k] = 1
        return table


def picked(values, table, parts=3):
    total, rest = None, values
    for part in range(parts):
        head = rest.astype(BF16)
        product = jnp.dot(head, table, preferred_element_type=F32)
        total = product if total is None else total + product
        if part + 1 < parts:
            rest = rest - head.astype(F32)
    return total


def pick_into(out_ref, values_ref, table_ref):
    width = table_ref.shape[1]
    chunk = width if width <= 1024 else 512
    for first in range(0, width, chunk):
        out_ref[:, first : first + chunk] = picked(
            values_ref[:, : table_ref.shape[0]], table_ref[:, first : first + chunk]
        )


def swap_quarters(parts):
    quarter = lax.broadcasted_iota(jnp.int32, parts[0].shape, 1) // NY
    swapped = []
    for j in range(4):
        total = parts[j]
        for i in range(4):
            if i != j:
                turned = pltpu.roll(parts[i], (i - j) % 4 * NY, 1)
                total = jnp.where(quarter == i, turned, total)
        swapped.append(total)
    return swapped


def strided(start, size, step):
    return pl.ds(start, size) if size == 1 or step == 1 else pl.ds(start, size, stride=step)


def store_moduli(plan, chaos_at, moduli_ref, msg_ref):
    quarter = lax.broadcasted_iota(jnp.int32, (1, 128), 1) // NY
    own = [moduli_ref[pl.ds(share * plan.per_share + chaos_at, 1), :] for share in range(plan.shares)]
    count, first = plan.shares * plan.rx, plan.sp * plan.rx
    for xb in range(plan.nxb):
        for start in range(0, count, 4):
            line = jnp.zeros((1, 128), F32)
            for number in range(start, min(count, start + 4)):
                share, k = divmod(number, plan.rx)
                x = xb * plan.tx - 1 + k
                if 0 <= x < NX:
                    piece = own[share][:, x // 4 * 128 : (x // 4 + 1) * 128]
                    turned = pltpu.roll(piece, (number - x) % 4 * NY, 1)
                    line = jnp.where(quarter == number % 4, turned, line)
            row, column = divmod(start // 4, plan.lanes // 128)
            for yb in range(plan.nyb):
                tile = xb * plan.nyb + yb
                msg_ref[tile, first + row : first + row + 1, column * 128 : (column + 1) * 128] = line


def gather_moduli(plan, tile_at, msg_ref, mtab_ref, mods_ref):
    quarter = lax.broadcasted_iota(jnp.int32, (plan.per_share, 128), 1) // NY
    first, rows = plan.sp * plan.rx, plan.rows_in
    table = mtab_ref[lax.rem(tile_at, plan.nyb)]
    mods_ref[...] = jnp.zeros(mods_ref.shape, F32)
    for share in range(plan.shares):
        lines = []
        for k in range(plan.rx):
            number = share * plan.rx + k
            row, column = divmod(number // 4, plan.lanes // 128)
            parts = []
            for t in range(plan.nz // 4):
                total = jnp.zeros((plan.per_share, 128), F32)
                for i in range(4):
                    at, columns = (4 * t + i) * rows + first + row, slice(column * 128, (column + 1) * 128)
                    if plan.lanes == 128:
                        piece = msg_ref[pl.ds(at, plan.per_share, stride=plan.slab * rows), columns]
                    else:
                        lone = [at + j * plan.slab * rows for j in range(plan.per_share)]
                        piece = jnp.concatenate([msg_ref[j : j + 1, columns] for j in lone], axis=0)
                    total = jnp.where(quarter == i, pltpu.roll(piece, (i - number) % 4 * NY, 1), total)
                parts.append(total)
            lines.append(parts[0] if len(parts) == 1 else jnp.concatenate(parts, axis=1))
        here = picked(jnp.concatenate(lines, axis=0), table)
        for k in range(plan.rx):
            for v in range(min(plan.per_share, FIELDS - share * plan.per_share)):
                at = k * plan.per_share + v
                mods_ref[share * plan.per_share + v, k : k + 1, :] = here[at : at + 1]


def store_message(plan, rows_ref, msg_ref):
    blank = jnp.zeros((8, plan.lanes), F32)
    for tile in range(plan.n):
        if tile >= plan.nxb * plan.nyb:
            msg_ref[tile] = jnp.zeros((plan.rows_in, plan.lanes), F32)
            continue
        xb, yb = divmod(tile, plan.nyb)
        msg_ref[tile, plan.rows_in - 8 :, :] = blank
        for k in range(plan.rx):
            x = xb * plan.tx - 1 + k
            if 0 <= x < NX:
                rows = rows_ref[
                    x * plan.hs : x * plan.hs + plan.sp, yb * plan.lanes : (yb + 1) * plan.lanes
                ]
            else:
                rows = jnp.zeros((plan.sp, plan.lanes), F32)
            msg_ref[tile, strided(k, plan.sp, plan.rx), :] = rows


def rows_at(piece_of):
    return [jnp.concatenate(pieces, axis=1) if len(pieces) > 1 else pieces[0] for pieces in zip(*piece_of)]


def start_kernel(plan, place_ref, in_ref, mean_ref, modes_ref, pack_ref, msg_ref, lhs, rows, moduli):
    moduli[...] = jnp.zeros(moduli.shape, F32)
    moduli[0:1] = mean_ref[...]
    moduli[1:FIELDS] = modes_ref[...]
    for a in range(PLANE // 128):
        for c in range(3):
            pieces = rows_at(
                swap_quarters(
                    [
                        in_ref[c, (4 * t + i) * plan.sp : (4 * t + i + 1) * plan.sp, a * 128 : (a + 1) * 128]
                        for i in range(4)
                    ]
                )
                for t in range(plan.slab // 4)
            )
            for b, piece in enumerate(pieces):
                x = 4 * a + b
                lhs[x * plan.hs : x * plan.hs + plan.sp, c * plan.ls : (c + 1) * plan.ls] = piece
    pick_into(rows, lhs, pack_ref)
    store_message(plan, rows, msg_ref)
    store_moduli(plan, jnp.minimum(place_ref[0], plan.per_share - 1), moduli, msg_ref)


def split_kernel(plan, in_ref, mean_ref, out_ref):
    for group in range(plan.slab):
        out_ref[group, 3 * plan.sp : 3 * plan.sp + 1, :] = mean_ref[...]
        for c in range(3):
            out_ref[group, c * plan.sp : (c + 1) * plan.sp, :] = in_ref[
                c, group * plan.sp : (group + 1) * plan.sp, :
            ]


def load_kernel(plan, in_ref, out_ref, mean_ref):
    for a in range(PLANE // 128):
        pieces = rows_at(
            swap_quarters(
                [in_ref[4 * t + i, 3 * plan.sp : 3 * plan.sp + 1, a * 128 : (a + 1) * 128] for i in range(4)]
            )
            for t in range(plan.nz // 4)
        )
        for b, piece in enumerate(pieces):
            mean_ref[4 * a + b] = jnp.broadcast_to(piece, (plan.hs, plan.ls))
        for c in range(3):
            pieces = rows_at(
                swap_quarters(
                    [in_ref[4 * t + i, c * plan.sp : (c + 1) * plan.sp, a * 128 : (a + 1) * 128] for i in range(4)]
                )
                for t in range(plan.nz // 4)
            )
            for b, piece in enumerate(pieces):
                out_ref[4 * a + b, c, 0 : plan.sp, :] = piece


def finish_kernel(plan, in_ref, live_ref, start_ref, total_ref, residual_ref):
    for group in range(plan.slab):
        here = slice(group * plan.sp, (group + 1) * plan.sp)
        live = jnp.broadcast_to(live_ref[here, :], (plan.sp, PLANE)) != 0.0
        for c in range(3):
            total_ref[c, here, :] = jnp.where(live, start_ref[c, here, :], 0.0) + in_ref[
                group, c * plan.sp : (c + 1) * plan.sp, :
            ]
            residual_ref[c, here, :] = in_ref[group, (3 + c) * plan.sp : (4 + c) * plan.sp, :]


def regrouped(plan, msg_ref, out_ref):
    lane = lax.broadcasted_iota(jnp.int32, (plan.rows_in, plan.lanes), 1)
    height = lane % (plan.nz * plan.ry) // plan.ry

    def one(row, carry):
        parts = [
            msg_ref[pl.ds(pl.multiple_of((row * plan.slab + z) * plan.rows_in, 8), plan.rows_in), :] for z in range(plan.nz)
        ]
        for group in range(plan.slab):
            total = parts[group]
            for z in range(plan.nz):
                if z != group:
                    turned = pltpu.roll(parts[z], (z - group) * plan.ry % plan.lanes, 1)
                    total = jnp.where(height == z, turned, total)
            out_ref[row * plan.slab + group] = total
        return carry

    lax.fori_loop(0, plan.chaos, one, 0, unroll=4)


def first_mix_kernel(plan, low_count, parts, place_ref, nodes_ref, level_ref, msg_ref, mtab_ref, grad_ref, div_ref, out_ref, mods_ref, grad, flux, scaled, regroup):
    gather_moduli(plan, place_ref[0] * plan.slab + place_ref[1], msg_ref, mtab_ref, mods_ref)
    regrouped(plan, msg_ref, regroup)
    mix_kernel(plan, low_count, parts, nodes_ref, level_ref, regroup, mods_ref, grad_ref, div_ref, out_ref, grad, flux, scaled)


def mix_kernel(plan, low_count, parts, nodes_ref, level_ref, msg_ref, mods_ref, grad_ref, div_ref, out_ref, grad, flux, scaled):
    sp, rx, tx, lanes = plan.sp, plan.rx, plan.tx, plan.lanes
    for level in range(DEG):
        for v in range(KL):
            scaled[level * KL + v] = mods_ref[v + 1] * math.sqrt(level + 1)
    mean = mods_ref[0]

    def gradients(chunk, carry):
        windows, behind = [], []
        for i in range(4):
            source = chunk * 4 + i
            for s in range(sp):
                windows.append(msg_ref[source, s * rx : s * rx + 8, :])
                if s * rx + 9 <= plan.rows_in:
                    behind.append(msg_ref[source, s * rx + 1 : s * rx + 9, :])
                else:
                    behind.append(pltpu.roll(windows[-1], 7, 0))
        own = jnp.concatenate(windows, axis=0)
        slope_x = jnp.concatenate(behind, axis=0) - own
        full = picked(jnp.concatenate([own, slope_x], axis=1), grad_ref[...], parts)
        here = pl.ds(chunk * 4 * sp, 4 * sp)
        for d in range(3):
            part = full[:, d * lanes : (d + 1) * lanes].reshape(4 * sp, 8, lanes)
            grad[here, d] = part
            flux[here, d] = mean * part
        return carry

    lax.fori_loop(0, plan.n // 4, gradients, 0, unroll=8)

    def edges(number, carry):
        base = nodes_ref[number]
        own = [grad[base, d] for d in range(3)]
        total = [flux[base, d] for d in range(3)]
        for group in range(0, KL, 5):
            at = [nodes_ref[low_count + number * KL + v] for v in range(group, group + 5)]
            field = [scaled[level_ref[number * KL + v] * KL + v] for v in range(group, group + 5)]
            fresh = [
                [flux[spot, d] + weight * own[d] for d in range(3)] for spot, weight in zip(at, field)
            ]
            for spot, weight in zip(at, field):
                total = [total[d] + weight * grad[spot, d] for d in range(3)]
            for spot, values in zip(at, fresh):
                for d in range(3):
                    flux[spot, d] = values[d]
        for d in range(3):
            flux[base, d] = total[d]
        return carry

    lax.fori_loop(0, low_count, edges, 0, unroll=2)

    def divergences(chunk, carry):
        here = pl.ds(chunk * 4 * sp, 4 * sp)
        flux_x, flux_y, flux_z = (flux[here, d] for d in range(3))
        flux_x = flux_x - pltpu.roll(flux_x, 1, 1)
        values = jnp.concatenate([flux_x, flux_y, flux_z], axis=2).reshape(4 * sp * 8, 3 * lanes)
        total = picked(values, div_ref[...], parts).reshape(4, sp, 8, plan.lanes_out)
        for i in range(4):
            for s in range(plan.kept):
                out_ref[chunk * 4 + i, s * tx : (s + 1) * tx, :] = total[i, s, 1 : 1 + tx]
            for number in range(3 * plan.moved):
                slot, c = plan.kept + number // 3, number % 3
                turned = pltpu.roll(total[i, slot], (3 - c) * plan.segment, 1)
                out_ref[chunk * 4 + i, number * tx : (number + 1) * tx, 3 * plan.segment : 4 * plan.segment] = turned[
                    1 : 1 + tx, 3 * plan.segment : 4 * plan.segment
                ]
        return carry

    lax.fori_loop(0, plan.n // 4, divergences, 0, unroll=8)


def unpack_image(plan, image_ref, unpack_ref, lhs, rows):
    for xb in range(plan.nxb):
        for k in range(plan.tx):
            x = xb * plan.tx + k
            for yb in range(plan.nyb):
                lhs[x * plan.hs : x * plan.hs + plan.kept, yb * plan.lanes_out : (yb + 1) * plan.lanes_out] = image_ref[
                    xb * plan.nyb + yb, strided(k, plan.kept, plan.tx), :
                ]
    pick_into(rows, lhs, unpack_ref)


def add_image(plan, base_ref, live_ref, rows, residual_ref):
    live = live_ref[...] != 0.0
    slot = lax.broadcasted_iota(jnp.int32, (plan.hs, plan.ls), 0)

    def one(x, carry):
        block = rows.at[pl.ds(pl.multiple_of(x * plan.hs, plan.hs), plan.hs)]
        for c in range(3):
            image = block[:, c * plan.ls : (c + 1) * plan.ls]
            for q in range(plan.moved):
                line = block[3 * q + c : 3 * q + c + 1, 3 * plan.ls : 4 * plan.ls]
                image = jnp.where(slot == plan.kept + q, line, image)
            residual_ref[x, c] = jnp.where(live, base_ref[x, c] + image, 0.0)
        return carry

    lax.fori_loop(0, NX, one, 0, unroll=6)


def smooth(plan, mean_ref, slope_ref, back_ref, residual_ref, update, step):
    hs, ls, many = plan.hs, plan.ls, 6
    center_value = 0.5 * (bound_high + bound_low)
    half_width = 0.5 * (bound_high - bound_low)
    ratio_value = center_value / half_width

    def first(x, carry):
        for c in range(3):
            scaled = residual_ref[x, c] * (1.0 / center_value)
            update[x, c] = scaled
            step[x, c] = scaled
        return carry

    lax.fori_loop(0, NX, first, 0, unroll=6)
    update[NX] = jnp.zeros((3, hs, ls), F32)

    rho_prev = 1.0 / ratio_value
    for sweep in range(SWEEPS):
        rho_next = 1.0 / (2.0 * ratio_value - rho_prev)
        keep, gain = rho_next * rho_prev, 2.0 * rho_next / half_width

        def slabs_of(chunk, behind, keep=keep, gain=gain):
            here = pl.ds(chunk * many, many)
            own = update[here]
            slope_x = update[pl.ds(chunk * many + 1, many)] - own
            slopes = picked(own.reshape(many * 3 * hs, ls), slope_ref[...], 2)
            slopes = slopes.reshape(many, 3, hs, 2 * ls)
            modulus = mean_ref[here]
            spread = slope_x[:, 0] + slopes[:, 1, :, :ls] + slopes[:, 2, :, ls:]
            flux_x, flux_yz = [], []
            for c in range(3):
                parts = [slope_x[:, c], slopes[:, c, :, :ls], slopes[:, c, :, ls:]]
                parts[c] = parts[c] + spread
                flux_x.append(modulus * parts[0])
                flux_yz.append(jnp.concatenate([modulus * parts[1], modulus * parts[2]], axis=-1))
            flux_yz = jnp.stack(flux_yz, axis=1).reshape(many * 3 * hs, 2 * ls)
            back = picked(flux_yz, back_ref[...], 2).reshape(many, 3, hs, ls)
            for c in range(3):
                earlier = jnp.concatenate([behind[c][None], flux_x[c][:-1]], axis=0)
                total = flux_x[c] - earlier - back[:, c]
                moved = keep * step[here, c] + gain * (residual_ref[here, c] + total)
                step[here, c] = moved
                update[here, c] = own[:, c] + moved
            return tuple(flux[-1] for flux in flux_x)

        zero = jnp.zeros((hs, ls), F32)
        lax.fori_loop(0, NX // many, slabs_of, (zero, zero, zero), unroll=4)
        rho_prev = rho_next


def middle_kernel(plan, image_ref, base_ref, live_ref, mean_ref, slope_ref, back_ref, unpack_ref, pack_ref, msg_ref, residual_ref, update_ref, wide, narrow, step):
    unpack_image(plan, image_ref, unpack_ref, wide, narrow)
    add_image(plan, base_ref, live_ref, narrow, residual_ref)
    smooth(plan, mean_ref, slope_ref, back_ref, residual_ref, update_ref, step)
    for x in range(NX):
        for c in range(3):
            narrow[x * plan.hs : (x + 1) * plan.hs, c * plan.ls : (c + 1) * plan.ls] = update_ref[x, c]
    pick_into(wide, narrow, pack_ref)
    store_message(plan, wide, msg_ref)


def flat_rows(plan, values, out_ref, first, a):
    for t in range(plan.nz // 4):
        parts = [value[:, t * 128 : (t + 1) * 128] for value in values]
        for i, piece in enumerate(swap_quarters(parts)):
            out_ref[4 * t + i, first : first + plan.sp, a * 128 : (a + 1) * 128] = piece[: plan.sp]


def end_kernel(plan, image_ref, base_ref, live_ref, mean_ref, slope_ref, back_ref, unpack_ref, before_ref, out_ref, wide, narrow, residual, update, step):
    unpack_image(plan, image_ref, unpack_ref, wide, narrow)
    add_image(plan, base_ref, live_ref, narrow, residual)
    smooth(plan, mean_ref, slope_ref, back_ref, residual, update, step)
    for a in range(PLANE // 128):
        for c in range(3):
            flat_rows(plan, [update[4 * a + b, c] + before_ref[4 * a + b, c] for b in range(4)], out_ref, c * plan.sp, a)
            flat_rows(plan, [residual[4 * a + b, c] for b in range(4)], out_ref, (3 + c) * plan.sp, a)


def per_device(displacement, load, mean_modulus, modes, owner):
    chaos, slab = lax.axis_size("chaos"), lax.axis_size("slab")
    slots_dev, slots_all = displacement.shape[0], owner.shape[0]
    plan = Plan(chaos, slab, slots_dev)
    n, sp, hs, ls, lanes = plan.n, plan.sp, plan.hs, plan.ls, plan.lanes
    count, low, raised, level = edge_tables()
    at_chaos, at_slab = lax.axis_index("chaos"), lax.axis_index("slab")

    slots = np.arange(slots_all)
    places = (slots // slots_dev) * (slab * sp) + slots % slots_dev
    wanted = np.concatenate([low, raised])
    nodes = jnp.sum(
        jnp.where(wanted[:, None] == owner[None, :], jnp.asarray(places, jnp.int32)[None, :], 0), axis=1
    ).astype(jnp.int32)
    live_all = owner < count
    live_own = lax.dynamic_slice_in_dim(live_all, at_chaos * slots_dev, slots_dev, 0)
    live_here = jnp.pad(live_own.astype(F32), (0, slab * sp - slots_dev))
    live_here = lax.dynamic_slice_in_dim(live_here, at_slab * sp, sp, 0)
    live_here = jnp.broadcast_to(jnp.pad(live_here, (0, hs - sp))[:, None], (hs, ls))

    pack = jnp.asarray(plan.pack_table(), BF16)
    unpack = jnp.asarray(plan.unpack_table(), BF16)
    mtab = jnp.asarray(plan.modulus_table(), BF16)
    slopes, backs = (jnp.asarray(values, BF16) for values in (plan.slope_table(), plan.slope_table().T))
    grads, divs = (jnp.asarray(values, BF16) for values in (plan.gradient_table(), plan.divergence_table()))
    place = jnp.stack([at_chaos, at_slab]).astype(jnp.int32)

    slots_pad = slab * sp

    def by_component(values):
        return jnp.pad(jnp.transpose(values, (1, 0, 2)), ((0, 0), (0, slots_pad - slots_dev), (0, 0)))

    def everyone(values):
        return lax.all_to_all(values, ("chaos", "slab"), 0, 0, tiled=True)

    def column(values):
        return lax.all_to_all(values, "slab", 0, 0, tiled=True)

    smem = pl.BlockSpec(memory_space=pltpu.SMEM)
    vmem = pl.BlockSpec(memory_space=pltpu.VMEM)

    def call(kernel, name, in_specs, out_shape, scratch_shapes):
        return pl.pallas_call(
            kernel,
            out_shape=out_shape,
            in_specs=in_specs,
            out_specs=jax.tree.map(lambda _: vmem, out_shape),
            scratch_shapes=scratch_shapes,
            compiler_params=pltpu.CompilerParams(vmem_limit_bytes=(16 if plan.positions <= 512 and n <= 64 else 60) * MIB),
            name=name,
        )

    def array(*shape):
        return jax.ShapeDtypeStruct(shape, F32)

    message, image = array(n, plan.rows_in, lanes), array(n, plan.rows_out, plan.lanes_out)
    grid_field, grid_more = array(NX, 3, hs, ls), array(NX + 1, 3, hs, ls)
    wide = pltpu.VMEM((NX * hs, plan.nyb * lanes), F32)
    narrow = pltpu.VMEM((NX * hs, plan.image_width), F32)
    field_scratch, more_scratch = pltpu.VMEM(grid_field.shape, F32), pltpu.VMEM(grid_more.shape, F32)

    mean_row = mean_modulus.reshape(1, PLANE)
    msg = call(
        functools.partial(start_kernel, plan),
        "start",
        [smem, vmem, vmem, vmem, vmem],
        message,
        [narrow, wide, pltpu.VMEM((16, PLANE), F32)],
    )(place, by_component(displacement), mean_row, modes, pack)
    levels = jnp.asarray(level, jnp.int32)
    mix_scratch = [
        pltpu.VMEM((plan.positions, 3, 8, lanes), F32),
        pltpu.VMEM((plan.positions, 3, 8, lanes), F32),
        pltpu.VMEM((DEG * KL, 8, lanes), F32),
    ]

    arrived = everyone(msg)
    flat, parts = array(slab, plan.rows_flat, PLANE), array(3, slots_pad, PLANE)
    load_flat = call(functools.partial(split_kernel, plan), "split", [vmem, vmem], flat, [])(
        by_component(load), mean_row
    )
    load_flat, nodes, place = lax.optimization_barrier((load_flat, nodes, place))
    load_flat, arrived = lax.optimization_barrier((load_flat, arrived))
    load_s, mean_s = call(functools.partial(load_kernel, plan), "load", [vmem], (grid_field, array(NX, hs, ls)), [])(
        column(load_flat)
    )
    first_image, mods = call(
        functools.partial(first_mix_kernel, plan, len(low), 3),
        "mix",
        [smem, smem, smem, vmem, vmem, vmem, vmem],
        (image, array(FIELDS, 8, lanes)),
        mix_scratch + [pltpu.VMEM((n, plan.rows_in, lanes), F32)],
    )(place, nodes, levels, arrived.reshape(n * plan.rows_in, lanes), mtab, grads, divs)
    msg, residual_s, update_s = call(
        functools.partial(middle_kernel, plan),
        "middle",
        [vmem] * 8,
        (message, grid_field, grid_more),
        [wide, narrow, field_scratch],
    )(everyone(first_image), load_s, live_here, mean_s, slopes, backs, unpack, pack)

    second_image = call(
        functools.partial(mix_kernel, plan, len(low), 2), "mix", [smem, smem, vmem, vmem, vmem, vmem], image, mix_scratch
    )(nodes, levels, everyone(msg), mods, grads, divs)
    ending = call(
        functools.partial(end_kernel, plan),
        "end",
        [vmem] * 8,
        array(slab, plan.rows_end, PLANE),
        [wide, narrow, field_scratch, more_scratch, field_scratch],
    )(everyone(second_image), residual_s, live_here, mean_s, slopes, backs, unpack, update_s)
    live_pad = jnp.pad(live_own.astype(F32), (0, slots_pad - slots_dev))
    outs = call(functools.partial(finish_kernel, plan), "finish", [vmem] * 3, (parts, parts), [])(
        column(ending), live_pad[:, None], by_component(displacement)
    )
    return tuple(jnp.transpose(values, (1, 0, 2))[:slots_dev] for values in outs)


def solution(mesh):
    in_specs = (P("chaos", None, "slab"), P("chaos", None, "slab"), P("slab"), P(None, "slab"), P())
    out_specs = (P("chaos", None, "slab"), P("chaos", None, "slab"))
    return jax.shard_map(
        per_device, mesh=mesh, in_specs=in_specs, out_specs=out_specs, check_vma=False
    )
```

```python
import functools
import math

import jax
import jax.numpy as jnp
import numpy as np
from jax import lax
from jax.experimental import pallas as pl
from jax.experimental.pallas import tpu as pltpu
from jax.sharding import PartitionSpec as P

NX = 24
NY = 32
KL = 10
DEG = 3
SWEEPS = 4
PLANE = NX * NY
FIELDS = KL + 1

bound_high = 50.0
bound_low = 2.5
MIB = 1024 * 1024
F32 = jnp.float32
BF16 = jnp.bfloat16


def up8(count):
    return -(-count // 8) * 8


def multi_indices():
    listing = [[]]
    for variable in range(KL):
        extended_list = []
        for prefix in listing:
            for degree in range(DEG + 1 - sum(prefix)):
                extended_list.append(prefix + [degree])
        listing = extended_list
    return listing


def edge_tables():
    listing = multi_indices()
    lookup = {tuple(entry): number for number, entry in enumerate(listing)}
    low, raised, level = [], [], []
    for number, entry in enumerate(listing):
        if sum(entry) == DEG:
            continue
        low.append(number)
        for variable in range(KL):
            other = list(entry)
            other[variable] += 1
            raised.append(lookup[tuple(other)])
            level.append(entry[variable])
    return len(listing), np.array(low, np.int32), np.array(raised, np.int32), np.array(level, np.int32)


class Plan:
    def __init__(self, chaos, slab, slots_dev):
        self.chaos, self.slab, self.slots_dev = chaos, slab, slots_dev
        self.n = chaos * slab
        self.nz = slab
        self.sp = -(-slots_dev // slab)
        self.hs = up8(self.sp)
        self.ls = self.nz * NY
        best = None
        for tx in range(1, 7):
            for ty in range(1, NY + 1):
                if NX % tx or NY % ty or (NX // tx) * (NY // ty) > self.n:
                    continue
                lanes = -(-3 * self.nz * (ty + 2) // 128) * 128
                rows = up8((self.sp - 1) * (tx + 2) + 8)
                key = (-(NX // tx) * (NY // ty), rows * lanes)
                if best is None or key < best[0]:
                    best = (key, tx, ty, lanes, rows)
        _, self.tx, self.ty, self.lanes, self.rows_in = best
        self.rx = self.tx + 2
        self.ry = self.ty + 2
        self.nxb, self.nyb = NX // self.tx, NY // self.ty
        self.lanes_out = -(-3 * self.nz * self.ty // 128) * 128
        self.segment = self.nz * self.ty
        self.moved = self.sp // 4 if self.lanes_out >= 4 * self.segment else 0
        self.kept = self.sp - self.moved
        self.rows_out = up8(self.kept * self.tx)
        self.image_width = (4 if self.moved else 3) * self.ls
        self.rows_flat = up8(3 * self.sp + 1)
        self.rows_end = up8(6 * self.sp)
        self.shares = -(-FIELDS // min(chaos, 16))
        self.per_share = 16 // self.shares
        self.positions = self.n * self.sp

    def pack_table(self):
        table = np.zeros((3 * self.ls, self.nyb * self.lanes), np.float32)
        for c in range(3):
            for z in range(self.nz):
                for yb in range(self.nyb):
                    for k in range(self.ry):
                        y = yb * self.ty - 1 + k
                        if 0 <= y < NY:
                            table[
                                c * self.ls + z * NY + y,
                                yb * self.lanes + (c * self.nz + z) * self.ry + k,
                            ] = 1
        return table

    def unpack_table(self):
        table = np.zeros((self.nyb * self.lanes_out, self.image_width), np.float32)
        for c in range(self.image_width // self.ls):
            for z in range(self.nz):
                for y in range(NY):
                    yb, k = divmod(y, self.ty)
                    table[
                        yb * self.lanes_out + (c * self.nz + z) * self.ty + k, c * self.ls + z * NY + y
                    ] = 1
        return table

    def tile_lane(self, c, z, y):
        return (c * self.nz + z) * self.ry + y

    def gradient_table(self):
        table = np.zeros((2 * self.lanes, 3 * self.lanes), np.float32)
        at, wide = self.tile_lane, self.lanes

        def add(column, c, d, z, y, sign=1):
            if d == 0:
                table[wide + at(c, z, y), column] += 1
                return
            table[at(c, z, y), column] -= 1
            if d == 1 and y + 1 < self.ry:
                table[at(c, z, y + 1), column] += 1
            if d == 2 and z + 1 < self.nz:
                table[at(c, z + 1, y), column] += 1

        for z in range(self.nz):
            for y in range(self.ry):
                for c in range(3):
                    for d in range(3):
                        add(d * wide + at(c, z, y), c, d, z, y)
                        add(c * wide + at(c, z, y), d, d, z, y)
        return table

    def divergence_table(self):
        table = np.zeros((3 * self.lanes, self.lanes_out), np.float32)
        at, wide = self.tile_lane, self.lanes
        for c in range(3):
            for z in range(self.nz):
                for y in range(self.ty):
                    column = (c * self.nz + z) * self.ty + y
                    table[at(c, z, y + 1), column] = 1
                    table[wide + at(c, z, y + 1), column] = 1
                    table[wide + at(c, z, y), column] = -1
                    table[2 * wide + at(c, z, y + 1), column] = 1
                    if z:
                        table[2 * wide + at(c, z - 1, y + 1), column] = -1
        return table

    def slope_table(self):
        table = np.zeros((self.ls, 2 * self.ls), np.float32)
        for z in range(self.nz):
            for y in range(NY):
                j = z * NY + y
                table[j, j] = table[j, self.ls + j] = -1
                if y + 1 < NY:
                    table[j + 1, j] = 1
                if z + 1 < self.nz:
                    table[j + NY, self.ls + j] = 1
        return table

    def modulus_table(self):
        table = np.zeros((self.nyb, self.ls, self.lanes), np.float32)
        for yb in range(self.nyb):
            for z in range(self.nz):
                for k in range(self.ry):
                    y = yb * self.ty - 1 + k
                    if 0 <= y < NY:
                        for c in range(3):
                            table[yb, z * NY + y, (c * self.nz + z) * self.ry + k] = 1
        return table


def picked(values, table, parts=3):
    total, rest = None, values
    for part in range(parts):
        head = rest.astype(BF16)
        product = jnp.dot(head, table, preferred_element_type=F32)
        total = product if total is None else total + product
        if part + 1 < parts:
            rest = rest - head.astype(F32)
    return total


def pick_into(out_ref, values_ref, table_ref):
    width = table_ref.shape[1]
    chunk = width if width <= 1024 else 512
    for first in range(0, width, chunk):
        out_ref[:, first : first + chunk] = picked(
            values_ref[:, : table_ref.shape[0]], table_ref[:, first : first + chunk]
        )


def swap_quarters(parts):
    quarter = lax.broadcasted_iota(jnp.int32, parts[0].shape, 1) // NY
    swapped = []
    for j in range(4):
        total = parts[j]
        for i in range(4):
            if i != j:
                turned = pltpu.roll(parts[i], (i - j) % 4 * NY, 1)
                total = jnp.where(quarter == i, turned, total)
        swapped.append(total)
    return swapped


def strided(start, size, step):
    return pl.ds(start, size) if size == 1 or step == 1 else pl.ds(start, size, stride=step)


def store_moduli(plan, chaos_at, moduli_ref, msg_ref):
    quarter = lax.broadcasted_iota(jnp.int32, (1, 128), 1) // NY
    own = [moduli_ref[pl.ds(share * plan.per_share + chaos_at, 1), :] for share in range(plan.shares)]
    count, first = plan.shares * plan.rx, plan.sp * plan.rx
    for xb in range(plan.nxb):
        for start in range(0, count, 4):
            line = jnp.zeros((1, 128), F32)
            for number in range(start, min(count, start + 4)):
                share, k = divmod(number, plan.rx)
                x = xb * plan.tx - 1 + k
                if 0 <= x < NX:
                    piece = own[share][:, x // 4 * 128 : (x // 4 + 1) * 128]
                    turned = pltpu.roll(piece, (number - x) % 4 * NY, 1)
                    line = jnp.where(quarter == number % 4, turned, line)
            row, column = divmod(start // 4, plan.lanes // 128)
            for yb in range(plan.nyb):
                tile = xb * plan.nyb + yb
                msg_ref[tile, first + row : first + row + 1, column * 128 : (column + 1) * 128] = line


def gather_moduli(plan, tile_at, msg_ref, mtab_ref, mods_ref):
    quarter = lax.broadcasted_iota(jnp.int32, (plan.per_share, 128), 1) // NY
    first, rows = plan.sp * plan.rx, plan.rows_in
    table = mtab_ref[lax.rem(tile_at, plan.nyb)]
    mods_ref[...] = jnp.zeros(mods_ref.shape, F32)
    for share in range(plan.shares):
        lines = []
        for k in range(plan.rx):
            number = share * plan.rx + k
            row, column = divmod(number // 4, plan.lanes // 128)
            parts = []
            for t in range(plan.nz // 4):
                total = jnp.zeros((plan.per_share, 128), F32)
                for i in range(4):
                    at, columns = (4 * t + i) * rows + first + row, slice(column * 128, (column + 1) * 128)
                    if plan.lanes == 128:
                        piece = msg_ref[pl.ds(at, plan.per_share, stride=plan.slab * rows), columns]
                    else:
                        lone = [at + j * plan.slab * rows for j in range(plan.per_share)]
                        piece = jnp.concatenate([msg_ref[j : j + 1, columns] for j in lone], axis=0)
                    total = jnp.where(quarter == i, pltpu.roll(piece, (i - number) % 4 * NY, 1), total)
                parts.append(total)
            lines.append(parts[0] if len(parts) == 1 else jnp.concatenate(parts, axis=1))
        here = picked(jnp.concatenate(lines, axis=0), table)
        for k in range(plan.rx):
            for v in range(min(plan.per_share, FIELDS - share * plan.per_share)):
                at = k * plan.per_share + v
                mods_ref[share * plan.per_share + v, k : k + 1, :] = here[at : at + 1]


def store_message(plan, rows_ref, msg_ref):
    blank = jnp.zeros((8, plan.lanes), F32)
    for tile in range(plan.n):
        if tile >= plan.nxb * plan.nyb:
            msg_ref[tile] = jnp.zeros((plan.rows_in, plan.lanes), F32)
            continue
        xb, yb = divmod(tile, plan.nyb)
        msg_ref[tile, plan.rows_in - 8 :, :] = blank
        for k in range(plan.rx):
            x = xb * plan.tx - 1 + k
            if 0 <= x < NX:
                rows = rows_ref[
                    x * plan.hs : x * plan.hs + plan.sp, yb * plan.lanes : (yb + 1) * plan.lanes
                ]
            else:
                rows = jnp.zeros((plan.sp, plan.lanes), F32)
            msg_ref[tile, strided(k, plan.sp, plan.rx), :] = rows


def rows_at(piece_of):
    return [jnp.concatenate(pieces, axis=1) if len(pieces) > 1 else pieces[0] for pieces in zip(*piece_of)]


def start_kernel(plan, place_ref, in_hbm, mean_hbm, modes_hbm, pack_hbm, msg_ref, lhs, rows, moduli, in_ref, mean_ref, modes_ref, pack_ref, arrived):
    pairs = ((in_hbm, in_ref), (pack_hbm, pack_ref), (mean_hbm, mean_ref), (modes_hbm, modes_ref))
    copies = [pltpu.make_async_copy(source, target, arrived.at[i]) for i, (source, target) in enumerate(pairs)]
    for copy in copies:
        copy.start()
    copies[0].wait()
    for a in range(PLANE // 128):
        for c in range(3):
            pieces = rows_at(
                swap_quarters(
                    [
                        in_ref[c, (4 * t + i) * plan.sp : (4 * t + i + 1) * plan.sp, a * 128 : (a + 1) * 128]
                        for i in range(4)
                    ]
                )
                for t in range(plan.slab // 4)
            )
            for b, piece in enumerate(pieces):
                x = 4 * a + b
                lhs[x * plan.hs : x * plan.hs + plan.sp, c * plan.ls : (c + 1) * plan.ls] = piece
    copies[1].wait()
    pick_into(rows, lhs, pack_ref)
    store_message(plan, rows, msg_ref)
    copies[2].wait()
    copies[3].wait()
    moduli[...] = jnp.zeros(moduli.shape, F32)
    for a in range(PLANE // 128):
        moduli[0:1, a * 128 : (a + 1) * 128] = mean_ref[a : a + 1, :]
    moduli[1:FIELDS] = modes_ref[...]
    store_moduli(plan, jnp.minimum(place_ref[0], plan.per_share - 1), moduli, msg_ref)


def split_kernel(plan, place_ref, in_ref, mean_ref, *refs):
    out_refs, groups = refs[: plan.slab], refs[plan.slab]
    for group in range(plan.slab):
        step = lax.rem(group + plan.slab - place_ref[1], plan.slab)
        for c in range(3):
            groups[step, c * plan.sp : (c + 1) * plan.sp, :] = in_ref[c, group * plan.sp : (group + 1) * plan.sp, :]
        groups[step, 3 * plan.sp : 3 * plan.sp + 1, :] = mean_ref[...]
    for step, out_ref in enumerate(out_refs):
        out_ref[...] = groups[step]


def load_kernel(plan, place_ref, *refs):
    in_refs, (out_ref, mean_ref, planes) = refs[: plan.slab], refs[plan.slab :]
    for step, in_ref in enumerate(in_refs):
        planes[lax.rem(place_ref[1] + (plan.slab - step), plan.slab)] = in_ref[...]
    for a in range(PLANE // 128):
        lanes = slice(a * 128, (a + 1) * 128)
        pieces = rows_at(
            swap_quarters([planes[4 * t + i, 3 * plan.sp : 3 * plan.sp + 1, lanes] for i in range(4)])
            for t in range(plan.nz // 4)
        )
        for b, piece in enumerate(pieces):
            mean_ref[4 * a + b] = jnp.broadcast_to(piece, (plan.hs, plan.ls))
        for c in range(3):
            pieces = rows_at(
                swap_quarters([planes[4 * t + i, c * plan.sp : (c + 1) * plan.sp, lanes] for i in range(4)])
                for t in range(plan.nz // 4)
            )
            for b, piece in enumerate(pieces):
                out_ref[4 * a + b, c, 0 : plan.sp, :] = piece


def finish_kernel(plan, in_ref, live_ref, start_ref, total_ref, residual_ref):
    for group in range(plan.slab):
        here = slice(group * plan.sp, (group + 1) * plan.sp)
        live = jnp.broadcast_to(live_ref[here, :], (plan.sp, PLANE)) != 0.0
        for c in range(3):
            total_ref[c, here, :] = jnp.where(live, start_ref[c, here, :], 0.0) + in_ref[
                group, c * plan.sp : (c + 1) * plan.sp, :
            ]
            residual_ref[c, here, :] = in_ref[group, (3 + c) * plan.sp : (4 + c) * plan.sp, :]


def regrouped(plan, msg_ref, out_ref):
    lane = lax.broadcasted_iota(jnp.int32, (plan.rows_in, plan.lanes), 1)
    height = lane % (plan.nz * plan.ry) // plan.ry

    def one(row, carry):
        parts = [
            msg_ref[pl.ds(pl.multiple_of((row * plan.slab + z) * plan.rows_in, 8), plan.rows_in), :] for z in range(plan.nz)
        ]
        for group in range(plan.slab):
            total = parts[group]
            for z in range(plan.nz):
                if z != group:
                    turned = pltpu.roll(parts[z], (z - group) * plan.ry % plan.lanes, 1)
                    total = jnp.where(height == z, turned, total)
            out_ref[row * plan.slab + group] = total
        return carry

    lax.fori_loop(0, plan.chaos, one, 0, unroll=4)


def first_mix_kernel(plan, low_count, parts, place_ref, nodes_ref, level_ref, msg_ref, mtab_ref, grad_ref, div_ref, out_ref, mods_ref, grad, flux, scaled, regroup):
    gather_moduli(plan, place_ref[0] * plan.slab + place_ref[1], msg_ref, mtab_ref, mods_ref)
    regrouped(plan, msg_ref, regroup)
    mix_kernel(plan, low_count, parts, nodes_ref, level_ref, regroup, mods_ref, grad_ref, div_ref, out_ref, grad, flux, scaled)


def mix_kernel(plan, low_count, parts, nodes_ref, level_ref, msg_ref, mods_ref, grad_ref, div_ref, out_ref, grad, flux, scaled):
    sp, rx, tx, lanes = plan.sp, plan.rx, plan.tx, plan.lanes
    for level in range(DEG):
        for v in range(KL):
            scaled[level * KL + v] = mods_ref[v + 1] * math.sqrt(level + 1)
    mean = mods_ref[0]

    def gradients(chunk, carry):
        windows, behind = [], []
        for i in range(4):
            source = chunk * 4 + i
            for s in range(sp):
                windows.append(msg_ref[source, s * rx : s * rx + 8, :])
                if s * rx + 9 <= plan.rows_in:
                    behind.append(msg_ref[source, s * rx + 1 : s * rx + 9, :])
                else:
                    behind.append(pltpu.roll(windows[-1], 7, 0))
        own = jnp.concatenate(windows, axis=0)
        slope_x = jnp.concatenate(behind, axis=0) - own
        full = picked(jnp.concatenate([own, slope_x], axis=1), grad_ref[...], parts)
        here = pl.ds(chunk * 4 * sp, 4 * sp)
        for d in range(3):
            part = full[:, d * lanes : (d + 1) * lanes].reshape(4 * sp, 8, lanes)
            grad[here, d] = part
            flux[here, d] = mean * part
        return carry

    lax.fori_loop(0, plan.n // 4, gradients, 0, unroll=8)

    def edges(number, carry):
        base = nodes_ref[number]
        own = [grad[base, d] for d in range(3)]
        total = [flux[base, d] for d in range(3)]
        for group in range(0, KL, 5):
            at = [nodes_ref[low_count + number * KL + v] for v in range(group, group + 5)]
            field = [scaled[level_ref[number * KL + v] * KL + v] for v in range(group, group + 5)]
            fresh = [
                [flux[spot, d] + weight * own[d] for d in range(3)] for spot, weight in zip(at, field)
            ]
            for spot, weight in zip(at, field):
                total = [total[d] + weight * grad[spot, d] for d in range(3)]
            for spot, values in zip(at, fresh):
                for d in range(3):
                    flux[spot, d] = values[d]
        for d in range(3):
            flux[base, d] = total[d]
        return carry

    lax.fori_loop(0, low_count, edges, 0, unroll=2)

    def divergences(chunk, carry):
        here = pl.ds(chunk * 4 * sp, 4 * sp)
        flux_x, flux_y, flux_z = (flux[here, d] for d in range(3))
        flux_x = flux_x - pltpu.roll(flux_x, 1, 1)
        values = jnp.concatenate([flux_x, flux_y, flux_z], axis=2).reshape(4 * sp * 8, 3 * lanes)
        total = picked(values, div_ref[...], parts).reshape(4, sp, 8, plan.lanes_out)
        for i in range(4):
            for s in range(plan.kept):
                out_ref[chunk * 4 + i, s * tx : (s + 1) * tx, :] = total[i, s, 1 : 1 + tx]
            for number in range(3 * plan.moved):
                slot, c = plan.kept + number // 3, number % 3
                turned = pltpu.roll(total[i, slot], (3 - c) * plan.segment, 1)
                out_ref[chunk * 4 + i, number * tx : (number + 1) * tx, 3 * plan.segment : 4 * plan.segment] = turned[
                    1 : 1 + tx, 3 * plan.segment : 4 * plan.segment
                ]
        return carry

    lax.fori_loop(0, plan.n // 4, divergences, 0, unroll=8)


def unpack_image(plan, image_ref, unpack_ref, lhs, rows):
    for xb in range(plan.nxb):
        for k in range(plan.tx):
            x = xb * plan.tx + k
            for yb in range(plan.nyb):
                lhs[x * plan.hs : x * plan.hs + plan.kept, yb * plan.lanes_out : (yb + 1) * plan.lanes_out] = image_ref[
                    xb * plan.nyb + yb, strided(k, plan.kept, plan.tx), :
                ]
    pick_into(rows, lhs, unpack_ref)


def add_image(plan, base_ref, live_ref, rows, residual_ref):
    live = live_ref[...] != 0.0
    slot = lax.broadcasted_iota(jnp.int32, (plan.hs, plan.ls), 0)

    def one(x, carry):
        block = rows.at[pl.ds(pl.multiple_of(x * plan.hs, plan.hs), plan.hs)]
        for c in range(3):
            image = block[:, c * plan.ls : (c + 1) * plan.ls]
            for q in range(plan.moved):
                line = block[3 * q + c : 3 * q + c + 1, 3 * plan.ls : 4 * plan.ls]
                image = jnp.where(slot == plan.kept + q, line, image)
            residual_ref[x, c] = jnp.where(live, base_ref[x, c] + image, 0.0)
        return carry

    lax.fori_loop(0, NX, one, 0, unroll=6)


def smooth(plan, mean_ref, slope_ref, back_ref, residual_ref, update, step):
    hs, ls, many = plan.hs, plan.ls, 6
    center_value = 0.5 * (bound_high + bound_low)
    half_width = 0.5 * (bound_high - bound_low)
    ratio_value = center_value / half_width

    def first(x, carry):
        for c in range(3):
            scaled = residual_ref[x, c] * (1.0 / center_value)
            update[x, c] = scaled
            step[x, c] = scaled
        return carry

    lax.fori_loop(0, NX, first, 0, unroll=6)
    update[NX] = jnp.zeros((3, hs, ls), F32)

    rho_prev = 1.0 / ratio_value
    for sweep in range(SWEEPS):
        rho_next = 1.0 / (2.0 * ratio_value - rho_prev)
        keep, gain = rho_next * rho_prev, 2.0 * rho_next / half_width

        def slabs_of(chunk, behind, keep=keep, gain=gain):
            here = pl.ds(chunk * many, many)
            own = update[here]
            slope_x = update[pl.ds(chunk * many + 1, many)] - own
            slopes = picked(own.reshape(many * 3 * hs, ls), slope_ref[...], 2)
            slopes = slopes.reshape(many, 3, hs, 2 * ls)
            modulus = mean_ref[here]
            spread = slope_x[:, 0] + slopes[:, 1, :, :ls] + slopes[:, 2, :, ls:]
            flux_x, flux_yz = [], []
            for c in range(3):
                parts = [slope_x[:, c], slopes[:, c, :, :ls], slopes[:, c, :, ls:]]
                parts[c] = parts[c] + spread
                flux_x.append(modulus * parts[0])
                flux_yz.append(jnp.concatenate([modulus * parts[1], modulus * parts[2]], axis=-1))
            flux_yz = jnp.stack(flux_yz, axis=1).reshape(many * 3 * hs, 2 * ls)
            back = picked(flux_yz, back_ref[...], 2).reshape(many, 3, hs, ls)
            for c in range(3):
                earlier = jnp.concatenate([behind[c][None], flux_x[c][:-1]], axis=0)
                total = flux_x[c] - earlier - back[:, c]
                moved = keep * step[here, c] + gain * (residual_ref[here, c] + total)
                step[here, c] = moved
                update[here, c] = own[:, c] + moved
            return tuple(flux[-1] for flux in flux_x)

        zero = jnp.zeros((hs, ls), F32)
        lax.fori_loop(0, NX // many, slabs_of, (zero, zero, zero), unroll=4)
        rho_prev = rho_next


def middle_kernel(plan, image_ref, base_ref, live_ref, mean_ref, slope_ref, back_ref, unpack_ref, pack_ref, msg_ref, residual_ref, update_ref, wide, narrow, step):
    unpack_image(plan, image_ref, unpack_ref, wide, narrow)
    add_image(plan, base_ref, live_ref, narrow, residual_ref)
    smooth(plan, mean_ref, slope_ref, back_ref, residual_ref, update_ref, step)
    for x in range(NX):
        for c in range(3):
            narrow[x * plan.hs : (x + 1) * plan.hs, c * plan.ls : (c + 1) * plan.ls] = update_ref[x, c]
    pick_into(wide, narrow, pack_ref)
    store_message(plan, wide, msg_ref)


def flat_rows(plan, values, out_ref, first, a):
    for t in range(plan.nz // 4):
        parts = [value[:, t * 128 : (t + 1) * 128] for value in values]
        for i, piece in enumerate(swap_quarters(parts)):
            out_ref[4 * t + i, first : first + plan.sp, a * 128 : (a + 1) * 128] = piece[: plan.sp]


def end_kernel(plan, image_ref, base_ref, live_ref, mean_ref, slope_ref, back_ref, unpack_ref, before_ref, out_ref, wide, narrow, residual, update, step):
    unpack_image(plan, image_ref, unpack_ref, wide, narrow)
    add_image(plan, base_ref, live_ref, narrow, residual)
    smooth(plan, mean_ref, slope_ref, back_ref, residual, update, step)
    for a in range(PLANE // 128):
        for c in range(3):
            flat_rows(plan, [update[4 * a + b, c] + before_ref[4 * a + b, c] for b in range(4)], out_ref, c * plan.sp, a)
            flat_rows(plan, [residual[4 * a + b, c] for b in range(4)], out_ref, (3 + c) * plan.sp, a)


def per_device(displacement, load, mean_modulus, modes, owner):
    chaos, slab = lax.axis_size("chaos"), lax.axis_size("slab")
    slots_dev, slots_all = displacement.shape[0], owner.shape[0]
    plan = Plan(chaos, slab, slots_dev)
    n, sp, hs, ls, lanes = plan.n, plan.sp, plan.hs, plan.ls, plan.lanes
    count, low, raised, level = edge_tables()
    at_chaos, at_slab = lax.axis_index("chaos"), lax.axis_index("slab")

    slots = np.arange(slots_all)
    places = (slots // slots_dev) * (slab * sp) + slots % slots_dev
    wanted = np.concatenate([low, raised])
    nodes = jnp.sum(
        jnp.where(wanted[:, None] == owner[None, :], jnp.asarray(places, jnp.int32)[None, :], 0), axis=1
    ).astype(jnp.int32)
    live_all = owner < count
    live_own = lax.dynamic_slice_in_dim(live_all, at_chaos * slots_dev, slots_dev, 0)
    live_here = jnp.pad(live_own.astype(F32), (0, slab * sp - slots_dev))
    live_here = lax.dynamic_slice_in_dim(live_here, at_slab * sp, sp, 0)
    live_here = jnp.broadcast_to(jnp.pad(live_here, (0, hs - sp))[:, None], (hs, ls))

    pack = jnp.asarray(plan.pack_table(), BF16)
    unpack = jnp.asarray(plan.unpack_table(), BF16)
    mtab = jnp.asarray(plan.modulus_table(), BF16)
    slopes, backs = (jnp.asarray(values, BF16) for values in (plan.slope_table(), plan.slope_table().T))
    grads, divs = (jnp.asarray(values, BF16) for values in (plan.gradient_table(), plan.divergence_table()))
    place = jnp.stack([at_chaos, at_slab]).astype(jnp.int32)

    slots_pad = slab * sp

    def by_component(values):
        return jnp.pad(jnp.transpose(values, (1, 0, 2)), ((0, 0), (0, slots_pad - slots_dev), (0, 0)))

    def everyone(values):
        return lax.all_to_all(values, ("chaos", "slab"), 0, 0, tiled=True)

    def column(values):
        return lax.all_to_all(values, "slab", 0, 0, tiled=True)

    smem = pl.BlockSpec(memory_space=pltpu.SMEM)
    vmem = pl.BlockSpec(memory_space=pltpu.VMEM)
    hbm = pl.BlockSpec(memory_space=pltpu.HBM)

    def call(kernel, name, in_specs, out_shape, scratch_shapes, grant=16 if n <= 64 else 60):
        return pl.pallas_call(
            kernel,
            out_shape=out_shape,
            in_specs=in_specs,
            out_specs=jax.tree.map(lambda _: vmem, out_shape),
            scratch_shapes=scratch_shapes,
            compiler_params=pltpu.CompilerParams(vmem_limit_bytes=grant * MIB),
            name=name,
        )

    def array(*shape):
        return jax.ShapeDtypeStruct(shape, F32)

    message, image = array(n, plan.rows_in, lanes), array(n, plan.rows_out, plan.lanes_out)
    grid_field, grid_more = array(NX, 3, hs, ls), array(NX + 1, 3, hs, ls)
    wide = pltpu.VMEM((NX * hs, plan.nyb * lanes), F32)
    narrow = pltpu.VMEM((NX * hs, plan.image_width), F32)
    field_scratch, more_scratch = pltpu.VMEM(grid_field.shape, F32), pltpu.VMEM(grid_more.shape, F32)

    mean_row = mean_modulus.reshape(1, PLANE)
    msg = call(
        functools.partial(start_kernel, plan),
        "start",
        [smem, hbm, hbm, hbm, hbm],
        message,
        [
            narrow,
            wide,
            pltpu.VMEM((16, PLANE), F32),
            pltpu.VMEM((3, slots_pad, PLANE), F32),
            pltpu.VMEM((PLANE // 128, 128), F32),
            pltpu.VMEM((KL, PLANE), F32),
            pltpu.VMEM(pack.shape, BF16),
            pltpu.SemaphoreType.DMA((4,)),
        ],
        60,
    )(place, by_component(displacement), mean_modulus.reshape(PLANE // 128, 128), modes, pack)
    levels = jnp.asarray(level, jnp.int32)
    mix_scratch = [
        pltpu.VMEM((plan.positions, 3, 8, lanes), F32),
        pltpu.VMEM((plan.positions, 3, 8, lanes), F32),
        pltpu.VMEM((DEG * KL, 8, lanes), F32),
    ]

    arrived = everyone(msg)
    flat, parts = array(plan.rows_flat, PLANE), array(3, slots_pad, PLANE)
    load_flat = call(
        functools.partial(split_kernel, plan), "split", [smem, vmem, vmem], (flat,) * slab, [pltpu.VMEM((slab, plan.rows_flat, PLANE), F32)]
    )(place, by_component(load), mean_row)
    load_flat = [load_flat[0]] + [
        lax.ppermute(load_flat[step], "slab", [(z, (z + step) % slab) for z in range(slab)])
        for step in range(1, slab)
    ]
    arrived, nodes = lax.optimization_barrier((arrived, nodes))
    first_image, mods = call(
        functools.partial(first_mix_kernel, plan, len(low), 3),
        "mix",
        [smem, smem, smem, vmem, vmem, vmem, vmem],
        (image, array(FIELDS, 8, lanes)),
        mix_scratch + [pltpu.VMEM((n, plan.rows_in, lanes), F32)],
    )(place, nodes, levels, arrived.reshape(n * plan.rows_in, lanes), mtab, grads, divs)
    load_flat, first_image = lax.optimization_barrier((load_flat, first_image))
    load_s, mean_s = call(
        functools.partial(load_kernel, plan),
        "load",
        [smem] + [vmem] * slab,
        (grid_field, array(NX, hs, ls)),
        [pltpu.VMEM((slab, plan.rows_flat, PLANE), F32)],
    )(place, *load_flat)
    msg, residual_s, update_s = call(
        functools.partial(middle_kernel, plan),
        "middle",
        [vmem] * 8,
        (message, grid_field, grid_more),
        [wide, narrow, field_scratch],
    )(everyone(first_image), load_s, live_here, mean_s, slopes, backs, unpack, pack)

    second_image = call(
        functools.partial(mix_kernel, plan, len(low), 2), "mix", [smem, smem, vmem, vmem, vmem, vmem], image, mix_scratch
    )(nodes, levels, everyone(msg), mods, grads, divs)
    ending = call(
        functools.partial(end_kernel, plan),
        "end",
        [vmem] * 8,
        array(slab, plan.rows_end, PLANE),
        [wide, narrow, field_scratch, more_scratch, field_scratch],
    )(everyone(second_image), residual_s, live_here, mean_s, slopes, backs, unpack, update_s)
    live_pad = jnp.pad(live_own.astype(F32), (0, slots_pad - slots_dev))
    outs = call(functools.partial(finish_kernel, plan), "finish", [vmem] * 3, (parts, parts), [])(
        column(ending), live_pad[:, None], by_component(displacement)
    )
    return tuple(jnp.transpose(values, (1, 0, 2))[:slots_dev] for values in outs)


def solution(mesh):
    in_specs = (P("chaos", None, "slab"), P("chaos", None, "slab"), P("slab"), P(None, "slab"), P())
    out_specs = (P("chaos", None, "slab"), P("chaos", None, "slab"))
    return jax.shard_map(
        per_device, mesh=mesh, in_specs=in_specs, out_specs=out_specs, check_vma=False
    )
```

```python
import functools
import math

import jax
import jax.numpy as jnp
import numpy as np
from jax import lax
from jax.experimental import pallas as pl
from jax.experimental.pallas import tpu as pltpu
from jax.sharding import PartitionSpec as P

NX = 24
NY = 32
KL = 10
DEG = 3
SWEEPS = 4
PLANE = NX * NY
FIELDS = KL + 1

bound_high = 50.0
bound_low = 2.5
MIB = 1024 * 1024
F32 = jnp.float32
BF16 = jnp.bfloat16


def up8(count):
    return -(-count // 8) * 8


def multi_indices():
    listing = [[]]
    for variable in range(KL):
        extended_list = []
        for prefix in listing:
            for degree in range(DEG + 1 - sum(prefix)):
                extended_list.append(prefix + [degree])
        listing = extended_list
    return listing


def edge_tables():
    listing = multi_indices()
    lookup = {tuple(entry): number for number, entry in enumerate(listing)}
    low, raised, level = [], [], []
    for number, entry in enumerate(listing):
        if sum(entry) == DEG:
            continue
        low.append(number)
        for variable in range(KL):
            other = list(entry)
            other[variable] += 1
            raised.append(lookup[tuple(other)])
            level.append(entry[variable])
    return len(listing), np.array(low, np.int32), np.array(raised, np.int32), np.array(level, np.int32)


class Plan:
    def __init__(self, chaos, slab, slots_dev):
        self.chaos, self.slab, self.slots_dev = chaos, slab, slots_dev
        self.n = chaos * slab
        self.nz = slab
        self.sp = -(-slots_dev // slab)
        self.hs = up8(self.sp)
        self.ls = self.nz * NY
        best = None
        for tx in range(1, 7):
            for ty in range(1, NY + 1):
                if NX % tx or NY % ty or (NX // tx) * (NY // ty) > self.n:
                    continue
                lanes = -(-3 * self.nz * (ty + 2) // 128) * 128
                rows = up8((self.sp - 1) * (tx + 2) + 8)
                key = (-(NX // tx) * (NY // ty), rows * lanes)
                if best is None or key < best[0]:
                    best = (key, tx, ty, lanes, rows)
        _, self.tx, self.ty, self.lanes, self.rows_in = best
        self.rx = self.tx + 2
        self.ry = self.ty + 2
        self.nxb, self.nyb = NX // self.tx, NY // self.ty
        self.lanes_out = -(-3 * self.nz * self.ty // 128) * 128
        self.segment = self.nz * self.ty
        self.moved = self.sp // 4 if self.lanes_out >= 4 * self.segment else 0
        self.kept = self.sp - self.moved
        self.rows_out = up8(self.kept * self.tx)
        self.image_width = (4 if self.moved else 3) * self.ls
        self.rows_flat = up8(3 * self.sp + 1)
        self.rows_end = up8(6 * self.sp)
        self.shares = -(-FIELDS // min(chaos, 16))
        self.per_share = 16 // self.shares
        self.positions = self.n * self.sp

    def pack_table(self):
        table = np.zeros((3 * self.ls, self.nyb * self.lanes), np.float32)
        for c in range(3):
            for z in range(self.nz):
                for yb in range(self.nyb):
                    for k in range(self.ry):
                        y = yb * self.ty - 1 + k
                        if 0 <= y < NY:
                            table[
                                c * self.ls + z * NY + y,
                                yb * self.lanes + (c * self.nz + z) * self.ry + k,
                            ] = 1
        return table

    def unpack_table(self):
        table = np.zeros((self.nyb * self.lanes_out, self.image_width), np.float32)
        for c in range(self.image_width // self.ls):
            for z in range(self.nz):
                for y in range(NY):
                    yb, k = divmod(y, self.ty)
                    table[
                        yb * self.lanes_out + (c * self.nz + z) * self.ty + k, c * self.ls + z * NY + y
                    ] = 1
        return table

    def tile_lane(self, c, z, y):
        return (c * self.nz + z) * self.ry + y

    def gradient_table(self):
        table = np.zeros((2 * self.lanes, 3 * self.lanes), np.float32)
        at, wide = self.tile_lane, self.lanes

        def add(column, c, d, z, y, sign=1):
            if d == 0:
                table[wide + at(c, z, y), column] += 1
                return
            table[at(c, z, y), column] -= 1
            if d == 1 and y + 1 < self.ry:
                table[at(c, z, y + 1), column] += 1
            if d == 2 and z + 1 < self.nz:
                table[at(c, z + 1, y), column] += 1

        for z in range(self.nz):
            for y in range(self.ry):
                for c in range(3):
                    for d in range(3):
                        add(d * wide + at(c, z, y), c, d, z, y)
                        add(c * wide + at(c, z, y), d, d, z, y)
        return table

    def divergence_table(self):
        table = np.zeros((3 * self.lanes, self.lanes_out), np.float32)
        at, wide = self.tile_lane, self.lanes
        for c in range(3):
            for z in range(self.nz):
                for y in range(self.ty):
                    column = (c * self.nz + z) * self.ty + y
                    table[at(c, z, y + 1), column] = 1
                    table[wide + at(c, z, y + 1), column] = 1
                    table[wide + at(c, z, y), column] = -1
                    table[2 * wide + at(c, z, y + 1), column] = 1
                    if z:
                        table[2 * wide + at(c, z - 1, y + 1), column] = -1
        return table

    def slope_table(self):
        table = np.zeros((self.ls, 2 * self.ls), np.float32)
        for z in range(self.nz):
            for y in range(NY):
                j = z * NY + y
                table[j, j] = table[j, self.ls + j] = -1
                if y + 1 < NY:
                    table[j + 1, j] = 1
                if z + 1 < self.nz:
                    table[j + NY, self.ls + j] = 1
        return table

    def modulus_table(self):
        table = np.zeros((self.nyb, self.ls, self.lanes), np.float32)
        for yb in range(self.nyb):
            for z in range(self.nz):
                for k in range(self.ry):
                    y = yb * self.ty - 1 + k
                    if 0 <= y < NY:
                        for c in range(3):
                            table[yb, z * NY + y, (c * self.nz + z) * self.ry + k] = 1
        return table


def picked(values, table, parts=3):
    total, rest = None, values
    for part in range(parts):
        head = rest.astype(BF16)
        product = jnp.dot(head, table, preferred_element_type=F32)
        total = product if total is None else total + product
        if part + 1 < parts:
            rest = rest - head.astype(F32)
    return total


def pick_into(out_ref, values_ref, table_ref):
    width = table_ref.shape[1]
    chunk = width if width <= 1024 else 512
    for first in range(0, width, chunk):
        out_ref[:, first : first + chunk] = picked(
            values_ref[:, : table_ref.shape[0]], table_ref[:, first : first + chunk]
        )


def swap_quarters(parts):
    quarter = lax.broadcasted_iota(jnp.int32, parts[0].shape, 1) // NY
    swapped = []
    for j in range(4):
        total = parts[j]
        for i in range(4):
            if i != j:
                turned = pltpu.roll(parts[i], (i - j) % 4 * NY, 1)
                total = jnp.where(quarter == i, turned, total)
        swapped.append(total)
    return swapped


def strided(start, size, step):
    return pl.ds(start, size) if size == 1 or step == 1 else pl.ds(start, size, stride=step)


def store_moduli(plan, chaos_at, moduli_ref, msg_ref):
    quarter = lax.broadcasted_iota(jnp.int32, (1, 128), 1) // NY
    own = [moduli_ref[pl.ds(share * plan.per_share + chaos_at, 1), :] for share in range(plan.shares)]
    count, first = plan.shares * plan.rx, plan.sp * plan.rx
    for xb in range(plan.nxb):
        for start in range(0, count, 4):
            line = jnp.zeros((1, 128), F32)
            for number in range(start, min(count, start + 4)):
                share, k = divmod(number, plan.rx)
                x = xb * plan.tx - 1 + k
                if 0 <= x < NX:
                    piece = own[share][:, x // 4 * 128 : (x // 4 + 1) * 128]
                    turned = pltpu.roll(piece, (number - x) % 4 * NY, 1)
                    line = jnp.where(quarter == number % 4, turned, line)
            row, column = divmod(start // 4, plan.lanes // 128)
            for yb in range(plan.nyb):
                tile = xb * plan.nyb + yb
                msg_ref[tile, first + row : first + row + 1, column * 128 : (column + 1) * 128] = line


def gather_moduli(plan, tile_at, msg_ref, mtab_ref, mods_ref):
    quarter = lax.broadcasted_iota(jnp.int32, (plan.per_share, 128), 1) // NY
    first, rows = plan.sp * plan.rx, plan.rows_in
    table = mtab_ref[lax.rem(tile_at, plan.nyb)]
    mods_ref[...] = jnp.zeros(mods_ref.shape, F32)
    for share in range(plan.shares):
        lines = []
        for k in range(plan.rx):
            number = share * plan.rx + k
            row, column = divmod(number // 4, plan.lanes // 128)
            parts = []
            for t in range(plan.nz // 4):
                total = jnp.zeros((plan.per_share, 128), F32)
                for i in range(4):
                    at, columns = (4 * t + i) * rows + first + row, slice(column * 128, (column + 1) * 128)
                    if plan.lanes == 128:
                        piece = msg_ref[pl.ds(at, plan.per_share, stride=plan.slab * rows), columns]
                    else:
                        lone = [at + j * plan.slab * rows for j in range(plan.per_share)]
                        piece = jnp.concatenate([msg_ref[j : j + 1, columns] for j in lone], axis=0)
                    total = jnp.where(quarter == i, pltpu.roll(piece, (i - number) % 4 * NY, 1), total)
                parts.append(total)
            lines.append(parts[0] if len(parts) == 1 else jnp.concatenate(parts, axis=1))
        here = picked(jnp.concatenate(lines, axis=0), table)
        for k in range(plan.rx):
            for v in range(min(plan.per_share, FIELDS - share * plan.per_share)):
                at = k * plan.per_share + v
                mods_ref[share * plan.per_share + v, k : k + 1, :] = here[at : at + 1]


def store_message(plan, rows_ref, msg_ref):
    blank = jnp.zeros((8, plan.lanes), F32)
    for tile in range(plan.n):
        if tile >= plan.nxb * plan.nyb:
            msg_ref[tile] = jnp.zeros((plan.rows_in, plan.lanes), F32)
            continue
        xb, yb = divmod(tile, plan.nyb)
        msg_ref[tile, plan.rows_in - 8 :, :] = blank
        for k in range(plan.rx):
            x = xb * plan.tx - 1 + k
            if 0 <= x < NX:
                rows = rows_ref[
                    x * plan.hs : x * plan.hs + plan.sp, yb * plan.lanes : (yb + 1) * plan.lanes
                ]
            else:
                rows = jnp.zeros((plan.sp, plan.lanes), F32)
            msg_ref[tile, strided(k, plan.sp, plan.rx), :] = rows


def rows_at(piece_of):
    return [jnp.concatenate(pieces, axis=1) if len(pieces) > 1 else pieces[0] for pieces in zip(*piece_of)]


def start_kernel(plan, in_hbm, mean_hbm, modes_hbm, pack_hbm, msg_ref, lhs, rows, moduli, in_ref, mean_ref, modes_ref, pack_ref, arrived):
    pairs = ((in_hbm, in_ref), (pack_hbm, pack_ref), (mean_hbm, mean_ref), (modes_hbm, modes_ref))
    copies = [pltpu.make_async_copy(source, target, arrived.at[i]) for i, (source, target) in enumerate(pairs)]
    for copy in copies:
        copy.start()
    copies[0].wait()
    for a in range(PLANE // 128):
        for c in range(3):
            pieces = rows_at(
                swap_quarters(
                    [
                        in_ref[c, (4 * t + i) * plan.sp : (4 * t + i + 1) * plan.sp, a * 128 : (a + 1) * 128]
                        for i in range(4)
                    ]
                )
                for t in range(plan.slab // 4)
            )
            for b, piece in enumerate(pieces):
                x = 4 * a + b
                lhs[x * plan.hs : x * plan.hs + plan.sp, c * plan.ls : (c + 1) * plan.ls] = piece
    copies[1].wait()
    pick_into(rows, lhs, pack_ref)
    store_message(plan, rows, msg_ref)
    copies[2].wait()
    copies[3].wait()
    moduli[...] = jnp.zeros(moduli.shape, F32)
    for a in range(PLANE // 128):
        moduli[0:1, a * 128 : (a + 1) * 128] = mean_ref[a : a + 1, :]
    moduli[1:FIELDS] = modes_ref[...]
    store_moduli(plan, jnp.minimum(lax.axis_index("chaos"), plan.per_share - 1), moduli, msg_ref)


def split_kernel(plan, in_ref, mean_ref, *refs):
    out_refs, groups = refs[: plan.slab], refs[plan.slab]
    for group in range(plan.slab):
        step = lax.rem(group + plan.slab - lax.axis_index("slab"), plan.slab)
        for c in range(3):
            groups[step, c * plan.sp : (c + 1) * plan.sp, :] = in_ref[c, group * plan.sp : (group + 1) * plan.sp, :]
        groups[step, 3 * plan.sp : 3 * plan.sp + 1, :] = mean_ref[...]
    for step, out_ref in enumerate(out_refs):
        out_ref[...] = groups[step]


def load_kernel(plan, *refs):
    in_refs, (out_ref, mean_ref, planes) = refs[: plan.slab], refs[plan.slab :]
    for step, in_ref in enumerate(in_refs):
        planes[lax.rem(lax.axis_index("slab") + (plan.slab - step), plan.slab)] = in_ref[...]
    for a in range(PLANE // 128):
        lanes = slice(a * 128, (a + 1) * 128)
        pieces = rows_at(
            swap_quarters([planes[4 * t + i, 3 * plan.sp : 3 * plan.sp + 1, lanes] for i in range(4)])
            for t in range(plan.nz // 4)
        )
        for b, piece in enumerate(pieces):
            mean_ref[4 * a + b] = jnp.broadcast_to(piece, (plan.hs, plan.ls))
        for c in range(3):
            pieces = rows_at(
                swap_quarters([planes[4 * t + i, c * plan.sp : (c + 1) * plan.sp, lanes] for i in range(4)])
                for t in range(plan.nz // 4)
            )
            for b, piece in enumerate(pieces):
                out_ref[4 * a + b, c, 0 : plan.sp, :] = piece


def finish_kernel(plan, live_ref, start_ref, *refs):
    piece_refs, (total_ref, residual_ref, groups) = refs[: plan.slab], refs[plan.slab :]
    for step, piece_ref in enumerate(piece_refs):
        groups[lax.rem(lax.axis_index("slab") + (plan.slab - step), plan.slab)] = piece_ref[...]
    for group in range(plan.slab):
        here = slice(group * plan.sp, (group + 1) * plan.sp)
        live = jnp.broadcast_to(live_ref[here, :], (plan.sp, PLANE)) != 0.0
        for c in range(3):
            total_ref[c, here, :] = jnp.where(live, start_ref[c, here, :], 0.0) + groups[
                group, c * plan.sp : (c + 1) * plan.sp, :
            ]
            residual_ref[c, here, :] = groups[group, (3 + c) * plan.sp : (4 + c) * plan.sp, :]


def regrouped(plan, msg_ref, out_ref):
    lane = lax.broadcasted_iota(jnp.int32, (plan.rows_in, plan.lanes), 1)
    height = lane % (plan.nz * plan.ry) // plan.ry

    def one(row, carry):
        parts = [
            msg_ref[pl.ds(pl.multiple_of((row * plan.slab + z) * plan.rows_in, 8), plan.rows_in), :] for z in range(plan.nz)
        ]
        for group in range(plan.slab):
            total = parts[group]
            for z in range(plan.nz):
                if z != group:
                    turned = pltpu.roll(parts[z], (z - group) * plan.ry % plan.lanes, 1)
                    total = jnp.where(height == z, turned, total)
            out_ref[row * plan.slab + group] = total
        return carry

    lax.fori_loop(0, plan.chaos, one, 0, unroll=4)


def first_mix_kernel(plan, low_count, parts, nodes_ref, level_ref, msg_ref, mtab_ref, grad_ref, div_ref, out_ref, mods_ref, grad, flux, scaled, regroup):
    gather_moduli(plan, lax.axis_index("chaos") * plan.slab + lax.axis_index("slab"), msg_ref, mtab_ref, mods_ref)
    regrouped(plan, msg_ref, regroup)
    mix_kernel(plan, low_count, parts, nodes_ref, level_ref, regroup, mods_ref, grad_ref, div_ref, out_ref, grad, flux, scaled)


def mix_kernel(plan, low_count, parts, nodes_ref, level_ref, msg_ref, mods_ref, grad_ref, div_ref, out_ref, grad, flux, scaled):
    sp, rx, tx, lanes = plan.sp, plan.rx, plan.tx, plan.lanes
    for level in range(DEG):
        for v in range(KL):
            scaled[level * KL + v] = mods_ref[v + 1] * math.sqrt(level + 1)
    mean = mods_ref[0]

    def gradients(chunk, carry):
        windows, behind = [], []
        for i in range(4):
            source = chunk * 4 + i
            for s in range(sp):
                windows.append(msg_ref[source, s * rx : s * rx + 8, :])
                if s * rx + 9 <= plan.rows_in:
                    behind.append(msg_ref[source, s * rx + 1 : s * rx + 9, :])
                else:
                    behind.append(pltpu.roll(windows[-1], 7, 0))
        own = jnp.concatenate(windows, axis=0)
        slope_x = jnp.concatenate(behind, axis=0) - own
        full = picked(jnp.concatenate([own, slope_x], axis=1), grad_ref[...], parts)
        here = pl.ds(chunk * 4 * sp, 4 * sp)
        for d in range(3):
            part = full[:, d * lanes : (d + 1) * lanes].reshape(4 * sp, 8, lanes)
            grad[here, d] = part
            flux[here, d] = mean * part
        return carry

    lax.fori_loop(0, plan.n // 4, gradients, 0, unroll=8)

    def edges(number, carry):
        base = nodes_ref[number]
        own = [grad[base, d] for d in range(3)]
        total = [flux[base, d] for d in range(3)]
        for group in range(0, KL, 5):
            at = [nodes_ref[low_count + number * KL + v] for v in range(group, group + 5)]
            field = [scaled[level_ref[number * KL + v] * KL + v] for v in range(group, group + 5)]
            fresh = [
                [flux[spot, d] + weight * own[d] for d in range(3)] for spot, weight in zip(at, field)
            ]
            for spot, weight in zip(at, field):
                total = [total[d] + weight * grad[spot, d] for d in range(3)]
            for spot, values in zip(at, fresh):
                for d in range(3):
                    flux[spot, d] = values[d]
        for d in range(3):
            flux[base, d] = total[d]
        return carry

    lax.fori_loop(0, low_count, edges, 0, unroll=2)

    def divergences(chunk, carry):
        here = pl.ds(chunk * 4 * sp, 4 * sp)
        flux_x, flux_y, flux_z = (flux[here, d] for d in range(3))
        flux_x = flux_x - pltpu.roll(flux_x, 1, 1)
        values = jnp.concatenate([flux_x, flux_y, flux_z], axis=2).reshape(4 * sp * 8, 3 * lanes)
        total = picked(values, div_ref[...], parts).reshape(4, sp, 8, plan.lanes_out)
        for i in range(4):
            for s in range(plan.kept):
                out_ref[chunk * 4 + i, s * tx : (s + 1) * tx, :] = total[i, s, 1 : 1 + tx]
            for number in range(3 * plan.moved):
                slot, c = plan.kept + number // 3, number % 3
                turned = pltpu.roll(total[i, slot], (3 - c) * plan.segment, 1)
                out_ref[chunk * 4 + i, number * tx : (number + 1) * tx, 3 * plan.segment : 4 * plan.segment] = turned[
                    1 : 1 + tx, 3 * plan.segment : 4 * plan.segment
                ]
        return carry

    lax.fori_loop(0, plan.n // 4, divergences, 0, unroll=8)


def unpack_image(plan, image_ref, unpack_ref, lhs, rows):
    for xb in range(plan.nxb):
        for k in range(plan.tx):
            x = xb * plan.tx + k
            for yb in range(plan.nyb):
                lhs[x * plan.hs : x * plan.hs + plan.kept, yb * plan.lanes_out : (yb + 1) * plan.lanes_out] = image_ref[
                    xb * plan.nyb + yb, strided(k, plan.kept, plan.tx), :
                ]
    pick_into(rows, lhs, unpack_ref)


def add_image(plan, base_ref, live_ref, rows, residual_ref):
    live = live_ref[...] != 0.0
    slot = lax.broadcasted_iota(jnp.int32, (plan.hs, plan.ls), 0)

    def one(x, carry):
        block = rows.at[pl.ds(pl.multiple_of(x * plan.hs, plan.hs), plan.hs)]
        for c in range(3):
            image = block[:, c * plan.ls : (c + 1) * plan.ls]
            for q in range(plan.moved):
                line = block[3 * q + c : 3 * q + c + 1, 3 * plan.ls : 4 * plan.ls]
                image = jnp.where(slot == plan.kept + q, line, image)
            residual_ref[x, c] = jnp.where(live, base_ref[x, c] + image, 0.0)
        return carry

    lax.fori_loop(0, NX, one, 0, unroll=6)


def smooth(plan, mean_ref, slope_ref, back_ref, residual_ref, update, step):
    hs, ls, many = plan.hs, plan.ls, 6
    center_value = 0.5 * (bound_high + bound_low)
    half_width = 0.5 * (bound_high - bound_low)
    ratio_value = center_value / half_width

    def first(x, carry):
        for c in range(3):
            scaled = residual_ref[x, c] * (1.0 / center_value)
            update[x, c] = scaled
            step[x, c] = scaled
        return carry

    lax.fori_loop(0, NX, first, 0, unroll=6)
    update[NX] = jnp.zeros((3, hs, ls), F32)

    rho_prev = 1.0 / ratio_value
    for sweep in range(SWEEPS):
        rho_next = 1.0 / (2.0 * ratio_value - rho_prev)
        keep, gain = rho_next * rho_prev, 2.0 * rho_next / half_width

        def slabs_of(chunk, behind, keep=keep, gain=gain):
            here = pl.ds(chunk * many, many)
            own = update[here]
            slope_x = update[pl.ds(chunk * many + 1, many)] - own
            slopes = picked(own.reshape(many * 3 * hs, ls), slope_ref[...], 2)
            slopes = slopes.reshape(many, 3, hs, 2 * ls)
            modulus = mean_ref[here]
            spread = slope_x[:, 0] + slopes[:, 1, :, :ls] + slopes[:, 2, :, ls:]
            flux_x, flux_yz = [], []
            for c in range(3):
                parts = [slope_x[:, c], slopes[:, c, :, :ls], slopes[:, c, :, ls:]]
                parts[c] = parts[c] + spread
                flux_x.append(modulus * parts[0])
                flux_yz.append(jnp.concatenate([modulus * parts[1], modulus * parts[2]], axis=-1))
            flux_yz = jnp.stack(flux_yz, axis=1).reshape(many * 3 * hs, 2 * ls)
            back = picked(flux_yz, back_ref[...], 2).reshape(many, 3, hs, ls)
            for c in range(3):
                earlier = jnp.concatenate([behind[c][None], flux_x[c][:-1]], axis=0)
                total = flux_x[c] - earlier - back[:, c]
                moved = keep * step[here, c] + gain * (residual_ref[here, c] + total)
                step[here, c] = moved
                update[here, c] = own[:, c] + moved
            return tuple(flux[-1] for flux in flux_x)

        zero = jnp.zeros((hs, ls), F32)
        lax.fori_loop(0, NX // many, slabs_of, (zero, zero, zero), unroll=4)
        rho_prev = rho_next


def middle_kernel(plan, image_ref, base_ref, live_ref, mean_ref, slope_ref, back_ref, unpack_ref, pack_ref, msg_ref, residual_ref, update_ref, wide, narrow, step):
    unpack_image(plan, image_ref, unpack_ref, wide, narrow)
    add_image(plan, base_ref, live_ref, narrow, residual_ref)
    smooth(plan, mean_ref, slope_ref, back_ref, residual_ref, update_ref, step)
    for x in range(NX):
        for c in range(3):
            narrow[x * plan.hs : (x + 1) * plan.hs, c * plan.ls : (c + 1) * plan.ls] = update_ref[x, c]
    pick_into(wide, narrow, pack_ref)
    store_message(plan, wide, msg_ref)


def flat_rows(plan, values, out_ref, first, a):
    for t in range(plan.nz // 4):
        parts = [value[:, t * 128 : (t + 1) * 128] for value in values]
        for i, piece in enumerate(swap_quarters(parts)):
            out_ref[4 * t + i, first : first + plan.sp, a * 128 : (a + 1) * 128] = piece[: plan.sp]


def end_kernel(plan, image_ref, base_ref, live_ref, mean_ref, slope_ref, back_ref, unpack_ref, before_ref, *refs):
    out_refs, (wide, narrow, residual, update, step, planes) = refs[: plan.slab], refs[plan.slab :]
    unpack_image(plan, image_ref, unpack_ref, wide, narrow)
    add_image(plan, base_ref, live_ref, narrow, residual)
    smooth(plan, mean_ref, slope_ref, back_ref, residual, update, step)
    for a in range(PLANE // 128):
        for c in range(3):
            flat_rows(plan, [update[4 * a + b, c] + before_ref[4 * a + b, c] for b in range(4)], planes, c * plan.sp, a)
            flat_rows(plan, [residual[4 * a + b, c] for b in range(4)], planes, (3 + c) * plan.sp, a)
    for number, out_ref in enumerate(out_refs):
        out_ref[...] = planes[lax.rem(lax.axis_index("slab") + number, plan.slab)]


def per_device(displacement, load, mean_modulus, modes, owner):
    chaos, slab = lax.axis_size("chaos"), lax.axis_size("slab")
    slots_dev, slots_all = displacement.shape[0], owner.shape[0]
    plan = Plan(chaos, slab, slots_dev)
    n, sp, hs, ls, lanes = plan.n, plan.sp, plan.hs, plan.ls, plan.lanes
    count, low, raised, level = edge_tables()
    at_chaos, at_slab = lax.axis_index("chaos"), lax.axis_index("slab")

    slots = np.arange(slots_all)
    places = (slots // slots_dev) * (slab * sp) + slots % slots_dev
    wanted = np.concatenate([low, raised])
    nodes = jnp.sum(
        jnp.where(wanted[:, None] == owner[None, :], jnp.asarray(places, jnp.int32)[None, :], 0), axis=1
    ).astype(jnp.int32)
    live_all = owner < count
    live_own = lax.dynamic_slice_in_dim(live_all, at_chaos * slots_dev, slots_dev, 0)
    live_here = jnp.pad(live_own.astype(F32), (0, slab * sp - slots_dev))
    live_here = lax.dynamic_slice_in_dim(live_here, at_slab * sp, sp, 0)
    live_here = jnp.broadcast_to(jnp.pad(live_here, (0, hs - sp))[:, None], (hs, ls))

    pack = jnp.asarray(plan.pack_table(), BF16)
    unpack = jnp.asarray(plan.unpack_table(), BF16)
    mtab = jnp.asarray(plan.modulus_table(), BF16)
    slopes, backs = (jnp.asarray(values, BF16) for values in (plan.slope_table(), plan.slope_table().T))
    grads, divs = (jnp.asarray(values, BF16) for values in (plan.gradient_table(), plan.divergence_table()))

    slots_pad = slab * sp

    def by_component(values):
        return jnp.pad(jnp.transpose(values, (1, 0, 2)), ((0, 0), (0, slots_pad - slots_dev), (0, 0)))

    def everyone(values):
        return lax.all_to_all(values, ("chaos", "slab"), 0, 0, tiled=True)

    def column(pieces):
        return [pieces[0]] + [
            lax.ppermute(pieces[step], "slab", [(z, (z + step) % slab) for z in range(slab)])
            for step in range(1, slab)
        ]

    smem = pl.BlockSpec(memory_space=pltpu.SMEM)
    vmem = pl.BlockSpec(memory_space=pltpu.VMEM)
    hbm = pl.BlockSpec(memory_space=pltpu.HBM)

    def call(kernel, name, in_specs, out_shape, scratch_shapes, grant=16 if n <= 64 else 60):
        return pl.pallas_call(
            kernel,
            out_shape=out_shape,
            in_specs=in_specs,
            out_specs=jax.tree.map(lambda _: vmem, out_shape),
            scratch_shapes=scratch_shapes,
            compiler_params=pltpu.CompilerParams(vmem_limit_bytes=grant * MIB),
            name=name,
        )

    def array(*shape):
        return jax.ShapeDtypeStruct(shape, F32)

    message, image = array(n, plan.rows_in, lanes), array(n, plan.rows_out, plan.lanes_out)
    grid_field, grid_more = array(NX, 3, hs, ls), array(NX + 1, 3, hs, ls)
    wide = pltpu.VMEM((NX * hs, plan.nyb * lanes), F32)
    narrow = pltpu.VMEM((NX * hs, plan.image_width), F32)
    field_scratch, more_scratch = pltpu.VMEM(grid_field.shape, F32), pltpu.VMEM(grid_more.shape, F32)

    mean_row = mean_modulus.reshape(1, PLANE)
    msg = call(
        functools.partial(start_kernel, plan),
        "start",
        [hbm, hbm, hbm, hbm],
        message,
        [
            narrow,
            wide,
            pltpu.VMEM((16, PLANE), F32),
            pltpu.VMEM((3, slots_pad, PLANE), F32),
            pltpu.VMEM((PLANE // 128, 128), F32),
            pltpu.VMEM((KL, PLANE), F32),
            pltpu.VMEM(pack.shape, BF16),
            pltpu.SemaphoreType.DMA((4,)),
        ],
        60,
    )(by_component(displacement), mean_modulus.reshape(PLANE // 128, 128), modes, pack)
    levels = jnp.asarray(level, jnp.int32)
    mix_scratch = [
        pltpu.VMEM((plan.positions, 3, 8, lanes), F32),
        pltpu.VMEM((plan.positions, 3, 8, lanes), F32),
        pltpu.VMEM((DEG * KL, 8, lanes), F32),
    ]

    arrived = everyone(msg)
    flat, parts = array(plan.rows_flat, PLANE), array(3, slots_pad, PLANE)
    load_flat = call(
        functools.partial(split_kernel, plan), "split", [vmem, vmem], (flat,) * slab, [pltpu.VMEM((slab, plan.rows_flat, PLANE), F32)]
    )(by_component(load), mean_row)
    load_flat = column(load_flat)
    arrived, nodes = lax.optimization_barrier((arrived, nodes))
    first_image, mods = call(
        functools.partial(first_mix_kernel, plan, len(low), 3),
        "mix",
        [smem, smem, vmem, vmem, vmem, vmem],
        (image, array(FIELDS, 8, lanes)),
        mix_scratch + [pltpu.VMEM((n, plan.rows_in, lanes), F32)],
    )(nodes, levels, arrived.reshape(n * plan.rows_in, lanes), mtab, grads, divs)
    load_flat, first_image = lax.optimization_barrier((load_flat, first_image))
    load_s, mean_s = call(
        functools.partial(load_kernel, plan),
        "load",
        [vmem] * slab,
        (grid_field, array(NX, hs, ls)),
        [pltpu.VMEM((slab, plan.rows_flat, PLANE), F32)],
    )(*load_flat)
    msg, residual_s, update_s = call(
        functools.partial(middle_kernel, plan),
        "middle",
        [vmem] * 8,
        (message, grid_field, grid_more),
        [wide, narrow, field_scratch],
    )(everyone(first_image), load_s, live_here, mean_s, slopes, backs, unpack, pack)

    second_image = call(
        functools.partial(mix_kernel, plan, len(low), 2), "mix", [smem, smem, vmem, vmem, vmem, vmem], image, mix_scratch
    )(nodes, levels, everyone(msg), mods, grads, divs)
    around = pltpu.VMEM((slab, plan.rows_end, PLANE), F32)
    ending = call(
        functools.partial(end_kernel, plan),
        "end",
        [vmem] * 8,
        (array(plan.rows_end, PLANE),) * slab,
        [wide, narrow, field_scratch, more_scratch, field_scratch, around],
    )(everyone(second_image), residual_s, live_here, mean_s, slopes, backs, unpack, update_s)
    live_pad = jnp.pad(live_own.astype(F32), (0, slots_pad - slots_dev))
    outs = call(functools.partial(finish_kernel, plan), "finish", [vmem] * (2 + slab), (parts, parts), [around])(
        live_pad[:, None], by_component(displacement), *column(ending)
    )
    return tuple(jnp.transpose(values, (1, 0, 2))[:slots_dev] for values in outs)


def solution(mesh):
    in_specs = (P("chaos", None, "slab"), P("chaos", None, "slab"), P("slab"), P(None, "slab"), P())
    out_specs = (P("chaos", None, "slab"), P("chaos", None, "slab"))
    return jax.shard_map(
        per_device, mesh=mesh, in_specs=in_specs, out_specs=out_specs, check_vma=False
    )
```

```python
import functools
import math

import jax
import jax.numpy as jnp
import numpy as np
from jax import lax
from jax.experimental import pallas as pl
from jax.experimental.pallas import tpu as pltpu
from jax.sharding import PartitionSpec as P

NX = 24
NY = 32
KL = 10
DEG = 3
SWEEPS = 4
PLANE = NX * NY
FIELDS = KL + 1

bound_high = 50.0
bound_low = 2.5
MIB = 1024 * 1024
F32 = jnp.float32
BF16 = jnp.bfloat16


def up8(count):
    return -(-count // 8) * 8


def multi_indices():
    listing = [[]]
    for variable in range(KL):
        extended_list = []
        for prefix in listing:
            for degree in range(DEG + 1 - sum(prefix)):
                extended_list.append(prefix + [degree])
        listing = extended_list
    return listing


def edge_tables():
    listing = multi_indices()
    lookup = {tuple(entry): number for number, entry in enumerate(listing)}
    low, raised, level = [], [], []
    for number, entry in enumerate(listing):
        if sum(entry) == DEG:
            continue
        low.append(number)
        for variable in range(KL):
            other = list(entry)
            other[variable] += 1
            raised.append(lookup[tuple(other)])
            level.append(entry[variable])
    return len(listing), np.array(low, np.int32), np.array(raised, np.int32), np.array(level, np.int32)


class Plan:
    def __init__(self, chaos, slab, slots_dev):
        self.chaos, self.slab, self.slots_dev = chaos, slab, slots_dev
        self.n = chaos * slab
        self.nz = slab
        self.sp = -(-slots_dev // slab)
        self.hs = up8(self.sp)
        self.ls = self.nz * NY
        best = None
        for tx in range(1, 7):
            for ty in range(1, NY + 1):
                if NX % tx or NY % ty or (NX // tx) * (NY // ty) > self.n:
                    continue
                lanes = -(-3 * self.nz * (ty + 2) // 128) * 128
                rows = up8((self.sp - 1) * (tx + 2) + 8)
                key = (-(NX // tx) * (NY // ty), rows * lanes)
                if best is None or key < best[0]:
                    best = (key, tx, ty, lanes, rows)
        _, self.tx, self.ty, self.lanes, self.rows_in = best
        self.rx = self.tx + 2
        self.ry = self.ty + 2
        self.nxb, self.nyb = NX // self.tx, NY // self.ty
        self.lanes_out = -(-3 * self.nz * self.ty // 128) * 128
        self.segment = self.nz * self.ty
        self.moved = self.sp // 4 if self.lanes_out >= 4 * self.segment else 0
        self.kept = self.sp - self.moved
        self.rows_out = up8(self.kept * self.tx)
        self.image_width = (4 if self.moved else 3) * self.ls
        self.rows_flat = up8(3 * self.sp + 1)
        self.rows_end = up8(6 * self.sp)
        self.shares = -(-FIELDS // min(chaos, 16))
        self.per_share = 16 // self.shares
        self.positions = self.n * self.sp

    def pack_table(self):
        table = np.zeros((3 * self.ls, self.nyb * self.lanes), np.float32)
        for c in range(3):
            for z in range(self.nz):
                for yb in range(self.nyb):
                    for k in range(self.ry):
                        y = yb * self.ty - 1 + k
                        if 0 <= y < NY:
                            table[
                                c * self.ls + z * NY + y,
                                yb * self.lanes + (c * self.nz + z) * self.ry + k,
                            ] = 1
        return table

    def unpack_table(self):
        table = np.zeros((self.nyb * self.lanes_out, self.image_width), np.float32)
        for c in range(self.image_width // self.ls):
            for z in range(self.nz):
                for y in range(NY):
                    yb, k = divmod(y, self.ty)
                    table[
                        yb * self.lanes_out + (c * self.nz + z) * self.ty + k, c * self.ls + z * NY + y
                    ] = 1
        return table

    def tile_lane(self, c, z, y):
        return (c * self.nz + z) * self.ry + y

    def gradient_table(self):
        table = np.zeros((2 * self.lanes, 3 * self.lanes), np.float32)
        at, wide = self.tile_lane, self.lanes

        def add(column, c, d, z, y, sign=1):
            if d == 0:
                table[wide + at(c, z, y), column] += 1
                return
            table[at(c, z, y), column] -= 1
            if d == 1 and y + 1 < self.ry:
                table[at(c, z, y + 1), column] += 1
            if d == 2 and z + 1 < self.nz:
                table[at(c, z + 1, y), column] += 1

        for z in range(self.nz):
            for y in range(self.ry):
                for c in range(3):
                    for d in range(3):
                        add(d * wide + at(c, z, y), c, d, z, y)
                        add(c * wide + at(c, z, y), d, d, z, y)
        return table

    def divergence_table(self):
        table = np.zeros((3 * self.lanes, self.lanes_out), np.float32)
        at, wide = self.tile_lane, self.lanes
        for c in range(3):
            for z in range(self.nz):
                for y in range(self.ty):
                    column = (c * self.nz + z) * self.ty + y
                    table[at(c, z, y + 1), column] = 1
                    table[wide + at(c, z, y + 1), column] = 1
                    table[wide + at(c, z, y), column] = -1
                    table[2 * wide + at(c, z, y + 1), column] = 1
                    if z:
                        table[2 * wide + at(c, z - 1, y + 1), column] = -1
        return table

    def slope_table(self):
        table = np.zeros((self.ls, 2 * self.ls), np.float32)
        for z in range(self.nz):
            for y in range(NY):
                j = z * NY + y
                table[j, j] = table[j, self.ls + j] = -1
                if y + 1 < NY:
                    table[j + 1, j] = 1
                if z + 1 < self.nz:
                    table[j + NY, self.ls + j] = 1
        return table

    def modulus_table(self):
        table = np.zeros((self.nyb, self.ls, self.lanes), np.float32)
        for yb in range(self.nyb):
            for z in range(self.nz):
                for k in range(self.ry):
                    y = yb * self.ty - 1 + k
                    if 0 <= y < NY:
                        for c in range(3):
                            table[yb, z * NY + y, (c * self.nz + z) * self.ry + k] = 1
        return table


def picked(values, table, parts=3):
    total, rest = None, values
    for part in range(parts):
        head = rest.astype(BF16)
        product = jnp.dot(head, table, preferred_element_type=F32)
        total = product if total is None else total + product
        if part + 1 < parts:
            rest = rest - head.astype(F32)
    return total


def pick_into(out_ref, values_ref, table_ref, parts=3):
    width = table_ref.shape[1]
    chunk = width if width <= 1024 else 512
    for first in range(0, width, chunk):
        out_ref[:, first : first + chunk] = picked(
            values_ref[:, : table_ref.shape[0]], table_ref[:, first : first + chunk], parts
        )


def swap_quarters(parts):
    quarter = lax.broadcasted_iota(jnp.int32, parts[0].shape, 1) // NY
    swapped = []
    for j in range(4):
        total = parts[j]
        for i in range(4):
            if i != j:
                turned = pltpu.roll(parts[i], (i - j) % 4 * NY, 1)
                total = jnp.where(quarter == i, turned, total)
        swapped.append(total)
    return swapped


def strided(start, size, step):
    return pl.ds(start, size) if size == 1 or step == 1 else pl.ds(start, size, stride=step)


def store_moduli(plan, chaos_at, moduli_ref, msg_ref):
    quarter = lax.broadcasted_iota(jnp.int32, (1, 128), 1) // NY
    own = [moduli_ref[pl.ds(share * plan.per_share + chaos_at, 1), :] for share in range(plan.shares)]
    count, first = plan.shares * plan.rx, plan.sp * plan.rx
    for xb in range(plan.nxb):
        for start in range(0, count, 4):
            line = jnp.zeros((1, 128), F32)
            for number in range(start, min(count, start + 4)):
                share, k = divmod(number, plan.rx)
                x = xb * plan.tx - 1 + k
                if 0 <= x < NX:
                    piece = own[share][:, x // 4 * 128 : (x // 4 + 1) * 128]
                    turned = pltpu.roll(piece, (number - x) % 4 * NY, 1)
                    line = jnp.where(quarter == number % 4, turned, line)
            row, column = divmod(start // 4, plan.lanes // 128)
            for yb in range(plan.nyb):
                tile = xb * plan.nyb + yb
                msg_ref[tile, first + row : first + row + 1, column * 128 : (column + 1) * 128] = line


def gather_moduli(plan, tile_at, msg_ref, mtab_ref, mods_ref):
    quarter = lax.broadcasted_iota(jnp.int32, (plan.per_share, 128), 1) // NY
    first, rows = plan.sp * plan.rx, plan.rows_in
    table = mtab_ref[lax.rem(tile_at, plan.nyb)]
    mods_ref[...] = jnp.zeros(mods_ref.shape, F32)
    for share in range(plan.shares):
        lines = []
        for k in range(plan.rx):
            number = share * plan.rx + k
            row, column = divmod(number // 4, plan.lanes // 128)
            parts = []
            for t in range(plan.nz // 4):
                total = jnp.zeros((plan.per_share, 128), F32)
                for i in range(4):
                    at, columns = (4 * t + i) * rows + first + row, slice(column * 128, (column + 1) * 128)
                    if plan.lanes == 128:
                        piece = msg_ref[pl.ds(at, plan.per_share, stride=plan.slab * rows), columns]
                    else:
                        lone = [at + j * plan.slab * rows for j in range(plan.per_share)]
                        piece = jnp.concatenate([msg_ref[j : j + 1, columns] for j in lone], axis=0)
                    total = jnp.where(quarter == i, pltpu.roll(piece, (i - number) % 4 * NY, 1), total)
                parts.append(total)
            lines.append(parts[0] if len(parts) == 1 else jnp.concatenate(parts, axis=1))
        here = picked(jnp.concatenate(lines, axis=0), table)
        for k in range(plan.rx):
            for v in range(min(plan.per_share, FIELDS - share * plan.per_share)):
                at = k * plan.per_share + v
                mods_ref[share * plan.per_share + v, k : k + 1, :] = here[at : at + 1]


def store_message(plan, rows_ref, msg_ref):
    blank = jnp.zeros((8, plan.lanes), F32)
    for tile in range(plan.n):
        if tile >= plan.nxb * plan.nyb:
            msg_ref[tile] = jnp.zeros((plan.rows_in, plan.lanes), F32)
            continue
        xb, yb = divmod(tile, plan.nyb)
        msg_ref[tile, plan.rows_in - 8 :, :] = blank
        for k in range(plan.rx):
            x = xb * plan.tx - 1 + k
            if 0 <= x < NX:
                rows = rows_ref[
                    x * plan.hs : x * plan.hs + plan.sp, yb * plan.lanes : (yb + 1) * plan.lanes
                ]
            else:
                rows = jnp.zeros((plan.sp, plan.lanes), F32)
            msg_ref[tile, strided(k, plan.sp, plan.rx), :] = rows


def rows_at(piece_of):
    return [jnp.concatenate(pieces, axis=1) if len(pieces) > 1 else pieces[0] for pieces in zip(*piece_of)]


def start_kernel(plan, in_hbm, mean_hbm, modes_hbm, pack_hbm, msg_ref, lhs, rows, moduli, in_ref, mean_ref, modes_ref, pack_ref, arrived):
    pairs = ((in_hbm, in_ref), (pack_hbm, pack_ref), (mean_hbm, mean_ref), (modes_hbm, modes_ref))
    copies = [pltpu.make_async_copy(source, target, arrived.at[i]) for i, (source, target) in enumerate(pairs)]
    for copy in copies:
        copy.start()
    copies[0].wait()
    for a in range(PLANE // 128):
        for c in range(3):
            pieces = rows_at(
                swap_quarters(
                    [
                        in_ref[c, (4 * t + i) * plan.sp : (4 * t + i + 1) * plan.sp, a * 128 : (a + 1) * 128]
                        for i in range(4)
                    ]
                )
                for t in range(plan.slab // 4)
            )
            for b, piece in enumerate(pieces):
                x = 4 * a + b
                lhs[x * plan.hs : x * plan.hs + plan.sp, c * plan.ls : (c + 1) * plan.ls] = piece
    copies[1].wait()
    pick_into(rows, lhs, pack_ref)
    store_message(plan, rows, msg_ref)
    copies[2].wait()
    copies[3].wait()
    moduli[...] = jnp.zeros(moduli.shape, F32)
    for a in range(PLANE // 128):
        moduli[0:1, a * 128 : (a + 1) * 128] = mean_ref[a : a + 1, :]
    moduli[1:FIELDS] = modes_ref[...]
    store_moduli(plan, jnp.minimum(lax.axis_index("chaos"), plan.per_share - 1), moduli, msg_ref)


def split_kernel(plan, in_ref, mean_ref, *refs):
    out_refs, groups = refs[: plan.slab], refs[plan.slab]
    for group in range(plan.slab):
        step = lax.rem(group + plan.slab - lax.axis_index("slab"), plan.slab)
        for c in range(3):
            groups[step, c * plan.sp : (c + 1) * plan.sp, :] = in_ref[c, group * plan.sp : (group + 1) * plan.sp, :]
        groups[step, 3 * plan.sp : 3 * plan.sp + 1, :] = mean_ref[...]
    for step, out_ref in enumerate(out_refs):
        out_ref[...] = groups[step]


def load_kernel(plan, *refs):
    in_refs, (out_ref, mean_ref, planes) = refs[: plan.slab], refs[plan.slab :]
    for step, in_ref in enumerate(in_refs):
        planes[lax.rem(lax.axis_index("slab") + (plan.slab - step), plan.slab)] = in_ref[...]
    for a in range(PLANE // 128):
        lanes = slice(a * 128, (a + 1) * 128)
        pieces = rows_at(
            swap_quarters([planes[4 * t + i, 3 * plan.sp : 3 * plan.sp + 1, lanes] for i in range(4)])
            for t in range(plan.nz // 4)
        )
        for b, piece in enumerate(pieces):
            mean_ref[4 * a + b] = jnp.broadcast_to(piece, (plan.hs, plan.ls))
        for c in range(3):
            pieces = rows_at(
                swap_quarters([planes[4 * t + i, c * plan.sp : (c + 1) * plan.sp, lanes] for i in range(4)])
                for t in range(plan.nz // 4)
            )
            for b, piece in enumerate(pieces):
                out_ref[4 * a + b, c, 0 : plan.sp, :] = piece


def finish_kernel(plan, live_ref, start_ref, *refs):
    piece_refs, (total_ref, residual_ref, groups) = refs[: plan.slab], refs[plan.slab :]
    for step, piece_ref in enumerate(piece_refs):
        groups[lax.rem(lax.axis_index("slab") + (plan.slab - step), plan.slab)] = piece_ref[...]
    for group in range(plan.slab):
        here = slice(group * plan.sp, (group + 1) * plan.sp)
        live = jnp.broadcast_to(live_ref[here, :], (plan.sp, PLANE)) != 0.0
        for c in range(3):
            total_ref[c, here, :] = jnp.where(live, start_ref[c, here, :], 0.0) + groups[
                group, c * plan.sp : (c + 1) * plan.sp, :
            ]
            residual_ref[c, here, :] = groups[group, (3 + c) * plan.sp : (4 + c) * plan.sp, :]


def regrouped(plan, msg_ref, out_ref):
    lane = lax.broadcasted_iota(jnp.int32, (plan.rows_in, plan.lanes), 1)
    height = lane % (plan.nz * plan.ry) // plan.ry

    def one(row, carry):
        parts = [
            msg_ref[pl.ds(pl.multiple_of((row * plan.slab + z) * plan.rows_in, 8), plan.rows_in), :] for z in range(plan.nz)
        ]
        for group in range(plan.slab):
            total = parts[group]
            for z in range(plan.nz):
                if z != group:
                    turned = pltpu.roll(parts[z], (z - group) * plan.ry % plan.lanes, 1)
                    total = jnp.where(height == z, turned, total)
            out_ref[row * plan.slab + group] = total
        return carry

    lax.fori_loop(0, plan.chaos, one, 0, unroll=4)


def first_mix_kernel(plan, low_count, parts, nodes_ref, level_ref, msg_ref, mtab_ref, grad_ref, div_ref, out_ref, mods_ref, grad, flux, scaled, regroup):
    gather_moduli(plan, lax.axis_index("chaos") * plan.slab + lax.axis_index("slab"), msg_ref, mtab_ref, mods_ref)
    regrouped(plan, msg_ref, regroup)
    mix_kernel(plan, low_count, parts, nodes_ref, level_ref, regroup, mods_ref, grad_ref, div_ref, out_ref, grad, flux, scaled)


def mix_kernel(plan, low_count, parts, nodes_ref, level_ref, msg_ref, mods_ref, grad_ref, div_ref, out_ref, grad, flux, scaled):
    sp, rx, tx, lanes = plan.sp, plan.rx, plan.tx, plan.lanes
    for level in range(DEG):
        for v in range(KL):
            scaled[level * KL + v] = mods_ref[v + 1] * math.sqrt(level + 1)
    mean = mods_ref[0]

    def gradients(chunk, carry):
        windows, behind = [], []
        for i in range(4):
            source = chunk * 4 + i
            for s in range(sp):
                windows.append(msg_ref[source, s * rx : s * rx + 8, :])
                if s * rx + 9 <= plan.rows_in:
                    behind.append(msg_ref[source, s * rx + 1 : s * rx + 9, :])
                else:
                    behind.append(pltpu.roll(windows[-1], 7, 0))
        own = jnp.concatenate(windows, axis=0)
        slope_x = jnp.concatenate(behind, axis=0) - own
        full = picked(jnp.concatenate([own, slope_x], axis=1), grad_ref[...], parts)
        here = pl.ds(chunk * 4 * sp, 4 * sp)
        for d in range(3):
            part = full[:, d * lanes : (d + 1) * lanes].reshape(4 * sp, 8, lanes)
            grad[here, d] = part
            flux[here, d] = mean * part
        return carry

    lax.fori_loop(0, plan.n // 4, gradients, 0, unroll=8)

    def edges(number, carry):
        base = nodes_ref[number]
        own = [grad[base, d] for d in range(3)]
        total = [flux[base, d] for d in range(3)]
        for group in range(0, KL, 5):
            at = [nodes_ref[low_count + number * KL + v] for v in range(group, group + 5)]
            field = [scaled[level_ref[number * KL + v] * KL + v] for v in range(group, group + 5)]
            fresh = [
                [flux[spot, d] + weight * own[d] for d in range(3)] for spot, weight in zip(at, field)
            ]
            for spot, weight in zip(at, field):
                total = [total[d] + weight * grad[spot, d] for d in range(3)]
            for spot, values in zip(at, fresh):
                for d in range(3):
                    flux[spot, d] = values[d]
        for d in range(3):
            flux[base, d] = total[d]
        return carry

    lax.fori_loop(0, low_count, edges, 0, unroll=6)

    def divergences(chunk, carry):
        here = pl.ds(chunk * 4 * sp, 4 * sp)
        flux_x, flux_y, flux_z = (flux[here, d] for d in range(3))
        flux_x = flux_x - pltpu.roll(flux_x, 1, 1)
        values = jnp.concatenate([flux_x, flux_y, flux_z], axis=2).reshape(4 * sp * 8, 3 * lanes)
        total = picked(values, div_ref[...], parts).reshape(4, sp, 8, plan.lanes_out)
        for i in range(4):
            for s in range(plan.kept):
                out_ref[chunk * 4 + i, s * tx : (s + 1) * tx, :] = total[i, s, 1 : 1 + tx]
            for number in range(3 * plan.moved):
                slot, c = plan.kept + number // 3, number % 3
                turned = pltpu.roll(total[i, slot], (3 - c) * plan.segment, 1)
                out_ref[chunk * 4 + i, number * tx : (number + 1) * tx, 3 * plan.segment : 4 * plan.segment] = turned[
                    1 : 1 + tx, 3 * plan.segment : 4 * plan.segment
                ]
        return carry

    lax.fori_loop(0, plan.n // 4, divergences, 0, unroll=8)


def unpack_image(plan, image_ref, unpack_ref, lhs, rows, parts):
    for xb in range(plan.nxb):
        for k in range(plan.tx):
            x = xb * plan.tx + k
            for yb in range(plan.nyb):
                lhs[x * plan.hs : x * plan.hs + plan.kept, yb * plan.lanes_out : (yb + 1) * plan.lanes_out] = image_ref[
                    xb * plan.nyb + yb, strided(k, plan.kept, plan.tx), :
                ]
    pick_into(rows, lhs, unpack_ref, parts)


def add_image(plan, base_ref, live_ref, rows, residual_ref):
    live = live_ref[...] != 0.0
    slot = lax.broadcasted_iota(jnp.int32, (plan.hs, plan.ls), 0)

    def one(x, carry):
        block = rows.at[pl.ds(pl.multiple_of(x * plan.hs, plan.hs), plan.hs)]
        for c in range(3):
            image = block[:, c * plan.ls : (c + 1) * plan.ls]
            for q in range(plan.moved):
                line = block[3 * q + c : 3 * q + c + 1, 3 * plan.ls : 4 * plan.ls]
                image = jnp.where(slot == plan.kept + q, line, image)
            residual_ref[x, c] = jnp.where(live, base_ref[x, c] + image, 0.0)
        return carry

    lax.fori_loop(0, NX, one, 0, unroll=6)


def smooth(plan, mean_ref, slope_ref, back_ref, residual_ref, update, step):
    hs, ls, many = plan.hs, plan.ls, 6
    center_value = 0.5 * (bound_high + bound_low)
    half_width = 0.5 * (bound_high - bound_low)
    ratio_value = center_value / half_width

    def first(x, carry):
        for c in range(3):
            scaled = residual_ref[x, c] * (1.0 / center_value)
            update[x, c] = scaled
            step[x, c] = scaled
        return carry

    lax.fori_loop(0, NX, first, 0, unroll=6)
    update[NX] = jnp.zeros((3, hs, ls), F32)

    rho_prev = 1.0 / ratio_value
    for sweep in range(SWEEPS):
        rho_next = 1.0 / (2.0 * ratio_value - rho_prev)
        keep, gain = rho_next * rho_prev, 2.0 * rho_next / half_width

        def slabs_of(chunk, behind, keep=keep, gain=gain):
            here = pl.ds(chunk * many, many)
            own = update[here]
            slope_x = update[pl.ds(chunk * many + 1, many)] - own
            slopes = picked(own.reshape(many * 3 * hs, ls), slope_ref[...], 2)
            slopes = slopes.reshape(many, 3, hs, 2 * ls)
            modulus = mean_ref[here]
            spread = slope_x[:, 0] + slopes[:, 1, :, :ls] + slopes[:, 2, :, ls:]
            flux_x, flux_yz = [], []
            for c in range(3):
                parts = [slope_x[:, c], slopes[:, c, :, :ls], slopes[:, c, :, ls:]]
                parts[c] = parts[c] + spread
                flux_x.append(modulus * parts[0])
                flux_yz.append(jnp.concatenate([modulus * parts[1], modulus * parts[2]], axis=-1))
            flux_yz = jnp.stack(flux_yz, axis=1).reshape(many * 3 * hs, 2 * ls)
            back = picked(flux_yz, back_ref[...], 2).reshape(many, 3, hs, ls)
            for c in range(3):
                earlier = jnp.concatenate([behind[c][None], flux_x[c][:-1]], axis=0)
                total = flux_x[c] - earlier - back[:, c]
                moved = keep * step[here, c] + gain * (residual_ref[here, c] + total)
                step[here, c] = moved
                update[here, c] = own[:, c] + moved
            return tuple(flux[-1] for flux in flux_x)

        zero = jnp.zeros((hs, ls), F32)
        lax.fori_loop(0, NX // many, slabs_of, (zero, zero, zero), unroll=4)
        rho_prev = rho_next


def middle_kernel(plan, image_ref, base_ref, live_ref, mean_ref, slope_ref, back_ref, unpack_ref, pack_ref, msg_ref, residual_ref, update_ref, wide, narrow, step):
    unpack_image(plan, image_ref, unpack_ref, wide, narrow, 3)
    add_image(plan, base_ref, live_ref, narrow, residual_ref)
    smooth(plan, mean_ref, slope_ref, back_ref, residual_ref, update_ref, step)
    for x in range(NX):
        for c in range(3):
            narrow[x * plan.hs : (x + 1) * plan.hs, c * plan.ls : (c + 1) * plan.ls] = update_ref[x, c]
    pick_into(wide, narrow, pack_ref, 2)
    store_message(plan, wide, msg_ref)


def flat_rows(plan, values, out_ref, first, a):
    for t in range(plan.nz // 4):
        parts = [value[:, t * 128 : (t + 1) * 128] for value in values]
        for i, piece in enumerate(swap_quarters(parts)):
            out_ref[4 * t + i, first : first + plan.sp, a * 128 : (a + 1) * 128] = piece[: plan.sp]


def end_kernel(plan, image_ref, base_ref, live_ref, mean_ref, slope_ref, back_ref, unpack_ref, before_ref, *refs):
    out_refs, (wide, narrow, residual, update, step, planes) = refs[: plan.slab], refs[plan.slab :]
    unpack_image(plan, image_ref, unpack_ref, wide, narrow, 2)
    add_image(plan, base_ref, live_ref, narrow, residual)
    smooth(plan, mean_ref, slope_ref, back_ref, residual, update, step)
    for a in range(PLANE // 128):
        for c in range(3):
            flat_rows(plan, [update[4 * a + b, c] + before_ref[4 * a + b, c] for b in range(4)], planes, c * plan.sp, a)
            flat_rows(plan, [residual[4 * a + b, c] for b in range(4)], planes, (3 + c) * plan.sp, a)
    for number, out_ref in enumerate(out_refs):
        out_ref[...] = planes[lax.rem(lax.axis_index("slab") + number, plan.slab)]


def per_device(displacement, load, mean_modulus, modes, owner):
    chaos, slab = lax.axis_size("chaos"), lax.axis_size("slab")
    slots_dev, slots_all = displacement.shape[0], owner.shape[0]
    plan = Plan(chaos, slab, slots_dev)
    n, sp, hs, ls, lanes = plan.n, plan.sp, plan.hs, plan.ls, plan.lanes
    count, low, raised, level = edge_tables()
    at_chaos, at_slab = lax.axis_index("chaos"), lax.axis_index("slab")

    slots = np.arange(slots_all)
    places = (slots // slots_dev) * (slab * sp) + slots % slots_dev
    wanted = np.concatenate([low, raised])
    nodes = jnp.sum(
        jnp.where(wanted[:, None] == owner[None, :], jnp.asarray(places, jnp.int32)[None, :], 0), axis=1
    ).astype(jnp.int32)
    live_all = owner < count
    live_own = lax.dynamic_slice_in_dim(live_all, at_chaos * slots_dev, slots_dev, 0)
    live_here = jnp.pad(live_own.astype(F32), (0, slab * sp - slots_dev))
    live_here = lax.dynamic_slice_in_dim(live_here, at_slab * sp, sp, 0)
    live_here = jnp.broadcast_to(jnp.pad(live_here, (0, hs - sp))[:, None], (hs, ls))

    pack = jnp.asarray(plan.pack_table(), BF16)
    unpack = jnp.asarray(plan.unpack_table(), BF16)
    mtab = jnp.asarray(plan.modulus_table(), BF16)
    slopes, backs = (jnp.asarray(values, BF16) for values in (plan.slope_table(), plan.slope_table().T))
    grads, divs = (jnp.asarray(values, BF16) for values in (plan.gradient_table(), plan.divergence_table()))

    slots_pad = slab * sp

    def by_component(values):
        return jnp.pad(jnp.transpose(values, (1, 0, 2)), ((0, 0), (0, slots_pad - slots_dev), (0, 0)))

    def everyone(values):
        return lax.all_to_all(values, ("chaos", "slab"), 0, 0, tiled=True)

    def column(pieces):
        return [pieces[0]] + [
            lax.ppermute(pieces[step], "slab", [(z, (z + step) % slab) for z in range(slab)])
            for step in range(1, slab)
        ]

    smem = pl.BlockSpec(memory_space=pltpu.SMEM)
    vmem = pl.BlockSpec(memory_space=pltpu.VMEM)
    hbm = pl.BlockSpec(memory_space=pltpu.HBM)

    def call(kernel, name, in_specs, out_shape, scratch_shapes, grant=16 if n <= 64 else 60):
        return pl.pallas_call(
            kernel,
            out_shape=out_shape,
            in_specs=in_specs,
            out_specs=jax.tree.map(lambda _: vmem, out_shape),
            scratch_shapes=scratch_shapes,
            compiler_params=pltpu.CompilerParams(vmem_limit_bytes=grant * MIB),
            name=name,
        )

    def array(*shape):
        return jax.ShapeDtypeStruct(shape, F32)

    message, image = array(n, plan.rows_in, lanes), array(n, plan.rows_out, plan.lanes_out)
    grid_field, grid_more = array(NX, 3, hs, ls), array(NX + 1, 3, hs, ls)
    wide = pltpu.VMEM((NX * hs, plan.nyb * lanes), F32)
    narrow = pltpu.VMEM((NX * hs, plan.image_width), F32)
    field_scratch, more_scratch = pltpu.VMEM(grid_field.shape, F32), pltpu.VMEM(grid_more.shape, F32)

    mean_row = mean_modulus.reshape(1, PLANE)
    msg = call(
        functools.partial(start_kernel, plan),
        "start",
        [hbm, hbm, hbm, hbm],
        message,
        [
            narrow,
            wide,
            pltpu.VMEM((16, PLANE), F32),
            pltpu.VMEM((3, slots_pad, PLANE), F32),
            pltpu.VMEM((PLANE // 128, 128), F32),
            pltpu.VMEM((KL, PLANE), F32),
            pltpu.VMEM(pack.shape, BF16),
            pltpu.SemaphoreType.DMA((4,)),
        ],
        60,
    )(by_component(displacement), mean_modulus.reshape(PLANE // 128, 128), modes, pack)
    levels = jnp.asarray(level, jnp.int32)
    mix_scratch = [
        pltpu.VMEM((plan.positions, 3, 8, lanes), F32),
        pltpu.VMEM((plan.positions, 3, 8, lanes), F32),
        pltpu.VMEM((DEG * KL, 8, lanes), F32),
    ]

    arrived = everyone(msg)
    flat, parts = array(plan.rows_flat, PLANE), array(3, slots_pad, PLANE)
    load_flat = call(
        functools.partial(split_kernel, plan), "split", [vmem, vmem], (flat,) * slab, [pltpu.VMEM((slab, plan.rows_flat, PLANE), F32)]
    )(by_component(load), mean_row)
    load_flat = column(load_flat)
    arrived, nodes = lax.optimization_barrier((arrived, nodes))
    first_image, mods = call(
        functools.partial(first_mix_kernel, plan, len(low), 3),
        "mix",
        [smem, smem, vmem, vmem, vmem, vmem],
        (image, array(FIELDS, 8, lanes)),
        mix_scratch + [pltpu.VMEM((n, plan.rows_in, lanes), F32)],
    )(nodes, levels, arrived.reshape(n * plan.rows_in, lanes), mtab, grads, divs)
    load_flat, first_image = lax.optimization_barrier((load_flat, first_image))
    load_s, mean_s = call(
        functools.partial(load_kernel, plan),
        "load",
        [vmem] * slab,
        (grid_field, array(NX, hs, ls)),
        [pltpu.VMEM((slab, plan.rows_flat, PLANE), F32)],
    )(*load_flat)
    msg, residual_s, update_s = call(
        functools.partial(middle_kernel, plan),
        "middle",
        [vmem] * 8,
        (message, grid_field, grid_more),
        [wide, narrow, field_scratch],
    )(everyone(first_image), load_s, live_here, mean_s, slopes, backs, unpack, pack)

    second_image = call(
        functools.partial(mix_kernel, plan, len(low), 2), "mix", [smem, smem, vmem, vmem, vmem, vmem], image, mix_scratch
    )(nodes, levels, everyone(msg), mods, grads, divs)
    around = pltpu.VMEM((slab, plan.rows_end, PLANE), F32)
    ending = call(
        functools.partial(end_kernel, plan),
        "end",
        [vmem] * 8,
        (array(plan.rows_end, PLANE),) * slab,
        [wide, narrow, field_scratch, more_scratch, field_scratch, around],
    )(everyone(second_image), residual_s, live_here, mean_s, slopes, backs, unpack, update_s)
    live_pad = jnp.pad(live_own.astype(F32), (0, slots_pad - slots_dev))
    outs = call(functools.partial(finish_kernel, plan), "finish", [vmem] * (2 + slab), (parts, parts), [around])(
        live_pad[:, None], by_component(displacement), *column(ending)
    )
    return tuple(jnp.transpose(values, (1, 0, 2))[:slots_dev] for values in outs)


def solution(mesh):
    in_specs = (P("chaos", None, "slab"), P("chaos", None, "slab"), P("slab"), P(None, "slab"), P())
    out_specs = (P("chaos", None, "slab"), P("chaos", None, "slab"))
    return jax.shard_map(
        per_device, mesh=mesh, in_specs=in_specs, out_specs=out_specs, check_vma=False
    )
```

```python
import functools
import math

import jax
import jax.numpy as jnp
import numpy as np
from jax import lax
from jax.experimental import pallas as pl
from jax.experimental.pallas import tpu as pltpu
from jax.sharding import PartitionSpec as P

NX = 24
NY = 32
KL = 10
DEG = 3
SWEEPS = 4
PLANE = NX * NY
FIELDS = KL + 1

bound_high = 50.0
bound_low = 2.5
MIB = 1024 * 1024
F32 = jnp.float32
BF16 = jnp.bfloat16


def up8(count):
    return -(-count // 8) * 8


def multi_indices():
    listing = [[]]
    for variable in range(KL):
        extended_list = []
        for prefix in listing:
            for degree in range(DEG + 1 - sum(prefix)):
                extended_list.append(prefix + [degree])
        listing = extended_list
    return listing


def edge_tables():
    listing = multi_indices()
    lookup = {tuple(entry): number for number, entry in enumerate(listing)}
    low, raised, level = [], [], []
    for number, entry in enumerate(listing):
        if sum(entry) == DEG:
            continue
        low.append(number)
        for variable in range(KL):
            other = list(entry)
            other[variable] += 1
            raised.append(lookup[tuple(other)])
            level.append(entry[variable])
    return len(listing), np.array(low, np.int32), np.array(raised, np.int32), np.array(level, np.int32)


class Plan:
    def __init__(self, chaos, slab, slots_dev):
        self.chaos, self.slab, self.slots_dev = chaos, slab, slots_dev
        self.n = chaos * slab
        self.nz = slab
        self.sp = -(-slots_dev // slab)
        self.hs = up8(self.sp)
        self.ls = self.nz * NY
        best = None
        for tx in range(1, 7):
            for ty in range(1, NY + 1):
                if NX % tx or NY % ty or (NX // tx) * (NY // ty) > self.n:
                    continue
                lanes = -(-3 * self.nz * (ty + 2) // 128) * 128
                rows = up8((self.sp - 1) * (tx + 2) + 8)
                key = (-(NX // tx) * (NY // ty), rows * lanes)
                if best is None or key < best[0]:
                    best = (key, tx, ty, lanes, rows)
        _, self.tx, self.ty, self.lanes, self.rows_in = best
        self.rx = self.tx + 2
        self.ry = self.ty + 2
        self.nxb, self.nyb = NX // self.tx, NY // self.ty
        self.lanes_out = -(-3 * self.nz * self.ty // 128) * 128
        self.segment = self.nz * self.ty
        self.moved = self.sp // 4 if self.lanes_out >= 4 * self.segment else 0
        self.kept = self.sp - self.moved
        self.rows_out = up8(self.kept * self.tx)
        self.image_width = (4 if self.moved else 3) * self.ls
        self.rows_flat = up8(3 * self.sp + 1)
        self.rows_end = up8(6 * self.sp)
        self.shares = -(-FIELDS // min(chaos, 16))
        self.per_share = 16 // self.shares
        self.positions = self.n * self.sp

    def pack_table(self):
        table = np.zeros((3 * self.ls, self.nyb * self.lanes), np.float32)
        for c in range(3):
            for z in range(self.nz):
                for yb in range(self.nyb):
                    for k in range(self.ry):
                        y = yb * self.ty - 1 + k
                        if 0 <= y < NY:
                            table[
                                c * self.ls + z * NY + y,
                                yb * self.lanes + (c * self.nz + z) * self.ry + k,
                            ] = 1
        return table

    def unpack_table(self):
        table = np.zeros((self.nyb * self.lanes_out, self.image_width), np.float32)
        for c in range(self.image_width // self.ls):
            for z in range(self.nz):
                for y in range(NY):
                    yb, k = divmod(y, self.ty)
                    table[
                        yb * self.lanes_out + (c * self.nz + z) * self.ty + k, c * self.ls + z * NY + y
                    ] = 1
        return table

    def tile_lane(self, c, z, y):
        return (c * self.nz + z) * self.ry + y

    def gradient_table(self):
        table = np.zeros((2 * self.lanes, 3 * self.lanes), np.float32)
        at, wide = self.tile_lane, self.lanes

        def add(column, c, d, z, y, sign=1):
            if d == 0:
                table[wide + at(c, z, y), column] += 1
                return
            table[at(c, z, y), column] -= 1
            if d == 1 and y + 1 < self.ry:
                table[at(c, z, y + 1), column] += 1
            if d == 2 and z + 1 < self.nz:
                table[at(c, z + 1, y), column] += 1

        for z in range(self.nz):
            for y in range(self.ry):
                for c in range(3):
                    for d in range(3):
                        add(d * wide + at(c, z, y), c, d, z, y)
                        add(c * wide + at(c, z, y), d, d, z, y)
        return table

    def divergence_table(self):
        table = np.zeros((3 * self.lanes, self.lanes_out), np.float32)
        at, wide = self.tile_lane, self.lanes
        for c in range(3):
            for z in range(self.nz):
                for y in range(self.ty):
                    column = (c * self.nz + z) * self.ty + y
                    table[at(c, z, y + 1), column] = 1
                    table[wide + at(c, z, y + 1), column] = 1
                    table[wide + at(c, z, y), column] = -1
                    table[2 * wide + at(c, z, y + 1), column] = 1
                    if z:
                        table[2 * wide + at(c, z - 1, y + 1), column] = -1
        return table

    def slope_table(self):
        table = np.zeros((self.ls, 2 * self.ls), np.float32)
        for z in range(self.nz):
            for y in range(NY):
                j = z * NY + y
                table[j, j] = table[j, self.ls + j] = -1
                if y + 1 < NY:
                    table[j + 1, j] = 1
                if z + 1 < self.nz:
                    table[j + NY, self.ls + j] = 1
        return table

    def modulus_table(self):
        table = np.zeros((self.nyb, self.ls, self.lanes), np.float32)
        for yb in range(self.nyb):
            for z in range(self.nz):
                for k in range(self.ry):
                    y = yb * self.ty - 1 + k
                    if 0 <= y < NY:
                        for c in range(3):
                            table[yb, z * NY + y, (c * self.nz + z) * self.ry + k] = 1
        return table


def picked(values, table, parts=3):
    total, rest = None, values
    for part in range(parts):
        head = rest.astype(BF16)
        product = jnp.dot(head, table, preferred_element_type=F32)
        total = product if total is None else total + product
        if part + 1 < parts:
            rest = rest - head.astype(F32)
    return total


def pick_into(out_ref, values_ref, table_ref):
    width = table_ref.shape[1]
    chunk = width if width <= 1024 else 512
    for first in range(0, width, chunk):
        out_ref[:, first : first + chunk] = picked(
            values_ref[:, : table_ref.shape[0]], table_ref[:, first : first + chunk]
        )


def swap_quarters(parts):
    quarter = lax.broadcasted_iota(jnp.int32, parts[0].shape, 1) // NY
    swapped = []
    for j in range(4):
        total = parts[j]
        for i in range(4):
            if i != j:
                turned = pltpu.roll(parts[i], (i - j) % 4 * NY, 1)
                total = jnp.where(quarter == i, turned, total)
        swapped.append(total)
    return swapped


def strided(start, size, step):
    return pl.ds(start, size) if size == 1 or step == 1 else pl.ds(start, size, stride=step)


def store_moduli(plan, chaos_at, moduli_ref, msg_ref):
    quarter = lax.broadcasted_iota(jnp.int32, (1, 128), 1) // NY
    own = [moduli_ref[pl.ds(share * plan.per_share + chaos_at, 1), :] for share in range(plan.shares)]
    count, first = plan.shares * plan.rx, plan.sp * plan.rx
    for xb in range(plan.nxb):
        for start in range(0, count, 4):
            line = jnp.zeros((1, 128), F32)
            for number in range(start, min(count, start + 4)):
                share, k = divmod(number, plan.rx)
                x = xb * plan.tx - 1 + k
                if 0 <= x < NX:
                    piece = own[share][:, x // 4 * 128 : (x // 4 + 1) * 128]
                    turned = pltpu.roll(piece, (number - x) % 4 * NY, 1)
                    line = jnp.where(quarter == number % 4, turned, line)
            row, column = divmod(start // 4, plan.lanes // 128)
            for yb in range(plan.nyb):
                tile = xb * plan.nyb + yb
                msg_ref[tile, first + row : first + row + 1, column * 128 : (column + 1) * 128] = line


def gather_moduli(plan, tile_at, msg_ref, mtab_ref, mods_ref):
    quarter = lax.broadcasted_iota(jnp.int32, (plan.per_share, 128), 1) // NY
    first, rows = plan.sp * plan.rx, plan.rows_in
    table = mtab_ref[lax.rem(tile_at, plan.nyb)]
    mods_ref[...] = jnp.zeros(mods_ref.shape, F32)
    for share in range(plan.shares):
        lines = []
        for k in range(plan.rx):
            number = share * plan.rx + k
            row, column = divmod(number // 4, plan.lanes // 128)
            parts = []
            for t in range(plan.nz // 4):
                total = jnp.zeros((plan.per_share, 128), F32)
                for i in range(4):
                    at, columns = (4 * t + i) * rows + first + row, slice(column * 128, (column + 1) * 128)
                    if plan.lanes == 128:
                        piece = msg_ref[pl.ds(at, plan.per_share, stride=plan.slab * rows), columns]
                    else:
                        lone = [at + j * plan.slab * rows for j in range(plan.per_share)]
                        piece = jnp.concatenate([msg_ref[j : j + 1, columns] for j in lone], axis=0)
                    total = jnp.where(quarter == i, pltpu.roll(piece, (i - number) % 4 * NY, 1), total)
                parts.append(total)
            lines.append(parts[0] if len(parts) == 1 else jnp.concatenate(parts, axis=1))
        here = picked(jnp.concatenate(lines, axis=0), table)
        for k in range(plan.rx):
            for v in range(min(plan.per_share, FIELDS - share * plan.per_share)):
                at = k * plan.per_share + v
                mods_ref[share * plan.per_share + v, k : k + 1, :] = here[at : at + 1]


def store_message(plan, rows_ref, msg_ref):
    blank = jnp.zeros((8, plan.lanes), F32)
    for tile in range(plan.n):
        if tile >= plan.nxb * plan.nyb:
            msg_ref[tile] = jnp.zeros((plan.rows_in, plan.lanes), F32)
            continue
        xb, yb = divmod(tile, plan.nyb)
        msg_ref[tile, plan.rows_in - 8 :, :] = blank
        for k in range(plan.rx):
            x = xb * plan.tx - 1 + k
            if 0 <= x < NX:
                rows = rows_ref[
                    x * plan.hs : x * plan.hs + plan.sp, yb * plan.lanes : (yb + 1) * plan.lanes
                ]
            else:
                rows = jnp.zeros((plan.sp, plan.lanes), F32)
            msg_ref[tile, strided(k, plan.sp, plan.rx), :] = rows


def rows_at(piece_of):
    return [jnp.concatenate(pieces, axis=1) if len(pieces) > 1 else pieces[0] for pieces in zip(*piece_of)]


def start_kernel(plan, in_hbm, mean_hbm, modes_hbm, pack_hbm, msg_ref, lhs, rows, moduli, in_ref, mean_ref, modes_ref, pack_ref, arrived):
    pairs = ((in_hbm, in_ref), (pack_hbm, pack_ref), (mean_hbm, mean_ref), (modes_hbm, modes_ref))
    copies = [pltpu.make_async_copy(source, target, arrived.at[i]) for i, (source, target) in enumerate(pairs)]
    for copy in copies:
        copy.start()
    copies[0].wait()
    for a in range(PLANE // 128):
        for c in range(3):
            pieces = rows_at(
                swap_quarters(
                    [
                        in_ref[c, (4 * t + i) * plan.sp : (4 * t + i + 1) * plan.sp, a * 128 : (a + 1) * 128]
                        for i in range(4)
                    ]
                )
                for t in range(plan.slab // 4)
            )
            for b, piece in enumerate(pieces):
                x = 4 * a + b
                lhs[x * plan.hs : x * plan.hs + plan.sp, c * plan.ls : (c + 1) * plan.ls] = piece
    copies[1].wait()
    pick_into(rows, lhs, pack_ref)
    store_message(plan, rows, msg_ref)
    copies[2].wait()
    copies[3].wait()
    moduli[...] = jnp.zeros(moduli.shape, F32)
    for a in range(PLANE // 128):
        moduli[0:1, a * 128 : (a + 1) * 128] = mean_ref[a : a + 1, :]
    moduli[1:FIELDS] = modes_ref[...]
    store_moduli(plan, jnp.minimum(lax.axis_index("chaos"), plan.per_share - 1), moduli, msg_ref)


def split_kernel(plan, in_ref, mean_ref, *refs):
    out_refs, groups = refs[: plan.slab], refs[plan.slab]
    for group in range(plan.slab):
        step = lax.rem(group + plan.slab - lax.axis_index("slab"), plan.slab)
        for c in range(3):
            groups[step, c * plan.sp : (c + 1) * plan.sp, :] = in_ref[c, group * plan.sp : (group + 1) * plan.sp, :]
        groups[step, 3 * plan.sp : 3 * plan.sp + 1, :] = mean_ref[...]
    for step, out_ref in enumerate(out_refs):
        out_ref[...] = groups[step]


def load_kernel(plan, *refs):
    in_refs, (out_ref, mean_ref, planes) = refs[: plan.slab], refs[plan.slab :]
    for step, in_ref in enumerate(in_refs):
        planes[lax.rem(lax.axis_index("slab") + (plan.slab - step), plan.slab)] = in_ref[...]
    for a in range(PLANE // 128):
        lanes = slice(a * 128, (a + 1) * 128)
        pieces = rows_at(
            swap_quarters([planes[4 * t + i, 3 * plan.sp : 3 * plan.sp + 1, lanes] for i in range(4)])
            for t in range(plan.nz // 4)
        )
        for b, piece in enumerate(pieces):
            mean_ref[4 * a + b] = jnp.broadcast_to(piece, (plan.hs, plan.ls))
        for c in range(3):
            pieces = rows_at(
                swap_quarters([planes[4 * t + i, c * plan.sp : (c + 1) * plan.sp, lanes] for i in range(4)])
                for t in range(plan.nz // 4)
            )
            for b, piece in enumerate(pieces):
                out_ref[4 * a + b, c, 0 : plan.sp, :] = piece


def finish_kernel(plan, live_ref, start_ref, *refs):
    piece_refs, (total_ref, residual_ref, groups) = refs[: plan.slab], refs[plan.slab :]
    for step, piece_ref in enumerate(piece_refs):
        groups[lax.rem(lax.axis_index("slab") + (plan.slab - step), plan.slab)] = piece_ref[...]
    for group in range(plan.slab):
        here = slice(group * plan.sp, (group + 1) * plan.sp)
        live = jnp.broadcast_to(live_ref[here, :], (plan.sp, PLANE)) != 0.0
        for c in range(3):
            total_ref[c, here, :] = jnp.where(live, start_ref[c, here, :], 0.0) + groups[
                group, c * plan.sp : (c + 1) * plan.sp, :
            ]
            residual_ref[c, here, :] = groups[group, (3 + c) * plan.sp : (4 + c) * plan.sp, :]


def regrouped(plan, msg_ref, out_ref):
    lane = lax.broadcasted_iota(jnp.int32, (plan.rows_in, plan.lanes), 1)
    height = lane % (plan.nz * plan.ry) // plan.ry

    def one(row, carry):
        parts = [
            msg_ref[pl.ds(pl.multiple_of((row * plan.slab + z) * plan.rows_in, 8), plan.rows_in), :] for z in range(plan.nz)
        ]
        for group in range(plan.slab):
            total = parts[group]
            for z in range(plan.nz):
                if z != group:
                    turned = pltpu.roll(parts[z], (z - group) * plan.ry % plan.lanes, 1)
                    total = jnp.where(height == z, turned, total)
            out_ref[row * plan.slab + group] = total
        return carry

    lax.fori_loop(0, plan.chaos, one, 0, unroll=4)


def first_mix_kernel(plan, low_count, parts, nodes_ref, level_ref, msg_ref, mtab_ref, grad_ref, div_ref, out_ref, mods_ref, grad, flux, scaled, regroup):
    gather_moduli(plan, lax.axis_index("chaos") * plan.slab + lax.axis_index("slab"), msg_ref, mtab_ref, mods_ref)
    regrouped(plan, msg_ref, regroup)
    mix_kernel(plan, low_count, parts, nodes_ref, level_ref, regroup, mods_ref, grad_ref, div_ref, out_ref, grad, flux, scaled)


def mix_kernel(plan, low_count, parts, nodes_ref, level_ref, msg_ref, mods_ref, grad_ref, div_ref, out_ref, grad, flux, scaled):
    sp, rx, tx, lanes = plan.sp, plan.rx, plan.tx, plan.lanes
    for level in range(DEG):
        for v in range(KL):
            scaled[level * KL + v] = mods_ref[v + 1] * math.sqrt(level + 1)
    mean = mods_ref[0]

    def gradients(chunk, carry):
        windows, behind = [], []
        for i in range(4):
            source = chunk * 4 + i
            for s in range(sp):
                windows.append(msg_ref[source, s * rx : s * rx + 8, :])
                if s * rx + 9 <= plan.rows_in:
                    behind.append(msg_ref[source, s * rx + 1 : s * rx + 9, :])
                else:
                    behind.append(pltpu.roll(windows[-1], 7, 0))
        own = jnp.concatenate(windows, axis=0)
        slope_x = jnp.concatenate(behind, axis=0) - own
        full = picked(jnp.concatenate([own, slope_x], axis=1), grad_ref[...], parts)
        here = pl.ds(chunk * 4 * sp, 4 * sp)
        for d in range(3):
            part = full[:, d * lanes : (d + 1) * lanes].reshape(4 * sp, 8, lanes)
            grad[here, d] = part
            flux[here, d] = mean * part
        return carry

    lax.fori_loop(0, plan.n // 4, gradients, 0, unroll=8)

    def edges(number, carry):
        base = nodes_ref[number]
        own = [grad[base, d] for d in range(3)]
        total = [flux[base, d] for d in range(3)]
        for group in range(0, KL, 5):
            at = [nodes_ref[low_count + number * KL + v] for v in range(group, group + 5)]
            field = [scaled[level_ref[number * KL + v] * KL + v] for v in range(group, group + 5)]
            fresh = [
                [flux[spot, d] + weight * own[d] for d in range(3)] for spot, weight in zip(at, field)
            ]
            for spot, weight in zip(at, field):
                total = [total[d] + weight * grad[spot, d] for d in range(3)]
            for spot, values in zip(at, fresh):
                for d in range(3):
                    flux[spot, d] = values[d]
        for d in range(3):
            flux[base, d] = total[d]
        return carry

    lax.fori_loop(0, low_count, edges, 0, unroll=6)

    def divergences(chunk, carry):
        here = pl.ds(chunk * 4 * sp, 4 * sp)
        flux_x, flux_y, flux_z = (flux[here, d] for d in range(3))
        flux_x = flux_x - pltpu.roll(flux_x, 1, 1)
        values = jnp.concatenate([flux_x, flux_y, flux_z], axis=2).reshape(4 * sp * 8, 3 * lanes)
        total = picked(values, div_ref[...], parts).reshape(4, sp, 8, plan.lanes_out)
        for i in range(4):
            for s in range(plan.kept):
                out_ref[chunk * 4 + i, s * tx : (s + 1) * tx, :] = total[i, s, 1 : 1 + tx]
            for number in range(3 * plan.moved):
                slot, c = plan.kept + number // 3, number % 3
                turned = pltpu.roll(total[i, slot], (3 - c) * plan.segment, 1)
                out_ref[chunk * 4 + i, number * tx : (number + 1) * tx, 3 * plan.segment : 4 * plan.segment] = turned[
                    1 : 1 + tx, 3 * plan.segment : 4 * plan.segment
                ]
        return carry

    lax.fori_loop(0, plan.n // 4, divergences, 0, unroll=8)


def unpack_image(plan, image_ref, unpack_ref, lhs, rows):
    for xb in range(plan.nxb):
        for k in range(plan.tx):
            x = xb * plan.tx + k
            for yb in range(plan.nyb):
                lhs[x * plan.hs : x * plan.hs + plan.kept, yb * plan.lanes_out : (yb + 1) * plan.lanes_out] = image_ref[
                    xb * plan.nyb + yb, strided(k, plan.kept, plan.tx), :
                ]
    pick_into(rows, lhs, unpack_ref)


def add_image(plan, base_ref, live_ref, rows, residual_ref):
    live = live_ref[...] != 0.0
    slot = lax.broadcasted_iota(jnp.int32, (plan.hs, plan.ls), 0)

    def one(x, carry):
        block = rows.at[pl.ds(pl.multiple_of(x * plan.hs, plan.hs), plan.hs)]
        for c in range(3):
            image = block[:, c * plan.ls : (c + 1) * plan.ls]
            for q in range(plan.moved):
                line = block[3 * q + c : 3 * q + c + 1, 3 * plan.ls : 4 * plan.ls]
                image = jnp.where(slot == plan.kept + q, line, image)
            residual_ref[x, c] = jnp.where(live, base_ref[x, c] + image, 0.0)
        return carry

    lax.fori_loop(0, NX, one, 0, unroll=6)


def smooth(plan, mean_ref, slope_ref, back_ref, residual_ref, update, step):
    hs, ls, many = plan.hs, plan.ls, 6
    center_value = 0.5 * (bound_high + bound_low)
    half_width = 0.5 * (bound_high - bound_low)
    ratio_value = center_value / half_width

    def first(x, carry):
        for c in range(3):
            scaled = residual_ref[x, c] * (1.0 / center_value)
            update[x, c] = scaled
            step[x, c] = scaled
        return carry

    lax.fori_loop(0, NX, first, 0, unroll=6)
    update[NX] = jnp.zeros((3, hs, ls), F32)

    rho_prev = 1.0 / ratio_value
    for sweep in range(SWEEPS):
        rho_next = 1.0 / (2.0 * ratio_value - rho_prev)
        keep, gain = rho_next * rho_prev, 2.0 * rho_next / half_width

        def slabs_of(chunk, behind, keep=keep, gain=gain):
            here = pl.ds(chunk * many, many)
            own = update[here]
            slope_x = update[pl.ds(chunk * many + 1, many)] - own
            slopes = picked(own.reshape(many * 3 * hs, ls), slope_ref[...], 2)
            slopes = slopes.reshape(many, 3, hs, 2 * ls)
            modulus = mean_ref[here]
            spread = slope_x[:, 0] + slopes[:, 1, :, :ls] + slopes[:, 2, :, ls:]
            flux_x, flux_yz = [], []
            for c in range(3):
                parts = [slope_x[:, c], slopes[:, c, :, :ls], slopes[:, c, :, ls:]]
                parts[c] = parts[c] + spread
                flux_x.append(modulus * parts[0])
                flux_yz.append(jnp.concatenate([modulus * parts[1], modulus * parts[2]], axis=-1))
            flux_yz = jnp.stack(flux_yz, axis=1).reshape(many * 3 * hs, 2 * ls)
            back = picked(flux_yz, back_ref[...], 2).reshape(many, 3, hs, ls)
            for c in range(3):
                earlier = jnp.concatenate([behind[c][None], flux_x[c][:-1]], axis=0)
                total = flux_x[c] - earlier - back[:, c]
                moved = keep * step[here, c] + gain * (residual_ref[here, c] + total)
                step[here, c] = moved
                update[here, c] = own[:, c] + moved
            return tuple(flux[-1] for flux in flux_x)

        zero = jnp.zeros((hs, ls), F32)
        lax.fori_loop(0, NX // many, slabs_of, (zero, zero, zero), unroll=4)
        rho_prev = rho_next


def middle_kernel(plan, image_ref, base_ref, live_ref, mean_ref, slope_ref, back_ref, unpack_ref, pack_ref, msg_ref, residual_ref, update_ref, wide, narrow, step):
    unpack_image(plan, image_ref, unpack_ref, wide, narrow)
    add_image(plan, base_ref, live_ref, narrow, residual_ref)
    smooth(plan, mean_ref, slope_ref, back_ref, residual_ref, update_ref, step)
    for x in range(NX):
        for c in range(3):
            narrow[x * plan.hs : (x + 1) * plan.hs, c * plan.ls : (c + 1) * plan.ls] = update_ref[x, c]
    pick_into(wide, narrow, pack_ref)
    store_message(plan, wide, msg_ref)


def flat_rows(plan, values, out_ref, first, a):
    for t in range(plan.nz // 4):
        parts = [value[:, t * 128 : (t + 1) * 128] for value in values]
        for i, piece in enumerate(swap_quarters(parts)):
            out_ref[4 * t + i, first : first + plan.sp, a * 128 : (a + 1) * 128] = piece[: plan.sp]


def end_kernel(plan, image_ref, base_ref, live_ref, mean_ref, slope_ref, back_ref, unpack_ref, before_ref, *refs):
    out_refs, (wide, narrow, residual, update, step, planes) = refs[: plan.slab], refs[plan.slab :]
    unpack_image(plan, image_ref, unpack_ref, wide, narrow)
    add_image(plan, base_ref, live_ref, narrow, residual)
    smooth(plan, mean_ref, slope_ref, back_ref, residual, update, step)
    for a in range(PLANE // 128):
        for c in range(3):
            flat_rows(plan, [update[4 * a + b, c] + before_ref[4 * a + b, c] for b in range(4)], planes, c * plan.sp, a)
            flat_rows(plan, [residual[4 * a + b, c] for b in range(4)], planes, (3 + c) * plan.sp, a)
    for number, out_ref in enumerate(out_refs):
        out_ref[...] = planes[lax.rem(lax.axis_index("slab") + number, plan.slab)]


def per_device(displacement, load, mean_modulus, modes, owner):
    chaos, slab = lax.axis_size("chaos"), lax.axis_size("slab")
    slots_dev, slots_all = displacement.shape[0], owner.shape[0]
    plan = Plan(chaos, slab, slots_dev)
    n, sp, hs, ls, lanes = plan.n, plan.sp, plan.hs, plan.ls, plan.lanes
    count, low, raised, level = edge_tables()
    at_chaos, at_slab = lax.axis_index("chaos"), lax.axis_index("slab")

    slots = np.arange(slots_all)
    places = (slots // slots_dev) * (slab * sp) + slots % slots_dev
    wanted = np.concatenate([low, raised])
    nodes = jnp.sum(
        jnp.where(wanted[:, None] == owner[None, :], jnp.asarray(places, jnp.int32)[None, :], 0), axis=1
    ).astype(jnp.int32)
    live_all = owner < count
    live_own = lax.dynamic_slice_in_dim(live_all, at_chaos * slots_dev, slots_dev, 0)
    live_here = jnp.pad(live_own.astype(F32), (0, slab * sp - slots_dev))
    live_here = lax.dynamic_slice_in_dim(live_here, at_slab * sp, sp, 0)
    live_here = jnp.broadcast_to(jnp.pad(live_here, (0, hs - sp))[:, None], (hs, ls))

    pack = jnp.asarray(plan.pack_table(), BF16)
    unpack = jnp.asarray(plan.unpack_table(), BF16)
    mtab = jnp.asarray(plan.modulus_table(), BF16)
    slopes, backs = (jnp.asarray(values, BF16) for values in (plan.slope_table(), plan.slope_table().T))
    grads, divs = (jnp.asarray(values, BF16) for values in (plan.gradient_table(), plan.divergence_table()))

    slots_pad = slab * sp

    def by_component(values):
        return jnp.pad(jnp.transpose(values, (1, 0, 2)), ((0, 0), (0, slots_pad - slots_dev), (0, 0)))

    def everyone(values):
        return lax.all_to_all(values, ("chaos", "slab"), 0, 0, tiled=True)

    def column(pieces):
        return [pieces[0]] + [
            lax.ppermute(pieces[step], "slab", [(z, (z + step) % slab) for z in range(slab)])
            for step in range(1, slab)
        ]

    smem = pl.BlockSpec(memory_space=pltpu.SMEM)
    vmem = pl.BlockSpec(memory_space=pltpu.VMEM)
    hbm = pl.BlockSpec(memory_space=pltpu.HBM)

    def call(kernel, name, in_specs, out_shape, scratch_shapes, grant=16 if n <= 64 else 60):
        return pl.pallas_call(
            kernel,
            out_shape=out_shape,
            in_specs=in_specs,
            out_specs=jax.tree.map(lambda _: vmem, out_shape),
            scratch_shapes=scratch_shapes,
            compiler_params=pltpu.CompilerParams(vmem_limit_bytes=grant * MIB),
            name=name,
        )

    def array(*shape):
        return jax.ShapeDtypeStruct(shape, F32)

    message, image = array(n, plan.rows_in, lanes), array(n, plan.rows_out, plan.lanes_out)
    grid_field, grid_more = array(NX, 3, hs, ls), array(NX + 1, 3, hs, ls)
    wide = pltpu.VMEM((NX * hs, plan.nyb * lanes), F32)
    narrow = pltpu.VMEM((NX * hs, plan.image_width), F32)
    field_scratch, more_scratch = pltpu.VMEM(grid_field.shape, F32), pltpu.VMEM(grid_more.shape, F32)

    mean_row = mean_modulus.reshape(1, PLANE)
    msg = call(
        functools.partial(start_kernel, plan),
        "start",
        [hbm, hbm, hbm, hbm],
        message,
        [
            narrow,
            wide,
            pltpu.VMEM((16, PLANE), F32),
            pltpu.VMEM((3, slots_pad, PLANE), F32),
            pltpu.VMEM((PLANE // 128, 128), F32),
            pltpu.VMEM((KL, PLANE), F32),
            pltpu.VMEM(pack.shape, BF16),
            pltpu.SemaphoreType.DMA((4,)),
        ],
        60,
    )(by_component(displacement), mean_modulus.reshape(PLANE // 128, 128), modes, pack)
    levels = jnp.asarray(level, jnp.int32)
    mix_scratch = [
        pltpu.VMEM((plan.positions, 3, 8, lanes), F32),
        pltpu.VMEM((plan.positions, 3, 8, lanes), F32),
        pltpu.VMEM((DEG * KL, 8, lanes), F32),
    ]

    arrived = everyone(msg)
    flat, parts = array(plan.rows_flat, PLANE), array(3, slots_pad, PLANE)
    load_flat = call(
        functools.partial(split_kernel, plan), "split", [vmem, vmem], (flat,) * slab, [pltpu.VMEM((slab, plan.rows_flat, PLANE), F32)]
    )(by_component(load), mean_row)
    load_flat, arrived = lax.optimization_barrier((load_flat, arrived))
    load_flat = column(load_flat)
    arrived, nodes = lax.optimization_barrier((arrived, nodes))
    first_image, mods = call(
        functools.partial(first_mix_kernel, plan, len(low), 3),
        "mix",
        [smem, smem, vmem, vmem, vmem, vmem],
        (image, array(FIELDS, 8, lanes)),
        mix_scratch + [pltpu.VMEM((n, plan.rows_in, lanes), F32)],
    )(nodes, levels, arrived.reshape(n * plan.rows_in, lanes), mtab, grads, divs)
    load_flat, first_image = lax.optimization_barrier((load_flat, first_image))
    load_s, mean_s = call(
        functools.partial(load_kernel, plan),
        "load",
        [vmem] * slab,
        (grid_field, array(NX, hs, ls)),
        [pltpu.VMEM((slab, plan.rows_flat, PLANE), F32)],
    )(*load_flat)
    msg, residual_s, update_s = call(
        functools.partial(middle_kernel, plan),
        "middle",
        [vmem] * 8,
        (message, grid_field, grid_more),
        [wide, narrow, field_scratch],
    )(everyone(first_image), load_s, live_here, mean_s, slopes, backs, unpack, pack)

    second_image = call(
        functools.partial(mix_kernel, plan, len(low), 2), "mix", [smem, smem, vmem, vmem, vmem, vmem], image, mix_scratch
    )(nodes, levels, everyone(msg), mods, grads, divs)
    around = pltpu.VMEM((slab, plan.rows_end, PLANE), F32)
    ending = call(
        functools.partial(end_kernel, plan),
        "end",
        [vmem] * 8,
        (array(plan.rows_end, PLANE),) * slab,
        [wide, narrow, field_scratch, more_scratch, field_scratch, around],
    )(everyone(second_image), residual_s, live_here, mean_s, slopes, backs, unpack, update_s)
    live_pad = jnp.pad(live_own.astype(F32), (0, slots_pad - slots_dev))
    outs = call(functools.partial(finish_kernel, plan), "finish", [vmem] * (2 + slab), (parts, parts), [around])(
        live_pad[:, None], by_component(displacement), *column(ending)
    )
    return tuple(jnp.transpose(values, (1, 0, 2))[:slots_dev] for values in outs)


def solution(mesh):
    in_specs = (P("chaos", None, "slab"), P("chaos", None, "slab"), P("slab"), P(None, "slab"), P())
    out_specs = (P("chaos", None, "slab"), P("chaos", None, "slab"))
    return jax.shard_map(
        per_device, mesh=mesh, in_specs=in_specs, out_specs=out_specs, check_vma=False
    )
```

```python
import functools
import math

import jax
import jax.numpy as jnp
import numpy as np
from jax import lax
from jax.experimental import pallas as pl
from jax.experimental.pallas import tpu as pltpu
from jax.sharding import PartitionSpec as P

NX = 24
NY = 32
KL = 10
DEG = 3
SWEEPS = 4
PLANE = NX * NY
FIELDS = KL + 1

bound_high = 50.0
bound_low = 2.5
MIB = 1024 * 1024
F32 = jnp.float32
BF16 = jnp.bfloat16


def up8(count):
    return -(-count // 8) * 8


def multi_indices():
    listing = [[]]
    for variable in range(KL):
        extended_list = []
        for prefix in listing:
            for degree in range(DEG + 1 - sum(prefix)):
                extended_list.append(prefix + [degree])
        listing = extended_list
    return listing


def edge_tables():
    listing = multi_indices()
    lookup = {tuple(entry): number for number, entry in enumerate(listing)}
    low, raised, level = [], [], []
    for number, entry in enumerate(listing):
        if sum(entry) == DEG:
            continue
        low.append(number)
        for variable in range(KL):
            other = list(entry)
            other[variable] += 1
            raised.append(lookup[tuple(other)])
            level.append(entry[variable])
    return len(listing), np.array(low, np.int32), np.array(raised, np.int32), np.array(level, np.int32)


class Plan:
    def __init__(self, chaos, slab, slots_dev):
        self.chaos, self.slab, self.slots_dev = chaos, slab, slots_dev
        self.n = chaos * slab
        self.nz = slab
        self.sp = -(-slots_dev // slab)
        self.hs = up8(self.sp)
        self.ls = self.nz * NY
        best = None
        for tx in range(1, 7):
            for ty in range(1, NY + 1):
                if NX % tx or NY % ty or (NX // tx) * (NY // ty) > self.n:
                    continue
                lanes = -(-3 * self.nz * (ty + 2) // 128) * 128
                rows = up8((self.sp - 1) * (tx + 2) + 8)
                key = (-(NX // tx) * (NY // ty), rows * lanes)
                if best is None or key < best[0]:
                    best = (key, tx, ty, lanes, rows)
        _, self.tx, self.ty, self.lanes, self.rows_in = best
        self.rx = self.tx + 2
        self.ry = self.ty + 2
        self.nxb, self.nyb = NX // self.tx, NY // self.ty
        self.lanes_out = -(-3 * self.nz * self.ty // 128) * 128
        self.segment = self.nz * self.ty
        self.moved = self.sp // 4 if self.lanes_out >= 4 * self.segment else 0
        self.kept = self.sp - self.moved
        self.rows_out = up8(self.kept * self.tx)
        self.image_width = (4 if self.moved else 3) * self.ls
        self.rows_flat = up8(3 * self.sp + 1)
        self.rows_end = up8(6 * self.sp)
        self.shares = -(-FIELDS // min(chaos, 16))
        self.per_share = 16 // self.shares
        self.positions = self.n * self.sp

    def pack_table(self):
        table = np.zeros((3 * self.ls, self.nyb * self.lanes), np.float32)
        for c in range(3):
            for z in range(self.nz):
                for yb in range(self.nyb):
                    for k in range(self.ry):
                        y = yb * self.ty - 1 + k
                        if 0 <= y < NY:
                            table[
                                c * self.ls + z * NY + y,
                                yb * self.lanes + (c * self.nz + z) * self.ry + k,
                            ] = 1
        return table

    def unpack_table(self):
        table = np.zeros((self.nyb * self.lanes_out, self.image_width), np.float32)
        for c in range(self.image_width // self.ls):
            for z in range(self.nz):
                for y in range(NY):
                    yb, k = divmod(y, self.ty)
                    table[
                        yb * self.lanes_out + (c * self.nz + z) * self.ty + k, c * self.ls + z * NY + y
                    ] = 1
        return table

    def tile_lane(self, c, z, y):
        return (c * self.nz + z) * self.ry + y

    def gradient_table(self):
        table = np.zeros((2 * self.lanes, 3 * self.lanes), np.float32)
        at, wide = self.tile_lane, self.lanes

        def add(column, c, d, z, y, sign=1):
            if d == 0:
                table[wide + at(c, z, y), column] += 1
                return
            table[at(c, z, y), column] -= 1
            if d == 1 and y + 1 < self.ry:
                table[at(c, z, y + 1), column] += 1
            if d == 2 and z + 1 < self.nz:
                table[at(c, z + 1, y), column] += 1

        for z in range(self.nz):
            for y in range(self.ry):
                for c in range(3):
                    for d in range(3):
                        add(d * wide + at(c, z, y), c, d, z, y)
                        add(c * wide + at(c, z, y), d, d, z, y)
        return table

    def divergence_table(self):
        table = np.zeros((3 * self.lanes, self.lanes_out), np.float32)
        at, wide = self.tile_lane, self.lanes
        for c in range(3):
            for z in range(self.nz):
                for y in range(self.ty):
                    column = (c * self.nz + z) * self.ty + y
                    table[at(c, z, y + 1), column] = 1
                    table[wide + at(c, z, y + 1), column] = 1
                    table[wide + at(c, z, y), column] = -1
                    table[2 * wide + at(c, z, y + 1), column] = 1
                    if z:
                        table[2 * wide + at(c, z - 1, y + 1), column] = -1
        return table

    def slope_table(self):
        table = np.zeros((self.ls, 2 * self.ls), np.float32)
        for z in range(self.nz):
            for y in range(NY):
                j = z * NY + y
                table[j, j] = table[j, self.ls + j] = -1
                if y + 1 < NY:
                    table[j + 1, j] = 1
                if z + 1 < self.nz:
                    table[j + NY, self.ls + j] = 1
        return table

    def modulus_table(self):
        table = np.zeros((self.nyb, self.ls, self.lanes), np.float32)
        for yb in range(self.nyb):
            for z in range(self.nz):
                for k in range(self.ry):
                    y = yb * self.ty - 1 + k
                    if 0 <= y < NY:
                        for c in range(3):
                            table[yb, z * NY + y, (c * self.nz + z) * self.ry + k] = 1
        return table


def picked(values, table, parts=3):
    total, rest = None, values
    for part in range(parts):
        head = rest.astype(BF16)
        product = jnp.dot(head, table, preferred_element_type=F32)
        total = product if total is None else total + product
        if part + 1 < parts:
            rest = rest - head.astype(F32)
    return total


def pick_into(out_ref, values_ref, table_ref):
    width = table_ref.shape[1]
    chunk = width if width <= 1024 else 512
    for first in range(0, width, chunk):
        out_ref[:, first : first + chunk] = picked(
            values_ref[:, : table_ref.shape[0]], table_ref[:, first : first + chunk]
        )


def swap_quarters(parts):
    quarter = lax.broadcasted_iota(jnp.int32, parts[0].shape, 1) // NY
    swapped = []
    for j in range(4):
        total = parts[j]
        for i in range(4):
            if i != j:
                turned = pltpu.roll(parts[i], (i - j) % 4 * NY, 1)
                total = jnp.where(quarter == i, turned, total)
        swapped.append(total)
    return swapped


def strided(start, size, step):
    return pl.ds(start, size) if size == 1 or step == 1 else pl.ds(start, size, stride=step)


def store_moduli(plan, chaos_at, moduli_ref, msg_ref):
    quarter = lax.broadcasted_iota(jnp.int32, (1, 128), 1) // NY
    own = [moduli_ref[pl.ds(share * plan.per_share + chaos_at, 1), :] for share in range(plan.shares)]
    count, first = plan.shares * plan.rx, plan.sp * plan.rx
    for xb in range(plan.nxb):
        for start in range(0, count, 4):
            line = jnp.zeros((1, 128), F32)
            for number in range(start, min(count, start + 4)):
                share, k = divmod(number, plan.rx)
                x = xb * plan.tx - 1 + k
                if 0 <= x < NX:
                    piece = own[share][:, x // 4 * 128 : (x // 4 + 1) * 128]
                    turned = pltpu.roll(piece, (number - x) % 4 * NY, 1)
                    line = jnp.where(quarter == number % 4, turned, line)
            row, column = divmod(start // 4, plan.lanes // 128)
            for yb in range(plan.nyb):
                tile = xb * plan.nyb + yb
                msg_ref[tile, first + row : first + row + 1, column * 128 : (column + 1) * 128] = line


def gather_moduli(plan, tile_at, msg_ref, mtab_ref, mods_ref):
    quarter = lax.broadcasted_iota(jnp.int32, (plan.per_share, 128), 1) // NY
    first, rows = plan.sp * plan.rx, plan.rows_in
    table = mtab_ref[lax.rem(tile_at, plan.nyb)]
    mods_ref[...] = jnp.zeros(mods_ref.shape, F32)
    for share in range(plan.shares):
        lines = []
        for k in range(plan.rx):
            number = share * plan.rx + k
            row, column = divmod(number // 4, plan.lanes // 128)
            parts = []
            for t in range(plan.nz // 4):
                total = jnp.zeros((plan.per_share, 128), F32)
                for i in range(4):
                    at, columns = (4 * t + i) * rows + first + row, slice(column * 128, (column + 1) * 128)
                    if plan.lanes == 128:
                        piece = msg_ref[pl.ds(at, plan.per_share, stride=plan.slab * rows), columns]
                    else:
                        lone = [at + j * plan.slab * rows for j in range(plan.per_share)]
                        piece = jnp.concatenate([msg_ref[j : j + 1, columns] for j in lone], axis=0)
                    total = jnp.where(quarter == i, pltpu.roll(piece, (i - number) % 4 * NY, 1), total)
                parts.append(total)
            lines.append(parts[0] if len(parts) == 1 else jnp.concatenate(parts, axis=1))
        here = picked(jnp.concatenate(lines, axis=0), table)
        for k in range(plan.rx):
            for v in range(min(plan.per_share, FIELDS - share * plan.per_share)):
                at = k * plan.per_share + v
                mods_ref[share * plan.per_share + v, k : k + 1, :] = here[at : at + 1]


def store_message(plan, rows_ref, msg_ref):
    blank = jnp.zeros((8, plan.lanes), F32)
    for tile in range(plan.n):
        if tile >= plan.nxb * plan.nyb:
            msg_ref[tile] = jnp.zeros((plan.rows_in, plan.lanes), F32)
            continue
        xb, yb = divmod(tile, plan.nyb)
        msg_ref[tile, plan.rows_in - 8 :, :] = blank
        for k in range(plan.rx):
            x = xb * plan.tx - 1 + k
            if 0 <= x < NX:
                rows = rows_ref[
                    x * plan.hs : x * plan.hs + plan.sp, yb * plan.lanes : (yb + 1) * plan.lanes
                ]
            else:
                rows = jnp.zeros((plan.sp, plan.lanes), F32)
            msg_ref[tile, strided(k, plan.sp, plan.rx), :] = rows


def rows_at(piece_of):
    return [jnp.concatenate(pieces, axis=1) if len(pieces) > 1 else pieces[0] for pieces in zip(*piece_of)]


def start_kernel(plan, in_hbm, mean_hbm, modes_hbm, pack_hbm, msg_ref, lhs, rows, moduli, in_ref, mean_ref, modes_ref, pack_ref, arrived):
    pairs = ((in_hbm, in_ref), (pack_hbm, pack_ref), (mean_hbm, mean_ref), (modes_hbm, modes_ref))
    copies = [pltpu.make_async_copy(source, target, arrived.at[i]) for i, (source, target) in enumerate(pairs)]
    for copy in copies:
        copy.start()
    copies[0].wait()
    for a in range(PLANE // 128):
        for c in range(3):
            pieces = rows_at(
                swap_quarters(
                    [
                        in_ref[c, (4 * t + i) * plan.sp : (4 * t + i + 1) * plan.sp, a * 128 : (a + 1) * 128]
                        for i in range(4)
                    ]
                )
                for t in range(plan.slab // 4)
            )
            for b, piece in enumerate(pieces):
                x = 4 * a + b
                lhs[x * plan.hs : x * plan.hs + plan.sp, c * plan.ls : (c + 1) * plan.ls] = piece
    copies[1].wait()
    pick_into(rows, lhs, pack_ref)
    store_message(plan, rows, msg_ref)
    copies[2].wait()
    copies[3].wait()
    moduli[...] = jnp.zeros(moduli.shape, F32)
    for a in range(PLANE // 128):
        moduli[0:1, a * 128 : (a + 1) * 128] = mean_ref[a : a + 1, :]
    moduli[1:FIELDS] = modes_ref[...]
    store_moduli(plan, jnp.minimum(lax.axis_index("chaos"), plan.per_share - 1), moduli, msg_ref)


def split_kernel(plan, in_ref, mean_ref, *refs):
    out_refs, groups = refs[: plan.slab], refs[plan.slab]
    for group in range(plan.slab):
        step = lax.rem(group + plan.slab - lax.axis_index("slab"), plan.slab)
        for c in range(3):
            groups[step, c * plan.sp : (c + 1) * plan.sp, :] = in_ref[c, group * plan.sp : (group + 1) * plan.sp, :]
        groups[step, 3 * plan.sp : 3 * plan.sp + 1, :] = mean_ref[...]
    for step, out_ref in enumerate(out_refs):
        out_ref[...] = groups[step]


def load_kernel(plan, *refs):
    in_refs, (out_ref, mean_ref, planes) = refs[: plan.slab], refs[plan.slab :]
    for step, in_ref in enumerate(in_refs):
        planes[lax.rem(lax.axis_index("slab") + (plan.slab - step), plan.slab)] = in_ref[...]
    for a in range(PLANE // 128):
        lanes = slice(a * 128, (a + 1) * 128)
        pieces = rows_at(
            swap_quarters([planes[4 * t + i, 3 * plan.sp : 3 * plan.sp + 1, lanes] for i in range(4)])
            for t in range(plan.nz // 4)
        )
        for b, piece in enumerate(pieces):
            mean_ref[4 * a + b] = jnp.broadcast_to(piece, (plan.hs, plan.ls))
        for c in range(3):
            pieces = rows_at(
                swap_quarters([planes[4 * t + i, c * plan.sp : (c + 1) * plan.sp, lanes] for i in range(4)])
                for t in range(plan.nz // 4)
            )
            for b, piece in enumerate(pieces):
                out_ref[4 * a + b, c, 0 : plan.sp, :] = piece


def finish_kernel(plan, live_ref, start_ref, *refs):
    piece_refs, (total_ref, residual_ref, groups) = refs[: plan.slab], refs[plan.slab :]
    for step, piece_ref in enumerate(piece_refs):
        groups[lax.rem(lax.axis_index("slab") + (plan.slab - step), plan.slab)] = piece_ref[...]
    for group in range(plan.slab):
        here = slice(group * plan.sp, (group + 1) * plan.sp)
        live = jnp.broadcast_to(live_ref[here, :], (plan.sp, PLANE)) != 0.0
        for c in range(3):
            total_ref[c, here, :] = jnp.where(live, start_ref[c, here, :], 0.0) + groups[
                group, c * plan.sp : (c + 1) * plan.sp, :
            ]
            residual_ref[c, here, :] = groups[group, (3 + c) * plan.sp : (4 + c) * plan.sp, :]


def regrouped(plan, msg_ref, out_ref):
    lane = lax.broadcasted_iota(jnp.int32, (plan.rows_in, plan.lanes), 1)
    height = lane % (plan.nz * plan.ry) // plan.ry

    def one(row, carry):
        parts = [
            msg_ref[pl.ds(pl.multiple_of((row * plan.slab + z) * plan.rows_in, 8), plan.rows_in), :] for z in range(plan.nz)
        ]
        for group in range(plan.slab):
            total = parts[group]
            for z in range(plan.nz):
                if z != group:
                    turned = pltpu.roll(parts[z], (z - group) * plan.ry % plan.lanes, 1)
                    total = jnp.where(height == z, turned, total)
            out_ref[row * plan.slab + group] = total
        return carry

    lax.fori_loop(0, plan.chaos, one, 0, unroll=4)


def first_mix_kernel(plan, low_count, parts, nodes_ref, level_ref, msg_ref, mtab_ref, grad_ref, div_ref, out_ref, mods_ref, grad, flux, scaled, regroup):
    gather_moduli(plan, lax.axis_index("chaos") * plan.slab + lax.axis_index("slab"), msg_ref, mtab_ref, mods_ref)
    regrouped(plan, msg_ref, regroup)
    mix_kernel(plan, low_count, parts, nodes_ref, level_ref, regroup, mods_ref, grad_ref, div_ref, out_ref, grad, flux, scaled)


def mix_kernel(plan, low_count, parts, nodes_ref, level_ref, msg_ref, mods_ref, grad_ref, div_ref, out_ref, grad, flux, scaled):
    sp, rx, tx, lanes = plan.sp, plan.rx, plan.tx, plan.lanes
    for level in range(DEG):
        for v in range(KL):
            scaled[level * KL + v] = mods_ref[v + 1] * math.sqrt(level + 1)
    mean = mods_ref[0]

    def gradients(chunk, carry):
        windows, behind = [], []
        for i in range(4):
            source = chunk * 4 + i
            for s in range(sp):
                windows.append(msg_ref[source, s * rx : s * rx + 8, :])
                if s * rx + 9 <= plan.rows_in:
                    behind.append(msg_ref[source, s * rx + 1 : s * rx + 9, :])
                else:
                    behind.append(pltpu.roll(windows[-1], 7, 0))
        own = jnp.concatenate(windows, axis=0)
        slope_x = jnp.concatenate(behind, axis=0) - own
        full = picked(jnp.concatenate([own, slope_x], axis=1), grad_ref[...], parts)
        here = pl.ds(chunk * 4 * sp, 4 * sp)
        for d in range(3):
            part = full[:, d * lanes : (d + 1) * lanes].reshape(4 * sp, 8, lanes)
            grad[here, d] = part
            flux[here, d] = mean * part
        return carry

    lax.fori_loop(0, plan.n // 4, gradients, 0, unroll=8)

    def edges(number, carry):
        base = nodes_ref[number]
        own = [grad[base, d] for d in range(3)]
        total = [flux[base, d] for d in range(3)]
        for group in range(0, KL, 5):
            at = [nodes_ref[low_count + number * KL + v] for v in range(group, group + 5)]
            field = [scaled[level_ref[number * KL + v] * KL + v] for v in range(group, group + 5)]
            fresh = [
                [flux[spot, d] + weight * own[d] for d in range(3)] for spot, weight in zip(at, field)
            ]
            for spot, weight in zip(at, field):
                total = [total[d] + weight * grad[spot, d] for d in range(3)]
            for spot, values in zip(at, fresh):
                for d in range(3):
                    flux[spot, d] = values[d]
        for d in range(3):
            flux[base, d] = total[d]
        return carry

    lax.fori_loop(0, low_count, edges, 0, unroll=6)

    def divergences(chunk, carry):
        here = pl.ds(chunk * 4 * sp, 4 * sp)
        flux_x, flux_y, flux_z = (flux[here, d] for d in range(3))
        flux_x = flux_x - pltpu.roll(flux_x, 1, 1)
        values = jnp.concatenate([flux_x, flux_y, flux_z], axis=2).reshape(4 * sp * 8, 3 * lanes)
        total = picked(values, div_ref[...], parts).reshape(4, sp, 8, plan.lanes_out)
        for i in range(4):
            for s in range(plan.kept):
                out_ref[chunk * 4 + i, s * tx : (s + 1) * tx, :] = total[i, s, 1 : 1 + tx]
            for number in range(3 * plan.moved):
                slot, c = plan.kept + number // 3, number % 3
                turned = pltpu.roll(total[i, slot], (3 - c) * plan.segment, 1)
                out_ref[chunk * 4 + i, number * tx : (number + 1) * tx, 3 * plan.segment : 4 * plan.segment] = turned[
                    1 : 1 + tx, 3 * plan.segment : 4 * plan.segment
                ]
        return carry

    lax.fori_loop(0, plan.n // 4, divergences, 0, unroll=8)


def unpack_image(plan, image_ref, unpack_ref, lhs, rows):
    for xb in range(plan.nxb):
        for k in range(plan.tx):
            x = xb * plan.tx + k
            for yb in range(plan.nyb):
                lhs[x * plan.hs : x * plan.hs + plan.kept, yb * plan.lanes_out : (yb + 1) * plan.lanes_out] = image_ref[
                    xb * plan.nyb + yb, strided(k, plan.kept, plan.tx), :
                ]
    pick_into(rows, lhs, unpack_ref)


def add_image(plan, base_ref, live_ref, rows, residual_ref):
    live = live_ref[...] != 0.0
    slot = lax.broadcasted_iota(jnp.int32, (plan.hs, plan.ls), 0)

    def one(x, carry):
        block = rows.at[pl.ds(pl.multiple_of(x * plan.hs, plan.hs), plan.hs)]
        for c in range(3):
            image = block[:, c * plan.ls : (c + 1) * plan.ls]
            for q in range(plan.moved):
                line = block[3 * q + c : 3 * q + c + 1, 3 * plan.ls : 4 * plan.ls]
                image = jnp.where(slot == plan.kept + q, line, image)
            residual_ref[x, c] = jnp.where(live, base_ref[x, c] + image, 0.0)
        return carry

    lax.fori_loop(0, NX, one, 0, unroll=6)


def smooth(plan, mean_ref, slope_ref, back_ref, residual_ref, update, step):
    hs, ls, many = plan.hs, plan.ls, 6
    center_value = 0.5 * (bound_high + bound_low)
    half_width = 0.5 * (bound_high - bound_low)
    ratio_value = center_value / half_width

    def first(x, carry):
        for c in range(3):
            scaled = residual_ref[x, c] * (1.0 / center_value)
            update[x, c] = scaled
            step[x, c] = scaled
        return carry

    lax.fori_loop(0, NX, first, 0, unroll=6)
    update[NX] = jnp.zeros((3, hs, ls), F32)

    rho_prev = 1.0 / ratio_value
    for sweep in range(SWEEPS):
        rho_next = 1.0 / (2.0 * ratio_value - rho_prev)
        keep, gain = rho_next * rho_prev, 2.0 * rho_next / half_width

        def slabs_of(chunk, behind, keep=keep, gain=gain):
            here = pl.ds(chunk * many, many)
            own = update[here]
            slope_x = update[pl.ds(chunk * many + 1, many)] - own
            slopes = picked(own.reshape(many * 3 * hs, ls), slope_ref[...], 2)
            slopes = slopes.reshape(many, 3, hs, 2 * ls)
            modulus = mean_ref[here]
            spread = slope_x[:, 0] + slopes[:, 1, :, :ls] + slopes[:, 2, :, ls:]
            flux_x, flux_yz = [], []
            for c in range(3):
                parts = [slope_x[:, c], slopes[:, c, :, :ls], slopes[:, c, :, ls:]]
                parts[c] = parts[c] + spread
                flux_x.append(modulus * parts[0])
                flux_yz.append(jnp.concatenate([modulus * parts[1], modulus * parts[2]], axis=-1))
            flux_yz = jnp.stack(flux_yz, axis=1).reshape(many * 3 * hs, 2 * ls)
            back = picked(flux_yz, back_ref[...], 2).reshape(many, 3, hs, ls)
            for c in range(3):
                earlier = jnp.concatenate([behind[c][None], flux_x[c][:-1]], axis=0)
                total = flux_x[c] - earlier - back[:, c]
                moved = keep * step[here, c] + gain * (residual_ref[here, c] + total)
                step[here, c] = moved
                update[here, c] = own[:, c] + moved
            return tuple(flux[-1] for flux in flux_x)

        zero = jnp.zeros((hs, ls), F32)
        lax.fori_loop(0, NX // many, slabs_of, (zero, zero, zero), unroll=4)
        rho_prev = rho_next


def middle_kernel(plan, image_ref, base_ref, live_ref, mean_ref, slope_ref, back_ref, unpack_ref, pack_ref, msg_ref, residual_ref, update_ref, wide, narrow, step):
    unpack_image(plan, image_ref, unpack_ref, wide, narrow)
    add_image(plan, base_ref, live_ref, narrow, residual_ref)
    smooth(plan, mean_ref, slope_ref, back_ref, residual_ref, update_ref, step)
    for x in range(NX):
        for c in range(3):
            narrow[x * plan.hs : (x + 1) * plan.hs, c * plan.ls : (c + 1) * plan.ls] = update_ref[x, c]
    pick_into(wide, narrow, pack_ref)
    store_message(plan, wide, msg_ref)


def flat_rows(plan, values, out_ref, first, a):
    for t in range(plan.nz // 4):
        parts = [value[:, t * 128 : (t + 1) * 128] for value in values]
        for i, piece in enumerate(swap_quarters(parts)):
            out_ref[4 * t + i, first : first + plan.sp, a * 128 : (a + 1) * 128] = piece[: plan.sp]


def end_kernel(plan, image_ref, base_ref, live_ref, mean_ref, slope_ref, back_ref, unpack_ref, before_ref, *refs):
    out_refs, (wide, narrow, residual, update, step, planes) = refs[: plan.slab], refs[plan.slab :]
    unpack_image(plan, image_ref, unpack_ref, wide, narrow)
    add_image(plan, base_ref, live_ref, narrow, residual)
    smooth(plan, mean_ref, slope_ref, back_ref, residual, update, step)
    for a in range(PLANE // 128):
        for c in range(3):
            flat_rows(plan, [update[4 * a + b, c] + before_ref[4 * a + b, c] for b in range(4)], planes, c * plan.sp, a)
            flat_rows(plan, [residual[4 * a + b, c] for b in range(4)], planes, (3 + c) * plan.sp, a)
    for number, out_ref in enumerate(out_refs):
        out_ref[...] = planes[lax.rem(lax.axis_index("slab") + number, plan.slab)]


def per_device(displacement, load, mean_modulus, modes, owner):
    chaos, slab = lax.axis_size("chaos"), lax.axis_size("slab")
    slots_dev, slots_all = displacement.shape[0], owner.shape[0]
    plan = Plan(chaos, slab, slots_dev)
    n, sp, hs, ls, lanes = plan.n, plan.sp, plan.hs, plan.ls, plan.lanes
    count, low, raised, level = edge_tables()
    at_chaos, at_slab = lax.axis_index("chaos"), lax.axis_index("slab")

    slots = np.arange(slots_all)
    places = (slots // slots_dev) * (slab * sp) + slots % slots_dev
    wanted = np.concatenate([low, raised])
    nodes = jnp.sum(
        jnp.where(wanted[:, None] == owner[None, :], jnp.asarray(places, jnp.int32)[None, :], 0), axis=1
    ).astype(jnp.int32)
    live_all = owner < count
    live_own = lax.dynamic_slice_in_dim(live_all, at_chaos * slots_dev, slots_dev, 0)
    live_here = jnp.pad(live_own.astype(F32), (0, slab * sp - slots_dev))
    live_here = lax.dynamic_slice_in_dim(live_here, at_slab * sp, sp, 0)
    live_here = jnp.broadcast_to(jnp.pad(live_here, (0, hs - sp))[:, None], (hs, ls))

    pack = jnp.asarray(plan.pack_table(), BF16)
    unpack = jnp.asarray(plan.unpack_table(), BF16)
    mtab = jnp.asarray(plan.modulus_table(), BF16)
    slopes, backs = (jnp.asarray(values, BF16) for values in (plan.slope_table(), plan.slope_table().T))
    grads, divs = (jnp.asarray(values, BF16) for values in (plan.gradient_table(), plan.divergence_table()))

    slots_pad = slab * sp

    def by_component(values):
        return jnp.pad(jnp.transpose(values, (1, 0, 2)), ((0, 0), (0, slots_pad - slots_dev), (0, 0)))

    def everyone(values):
        return lax.all_to_all(values, ("chaos", "slab"), 0, 0, tiled=True)

    def column(pieces):
        return [pieces[0]] + [
            lax.ppermute(pieces[step], "slab", [(z, (z + step) % slab) for z in range(slab)])
            for step in range(1, slab)
        ]

    smem = pl.BlockSpec(memory_space=pltpu.SMEM)
    vmem = pl.BlockSpec(memory_space=pltpu.VMEM)
    hbm = pl.BlockSpec(memory_space=pltpu.HBM)

    def call(kernel, name, in_specs, out_shape, scratch_shapes, grant=16 if n <= 64 else 60):
        return pl.pallas_call(
            kernel,
            out_shape=out_shape,
            in_specs=in_specs,
            out_specs=jax.tree.map(lambda _: vmem, out_shape),
            scratch_shapes=scratch_shapes,
            compiler_params=pltpu.CompilerParams(vmem_limit_bytes=grant * MIB),
            name=name,
        )

    def array(*shape):
        return jax.ShapeDtypeStruct(shape, F32)

    message, image = array(n, plan.rows_in, lanes), array(n, plan.rows_out, plan.lanes_out)
    grid_field, grid_more = array(NX, 3, hs, ls), array(NX + 1, 3, hs, ls)
    wide = pltpu.VMEM((NX * hs, plan.nyb * lanes), F32)
    narrow = pltpu.VMEM((NX * hs, plan.image_width), F32)
    field_scratch, more_scratch = pltpu.VMEM(grid_field.shape, F32), pltpu.VMEM(grid_more.shape, F32)

    mean_row = mean_modulus.reshape(1, PLANE)
    msg = call(
        functools.partial(start_kernel, plan),
        "start",
        [hbm, hbm, hbm, hbm],
        message,
        [
            narrow,
            wide,
            pltpu.VMEM((16, PLANE), F32),
            pltpu.VMEM((3, slots_pad, PLANE), F32),
            pltpu.VMEM((PLANE // 128, 128), F32),
            pltpu.VMEM((KL, PLANE), F32),
            pltpu.VMEM(pack.shape, BF16),
            pltpu.SemaphoreType.DMA((4,)),
        ],
        60,
    )(by_component(displacement), mean_modulus.reshape(PLANE // 128, 128), modes, pack)
    levels = jnp.asarray(level, jnp.int32)
    mix_scratch = [
        pltpu.VMEM((plan.positions, 3, 8, lanes), F32),
        pltpu.VMEM((plan.positions, 3, 8, lanes), F32),
        pltpu.VMEM((DEG * KL, 8, lanes), F32),
    ]

    arrived = everyone(msg)
    flat, parts = array(plan.rows_flat, PLANE), array(3, slots_pad, PLANE)
    load_flat = call(
        functools.partial(split_kernel, plan), "split", [vmem, vmem], (flat,) * slab, [pltpu.VMEM((slab, plan.rows_flat, PLANE), F32)]
    )(by_component(load), mean_row)
    later, arrived = lax.optimization_barrier((load_flat[2:], arrived))
    load_flat = column([*load_flat[:2], *later])
    arrived, nodes = lax.optimization_barrier((arrived, nodes))
    first_image, mods = call(
        functools.partial(first_mix_kernel, plan, len(low), 3),
        "mix",
        [smem, smem, vmem, vmem, vmem, vmem],
        (image, array(FIELDS, 8, lanes)),
        mix_scratch + [pltpu.VMEM((n, plan.rows_in, lanes), F32)],
    )(nodes, levels, arrived.reshape(n * plan.rows_in, lanes), mtab, grads, divs)
    load_flat, first_image = lax.optimization_barrier((load_flat, first_image))
    load_s, mean_s = call(
        functools.partial(load_kernel, plan),
        "load",
        [vmem] * slab,
        (grid_field, array(NX, hs, ls)),
        [pltpu.VMEM((slab, plan.rows_flat, PLANE), F32)],
    )(*load_flat)
    msg, residual_s, update_s = call(
        functools.partial(middle_kernel, plan),
        "middle",
        [vmem] * 8,
        (message, grid_field, grid_more),
        [wide, narrow, field_scratch],
    )(everyone(first_image), load_s, live_here, mean_s, slopes, backs, unpack, pack)

    second_image = call(
        functools.partial(mix_kernel, plan, len(low), 2), "mix", [smem, smem, vmem, vmem, vmem, vmem], image, mix_scratch
    )(nodes, levels, everyone(msg), mods, grads, divs)
    around = pltpu.VMEM((slab, plan.rows_end, PLANE), F32)
    ending = call(
        functools.partial(end_kernel, plan),
        "end",
        [vmem] * 8,
        (array(plan.rows_end, PLANE),) * slab,
        [wide, narrow, field_scratch, more_scratch, field_scratch, around],
    )(everyone(second_image), residual_s, live_here, mean_s, slopes, backs, unpack, update_s)
    live_pad = jnp.pad(live_own.astype(F32), (0, slots_pad - slots_dev))
    outs = call(functools.partial(finish_kernel, plan), "finish", [vmem] * (2 + slab), (parts, parts), [around])(
        live_pad[:, None], by_component(displacement), *column(ending)
    )
    return tuple(jnp.transpose(values, (1, 0, 2))[:slots_dev] for values in outs)


def solution(mesh):
    in_specs = (P("chaos", None, "slab"), P("chaos", None, "slab"), P("slab"), P(None, "slab"), P())
    out_specs = (P("chaos", None, "slab"), P("chaos", None, "slab"))
    return jax.shard_map(
        per_device, mesh=mesh, in_specs=in_specs, out_specs=out_specs, check_vma=False
    )
```

```python
import functools
import math

import jax
import jax.numpy as jnp
import numpy as np
from jax import lax
from jax.experimental import pallas as pl
from jax.experimental.pallas import tpu as pltpu
from jax.sharding import PartitionSpec as P

NX = 24
NY = 32
KL = 10
DEG = 3
SWEEPS = 4
PLANE = NX * NY
FIELDS = KL + 1

bound_high = 50.0
bound_low = 2.5
MIB = 1024 * 1024
F32 = jnp.float32
BF16 = jnp.bfloat16


def up8(count):
    return -(-count // 8) * 8


def multi_indices():
    listing = [[]]
    for variable in range(KL):
        extended_list = []
        for prefix in listing:
            for degree in range(DEG + 1 - sum(prefix)):
                extended_list.append(prefix + [degree])
        listing = extended_list
    return listing


def edge_tables():
    listing = multi_indices()
    lookup = {tuple(entry): number for number, entry in enumerate(listing)}
    low, raised, level = [], [], []
    for number, entry in enumerate(listing):
        if sum(entry) == DEG:
            continue
        low.append(number)
        for variable in range(KL):
            other = list(entry)
            other[variable] += 1
            raised.append(lookup[tuple(other)])
            level.append(entry[variable])
    return len(listing), np.array(low, np.int32), np.array(raised, np.int32), np.array(level, np.int32)


class Plan:
    def __init__(self, chaos, slab, slots_dev):
        self.chaos, self.slab, self.slots_dev = chaos, slab, slots_dev
        self.n = chaos * slab
        self.nz = slab
        self.sp = -(-slots_dev // slab)
        self.hs = up8(self.sp)
        self.ls = self.nz * NY
        best = None
        for tx in range(1, 7):
            for ty in range(1, NY + 1):
                if NX % tx or NY % ty or (NX // tx) * (NY // ty) > self.n:
                    continue
                lanes = -(-3 * self.nz * (ty + 2) // 128) * 128
                rows = up8((self.sp - 1) * (tx + 2) + 8)
                key = (-(NX // tx) * (NY // ty), rows * lanes)
                if best is None or key < best[0]:
                    best = (key, tx, ty, lanes, rows)
        _, self.tx, self.ty, self.lanes, self.rows_in = best
        self.rx = self.tx + 2
        self.ry = self.ty + 2
        self.nxb, self.nyb = NX // self.tx, NY // self.ty
        self.lanes_out = -(-3 * self.nz * self.ty // 128) * 128
        self.segment = self.nz * self.ty
        self.moved = self.sp // 4 if self.lanes_out >= 4 * self.segment else 0
        self.kept = self.sp - self.moved
        self.rows_out = up8(self.kept * self.tx)
        self.image_width = (4 if self.moved else 3) * self.ls
        self.rows_flat = up8(3 * self.sp + 1)
        self.rows_end = up8(6 * self.sp)
        self.shares = -(-FIELDS // min(chaos, 16))
        self.per_share = 16 // self.shares
        self.positions = self.n * self.sp

    def pack_table(self):
        table = np.zeros((3 * self.ls, self.nyb * self.lanes), np.float32)
        for c in range(3):
            for z in range(self.nz):
                for yb in range(self.nyb):
                    for k in range(self.ry):
                        y = yb * self.ty - 1 + k
                        if 0 <= y < NY:
                            table[
                                c * self.ls + z * NY + y,
                                yb * self.lanes + (c * self.nz + z) * self.ry + k,
                            ] = 1
        return table

    def unpack_table(self):
        table = np.zeros((self.nyb * self.lanes_out, self.image_width), np.float32)
        for c in range(self.image_width // self.ls):
            for z in range(self.nz):
                for y in range(NY):
                    yb, k = divmod(y, self.ty)
                    table[
                        yb * self.lanes_out + (c * self.nz + z) * self.ty + k, c * self.ls + z * NY + y
                    ] = 1
        return table

    def tile_lane(self, c, z, y):
        return (c * self.nz + z) * self.ry + y

    def gradient_table(self):
        table = np.zeros((2 * self.lanes, 3 * self.lanes), np.float32)
        at, wide = self.tile_lane, self.lanes

        def add(column, c, d, z, y, sign=1):
            if d == 0:
                table[wide + at(c, z, y), column] += 1
                return
            table[at(c, z, y), column] -= 1
            if d == 1 and y + 1 < self.ry:
                table[at(c, z, y + 1), column] += 1
            if d == 2 and z + 1 < self.nz:
                table[at(c, z + 1, y), column] += 1

        for z in range(self.nz):
            for y in range(self.ry):
                for c in range(3):
                    for d in range(3):
                        add(d * wide + at(c, z, y), c, d, z, y)
                        add(c * wide + at(c, z, y), d, d, z, y)
        return table

    def divergence_table(self):
        table = np.zeros((3 * self.lanes, self.lanes_out), np.float32)
        at, wide = self.tile_lane, self.lanes
        for c in range(3):
            for z in range(self.nz):
                for y in range(self.ty):
                    column = (c * self.nz + z) * self.ty + y
                    table[at(c, z, y + 1), column] = 1
                    table[wide + at(c, z, y + 1), column] = 1
                    table[wide + at(c, z, y), column] = -1
                    table[2 * wide + at(c, z, y + 1), column] = 1
                    if z:
                        table[2 * wide + at(c, z - 1, y + 1), column] = -1
        return table

    def slope_table(self):
        table = np.zeros((self.ls, 2 * self.ls), np.float32)
        for z in range(self.nz):
            for y in range(NY):
                j = z * NY + y
                table[j, j] = table[j, self.ls + j] = -1
                if y + 1 < NY:
                    table[j + 1, j] = 1
                if z + 1 < self.nz:
                    table[j + NY, self.ls + j] = 1
        return table

    def regroup_table(self):
        wide = self.slab * self.lanes
        if wide > 1024:
            return np.zeros((8, 128), np.float32)
        table = np.zeros((wide, wide), np.float32)
        for c in range(3):
            for z in range(self.nz):
                for group in range(self.slab):
                    for y in range(self.ry):
                        table[
                            z * self.lanes + self.tile_lane(c, group, y), group * self.lanes + self.tile_lane(c, z, y)
                        ] = 1
        return table

    def modulus_table(self):
        table = np.zeros((self.nyb, self.ls, self.lanes), np.float32)
        for yb in range(self.nyb):
            for z in range(self.nz):
                for k in range(self.ry):
                    y = yb * self.ty - 1 + k
                    if 0 <= y < NY:
                        for c in range(3):
                            table[yb, z * NY + y, (c * self.nz + z) * self.ry + k] = 1
        return table


def picked(values, table, parts=3):
    total, rest = None, values
    for part in range(parts):
        head = rest.astype(BF16)
        product = jnp.dot(head, table, preferred_element_type=F32)
        total = product if total is None else total + product
        if part + 1 < parts:
            rest = rest - head.astype(F32)
    return total


def pick_into(out_ref, values_ref, table_ref, parts=3):
    width = table_ref.shape[1]
    chunk = width if width <= 1024 else 512
    for first in range(0, width, chunk):
        out_ref[:, first : first + chunk] = picked(
            values_ref[:, : table_ref.shape[0]], table_ref[:, first : first + chunk], parts
        )


def swap_quarters(parts):
    quarter = lax.broadcasted_iota(jnp.int32, parts[0].shape, 1) // NY
    swapped = []
    for j in range(4):
        total = parts[j]
        for i in range(4):
            if i != j:
                turned = pltpu.roll(parts[i], (i - j) % 4 * NY, 1)
                total = jnp.where(quarter == i, turned, total)
        swapped.append(total)
    return swapped


def strided(start, size, step):
    return pl.ds(start, size) if size == 1 or step == 1 else pl.ds(start, size, stride=step)


def store_moduli(plan, chaos_at, moduli_ref, msg_ref):
    quarter = lax.broadcasted_iota(jnp.int32, (1, 128), 1) // NY
    own = [moduli_ref[pl.ds(share * plan.per_share + chaos_at, 1), :] for share in range(plan.shares)]
    count, first = plan.shares * plan.rx, plan.sp * plan.rx
    for xb in range(plan.nxb):
        for start in range(0, count, 4):
            line = jnp.zeros((1, 128), F32)
            for number in range(start, min(count, start + 4)):
                share, k = divmod(number, plan.rx)
                x = xb * plan.tx - 1 + k
                if 0 <= x < NX:
                    piece = own[share][:, x // 4 * 128 : (x // 4 + 1) * 128]
                    turned = pltpu.roll(piece, (number - x) % 4 * NY, 1)
                    line = jnp.where(quarter == number % 4, turned, line)
            row, column = divmod(start // 4, plan.lanes // 128)
            for yb in range(plan.nyb):
                tile = xb * plan.nyb + yb
                msg_ref[tile, first + row : first + row + 1, column * 128 : (column + 1) * 128] = line


def gather_moduli(plan, tile_at, msg_ref, mtab_ref, mods_ref):
    quarter = lax.broadcasted_iota(jnp.int32, (plan.per_share, 128), 1) // NY
    first, rows = plan.sp * plan.rx, plan.rows_in
    table = mtab_ref[lax.rem(tile_at, plan.nyb)]
    mods_ref[...] = jnp.zeros(mods_ref.shape, F32)
    for share in range(plan.shares):
        lines = []
        for k in range(plan.rx):
            number = share * plan.rx + k
            row, column = divmod(number // 4, plan.lanes // 128)
            parts = []
            for t in range(plan.nz // 4):
                total = jnp.zeros((plan.per_share, 128), F32)
                for i in range(4):
                    at, columns = (4 * t + i) * rows + first + row, slice(column * 128, (column + 1) * 128)
                    if plan.lanes == 128:
                        piece = msg_ref[pl.ds(at, plan.per_share, stride=plan.slab * rows), columns]
                    else:
                        lone = [at + j * plan.slab * rows for j in range(plan.per_share)]
                        piece = jnp.concatenate([msg_ref[j : j + 1, columns] for j in lone], axis=0)
                    total = jnp.where(quarter == i, pltpu.roll(piece, (i - number) % 4 * NY, 1), total)
                parts.append(total)
            lines.append(parts[0] if len(parts) == 1 else jnp.concatenate(parts, axis=1))
        here = picked(jnp.concatenate(lines, axis=0), table)
        for k in range(plan.rx):
            for v in range(min(plan.per_share, FIELDS - share * plan.per_share)):
                at = k * plan.per_share + v
                mods_ref[share * plan.per_share + v, k : k + 1, :] = here[at : at + 1]


def store_message(plan, rows_ref, msg_ref):
    blank = jnp.zeros((8, plan.lanes), F32)
    for tile in range(plan.n):
        if tile >= plan.nxb * plan.nyb:
            msg_ref[tile] = jnp.zeros((plan.rows_in, plan.lanes), F32)
            continue
        xb, yb = divmod(tile, plan.nyb)
        msg_ref[tile, plan.rows_in - 8 :, :] = blank
        for k in range(plan.rx):
            x = xb * plan.tx - 1 + k
            if 0 <= x < NX:
                rows = rows_ref[
                    x * plan.hs : x * plan.hs + plan.sp, yb * plan.lanes : (yb + 1) * plan.lanes
                ]
            else:
                rows = jnp.zeros((plan.sp, plan.lanes), F32)
            msg_ref[tile, strided(k, plan.sp, plan.rx), :] = rows


def rows_at(piece_of):
    return [jnp.concatenate(pieces, axis=1) if len(pieces) > 1 else pieces[0] for pieces in zip(*piece_of)]


def start_kernel(plan, in_hbm, mean_hbm, modes_hbm, pack_hbm, msg_ref, lhs, rows, moduli, in_ref, mean_ref, modes_ref, pack_ref, arrived):
    pairs = ((in_hbm, in_ref), (pack_hbm, pack_ref), (mean_hbm, mean_ref), (modes_hbm, modes_ref))
    copies = [pltpu.make_async_copy(source, target, arrived.at[i]) for i, (source, target) in enumerate(pairs)]
    for copy in copies:
        copy.start()
    copies[0].wait()
    for a in range(PLANE // 128):
        for c in range(3):
            pieces = rows_at(
                swap_quarters(
                    [
                        in_ref[c, (4 * t + i) * plan.sp : (4 * t + i + 1) * plan.sp, a * 128 : (a + 1) * 128]
                        for i in range(4)
                    ]
                )
                for t in range(plan.slab // 4)
            )
            for b, piece in enumerate(pieces):
                x = 4 * a + b
                lhs[x * plan.hs : x * plan.hs + plan.sp, c * plan.ls : (c + 1) * plan.ls] = piece
    copies[1].wait()
    pick_into(rows, lhs, pack_ref)
    store_message(plan, rows, msg_ref)
    copies[2].wait()
    copies[3].wait()
    moduli[...] = jnp.zeros(moduli.shape, F32)
    for a in range(PLANE // 128):
        moduli[0:1, a * 128 : (a + 1) * 128] = mean_ref[a : a + 1, :]
    moduli[1:FIELDS] = modes_ref[...]
    store_moduli(plan, jnp.minimum(lax.axis_index("chaos"), plan.per_share - 1), moduli, msg_ref)


def split_kernel(plan, in_ref, mean_ref, *refs):
    out_refs, groups = refs[: plan.slab], refs[plan.slab]
    for group in range(plan.slab):
        step = lax.rem(group + plan.slab - lax.axis_index("slab"), plan.slab)
        for c in range(3):
            groups[step, c * plan.sp : (c + 1) * plan.sp, :] = in_ref[c, group * plan.sp : (group + 1) * plan.sp, :]
        groups[step, 3 * plan.sp : 3 * plan.sp + 1, :] = mean_ref[...]
    for step, out_ref in enumerate(out_refs):
        out_ref[...] = groups[step]


def load_kernel(plan, *refs):
    in_refs, (out_ref, mean_ref, planes) = refs[: plan.slab], refs[plan.slab :]
    for step, in_ref in enumerate(in_refs):
        planes[lax.rem(lax.axis_index("slab") + (plan.slab - step), plan.slab)] = in_ref[...]
    for a in range(PLANE // 128):
        lanes = slice(a * 128, (a + 1) * 128)
        pieces = rows_at(
            swap_quarters([planes[4 * t + i, 3 * plan.sp : 3 * plan.sp + 1, lanes] for i in range(4)])
            for t in range(plan.nz // 4)
        )
        for b, piece in enumerate(pieces):
            mean_ref[4 * a + b] = jnp.broadcast_to(piece, (plan.hs, plan.ls))
        for c in range(3):
            pieces = rows_at(
                swap_quarters([planes[4 * t + i, c * plan.sp : (c + 1) * plan.sp, lanes] for i in range(4)])
                for t in range(plan.nz // 4)
            )
            for b, piece in enumerate(pieces):
                out_ref[4 * a + b, c, 0 : plan.sp, :] = piece


def finish_kernel(plan, live_ref, start_ref, *refs):
    piece_refs, (total_ref, residual_ref, groups) = refs[: plan.slab], refs[plan.slab :]
    for step, piece_ref in enumerate(piece_refs):
        groups[lax.rem(lax.axis_index("slab") + (plan.slab - step), plan.slab)] = piece_ref[...]
    for group in range(plan.slab):
        here = slice(group * plan.sp, (group + 1) * plan.sp)
        live = jnp.broadcast_to(live_ref[here, :], (plan.sp, PLANE)) != 0.0
        for c in range(3):
            total_ref[c, here, :] = jnp.where(live, start_ref[c, here, :], 0.0) + groups[
                group, c * plan.sp : (c + 1) * plan.sp, :
            ]
            residual_ref[c, here, :] = groups[group, (3 + c) * plan.sp : (4 + c) * plan.sp, :]


def regrouped(plan, msg_ref, table_ref, out_ref):
    if table_ref.shape[0] == plan.slab * plan.lanes:
        many = 4 if plan.chaos % 4 == 0 else 1
        for first in range(0, plan.chaos, many):
            blocks = [
                jnp.concatenate(
                    [
                        msg_ref[pl.ds((row * plan.slab + z) * plan.rows_in, plan.rows_in), :]
                        for z in range(plan.nz)
                    ],
                    axis=1,
                )
                for row in range(first, first + many)
            ]
            moved = picked(jnp.concatenate(blocks, axis=0), table_ref[...])
            for i in range(many):
                for group in range(plan.slab):
                    out_ref[(first + i) * plan.slab + group] = moved[
                        i * plan.rows_in : (i + 1) * plan.rows_in, group * plan.lanes : (group + 1) * plan.lanes
                    ]
        return
    lane = lax.broadcasted_iota(jnp.int32, (plan.rows_in, plan.lanes), 1)
    height = lane % (plan.nz * plan.ry) // plan.ry

    def one(row, carry):
        parts = [
            msg_ref[pl.ds(pl.multiple_of((row * plan.slab + z) * plan.rows_in, 8), plan.rows_in), :] for z in range(plan.nz)
        ]
        for group in range(plan.slab):
            total = parts[group]
            for z in range(plan.nz):
                if z != group:
                    turned = pltpu.roll(parts[z], (z - group) * plan.ry % plan.lanes, 1)
                    total = jnp.where(height == z, turned, total)
            out_ref[row * plan.slab + group] = total
        return carry

    lax.fori_loop(0, plan.chaos, one, 0, unroll=4)


def first_mix_kernel(plan, low_count, parts, nodes_ref, level_ref, msg_ref, mtab_ref, regroup_ref, grad_ref, div_ref, out_ref, mods_ref, grad, flux, scaled, regroup):
    gather_moduli(plan, lax.axis_index("chaos") * plan.slab + lax.axis_index("slab"), msg_ref, mtab_ref, mods_ref)
    regrouped(plan, msg_ref, regroup_ref, regroup)
    mix_kernel(plan, low_count, parts, nodes_ref, level_ref, regroup, mods_ref, grad_ref, div_ref, out_ref, grad, flux, scaled)


def mix_kernel(plan, low_count, parts, nodes_ref, level_ref, msg_ref, mods_ref, grad_ref, div_ref, out_ref, grad, flux, scaled):
    sp, rx, tx, lanes = plan.sp, plan.rx, plan.tx, plan.lanes
    for level in range(DEG):
        for v in range(KL):
            scaled[level * KL + v] = mods_ref[v + 1] * math.sqrt(level + 1)
    mean = mods_ref[0]

    def gradients(chunk, carry):
        windows, behind = [], []
        for i in range(4):
            source = chunk * 4 + i
            for s in range(sp):
                windows.append(msg_ref[source, s * rx : s * rx + 8, :])
                if s * rx + 9 <= plan.rows_in:
                    behind.append(msg_ref[source, s * rx + 1 : s * rx + 9, :])
                else:
                    behind.append(pltpu.roll(windows[-1], 7, 0))
        own = jnp.concatenate(windows, axis=0)
        slope_x = jnp.concatenate(behind, axis=0) - own
        full = picked(jnp.concatenate([own, slope_x], axis=1), grad_ref[...], parts)
        here = pl.ds(chunk * 4 * sp, 4 * sp)
        for d in range(3):
            part = full[:, d * lanes : (d + 1) * lanes].reshape(4 * sp, 8, lanes)
            grad[here, d] = part
            flux[here, d] = mean * part
        return carry

    lax.fori_loop(0, plan.n // 4, gradients, 0, unroll=8)

    def edges(number, carry):
        base = nodes_ref[number]
        own = [grad[base, d] for d in range(3)]
        total = [flux[base, d] for d in range(3)]
        for group in range(0, KL, 5):
            at = [nodes_ref[low_count + number * KL + v] for v in range(group, group + 5)]
            field = [scaled[level_ref[number * KL + v] * KL + v] for v in range(group, group + 5)]
            fresh = [
                [flux[spot, d] + weight * own[d] for d in range(3)] for spot, weight in zip(at, field)
            ]
            for spot, weight in zip(at, field):
                total = [total[d] + weight * grad[spot, d] for d in range(3)]
            for spot, values in zip(at, fresh):
                for d in range(3):
                    flux[spot, d] = values[d]
        for d in range(3):
            flux[base, d] = total[d]
        return carry

    lax.fori_loop(0, low_count, edges, 0, unroll=6)

    def divergences(chunk, carry):
        here = pl.ds(chunk * 4 * sp, 4 * sp)
        flux_x, flux_y, flux_z = (flux[here, d] for d in range(3))
        flux_x = flux_x - pltpu.roll(flux_x, 1, 1)
        values = jnp.concatenate([flux_x, flux_y, flux_z], axis=2).reshape(4 * sp * 8, 3 * lanes)
        total = picked(values, div_ref[...], parts).reshape(4, sp, 8, plan.lanes_out)
        for i in range(4):
            for s in range(plan.kept):
                out_ref[chunk * 4 + i, s * tx : (s + 1) * tx, :] = total[i, s, 1 : 1 + tx]
            for number in range(3 * plan.moved):
                slot, c = plan.kept + number // 3, number % 3
                turned = pltpu.roll(total[i, slot], (3 - c) * plan.segment, 1)
                out_ref[chunk * 4 + i, number * tx : (number + 1) * tx, 3 * plan.segment : 4 * plan.segment] = turned[
                    1 : 1 + tx, 3 * plan.segment : 4 * plan.segment
                ]
        return carry

    lax.fori_loop(0, plan.n // 4, divergences, 0, unroll=8)


def unpack_image(plan, image_ref, unpack_ref, lhs, rows, parts):
    for xb in range(plan.nxb):
        for k in range(plan.tx):
            x = xb * plan.tx + k
            for yb in range(plan.nyb):
                lhs[x * plan.hs : x * plan.hs + plan.kept, yb * plan.lanes_out : (yb + 1) * plan.lanes_out] = image_ref[
                    xb * plan.nyb + yb, strided(k, plan.kept, plan.tx), :
                ]
    pick_into(rows, lhs, unpack_ref, parts)


def add_image(plan, base_ref, live_ref, rows, residual_ref):
    live = live_ref[...] != 0.0
    slot = lax.broadcasted_iota(jnp.int32, (plan.hs, plan.ls), 0)

    def one(x, carry):
        block = rows.at[pl.ds(pl.multiple_of(x * plan.hs, plan.hs), plan.hs)]
        for c in range(3):
            image = block[:, c * plan.ls : (c + 1) * plan.ls]
            for q in range(plan.moved):
                line = block[3 * q + c : 3 * q + c + 1, 3 * plan.ls : 4 * plan.ls]
                image = jnp.where(slot == plan.kept + q, line, image)
            residual_ref[x, c] = jnp.where(live, base_ref[x, c] + image, 0.0)
        return carry

    lax.fori_loop(0, NX, one, 0, unroll=6)


def smooth(plan, mean_ref, slope_ref, back_ref, residual_ref, update, step):
    hs, ls, many = plan.hs, plan.ls, 6
    center_value = 0.5 * (bound_high + bound_low)
    half_width = 0.5 * (bound_high - bound_low)
    ratio_value = center_value / half_width

    def first(x, carry):
        for c in range(3):
            scaled = residual_ref[x, c] * (1.0 / center_value)
            update[x, c] = scaled
            step[x, c] = scaled
        return carry

    lax.fori_loop(0, NX, first, 0, unroll=6)
    update[NX] = jnp.zeros((3, hs, ls), F32)

    rho_prev = 1.0 / ratio_value
    for sweep in range(SWEEPS):
        rho_next = 1.0 / (2.0 * ratio_value - rho_prev)
        keep, gain = rho_next * rho_prev, 2.0 * rho_next / half_width

        def slabs_of(chunk, behind, keep=keep, gain=gain):
            here = pl.ds(chunk * many, many)
            own = update[here]
            slope_x = update[pl.ds(chunk * many + 1, many)] - own
            slopes = picked(own.reshape(many * 3 * hs, ls), slope_ref[...], 2)
            slopes = slopes.reshape(many, 3, hs, 2 * ls)
            modulus = mean_ref[here]
            spread = slope_x[:, 0] + slopes[:, 1, :, :ls] + slopes[:, 2, :, ls:]
            flux_x, flux_yz = [], []
            for c in range(3):
                parts = [slope_x[:, c], slopes[:, c, :, :ls], slopes[:, c, :, ls:]]
                parts[c] = parts[c] + spread
                flux_x.append(modulus * parts[0])
                flux_yz.append(jnp.concatenate([modulus * parts[1], modulus * parts[2]], axis=-1))
            flux_yz = jnp.stack(flux_yz, axis=1).reshape(many * 3 * hs, 2 * ls)
            back = picked(flux_yz, back_ref[...], 2).reshape(many, 3, hs, ls)
            for c in range(3):
                earlier = jnp.concatenate([behind[c][None], flux_x[c][:-1]], axis=0)
                total = flux_x[c] - earlier - back[:, c]
                moved = keep * step[here, c] + gain * (residual_ref[here, c] + total)
                step[here, c] = moved
                update[here, c] = own[:, c] + moved
            return tuple(flux[-1] for flux in flux_x)

        zero = jnp.zeros((hs, ls), F32)
        lax.fori_loop(0, NX // many, slabs_of, (zero, zero, zero), unroll=4)
        rho_prev = rho_next


def middle_kernel(plan, image_ref, base_ref, live_ref, mean_ref, slope_ref, back_ref, unpack_ref, pack_ref, msg_ref, residual_ref, update_ref, wide, narrow, step):
    unpack_image(plan, image_ref, unpack_ref, wide, narrow, 3)
    add_image(plan, base_ref, live_ref, narrow, residual_ref)
    smooth(plan, mean_ref, slope_ref, back_ref, residual_ref, update_ref, step)
    for x in range(NX):
        for c in range(3):
            narrow[x * plan.hs : (x + 1) * plan.hs, c * plan.ls : (c + 1) * plan.ls] = update_ref[x, c]
    pick_into(wide, narrow, pack_ref, 2)
    store_message(plan, wide, msg_ref)


def flat_rows(plan, values, out_ref, first, a):
    for t in range(plan.nz // 4):
        parts = [value[:, t * 128 : (t + 1) * 128] for value in values]
        for i, piece in enumerate(swap_quarters(parts)):
            out_ref[4 * t + i, first : first + plan.sp, a * 128 : (a + 1) * 128] = piece[: plan.sp]


def end_kernel(plan, image_ref, base_ref, live_ref, mean_ref, slope_ref, back_ref, unpack_ref, before_ref, *refs):
    out_refs, (wide, narrow, residual, update, step, planes) = refs[: plan.slab], refs[plan.slab :]
    unpack_image(plan, image_ref, unpack_ref, wide, narrow, 2)
    add_image(plan, base_ref, live_ref, narrow, residual)
    smooth(plan, mean_ref, slope_ref, back_ref, residual, update, step)
    for a in range(PLANE // 128):
        for c in range(3):
            flat_rows(plan, [update[4 * a + b, c] + before_ref[4 * a + b, c] for b in range(4)], planes, c * plan.sp, a)
            flat_rows(plan, [residual[4 * a + b, c] for b in range(4)], planes, (3 + c) * plan.sp, a)
    for number, out_ref in enumerate(out_refs):
        out_ref[...] = planes[lax.rem(lax.axis_index("slab") + number, plan.slab)]


def per_device(displacement, load, mean_modulus, modes, owner):
    chaos, slab = lax.axis_size("chaos"), lax.axis_size("slab")
    slots_dev, slots_all = displacement.shape[0], owner.shape[0]
    plan = Plan(chaos, slab, slots_dev)
    n, sp, hs, ls, lanes = plan.n, plan.sp, plan.hs, plan.ls, plan.lanes
    count, low, raised, level = edge_tables()
    at_chaos, at_slab = lax.axis_index("chaos"), lax.axis_index("slab")

    slots = np.arange(slots_all)
    places = (slots // slots_dev) * (slab * sp) + slots % slots_dev
    wanted = np.concatenate([low, raised])
    nodes = jnp.sum(
        jnp.where(wanted[:, None] == owner[None, :], jnp.asarray(places, jnp.int32)[None, :], 0), axis=1
    ).astype(jnp.int32)
    live_all = owner < count
    live_own = lax.dynamic_slice_in_dim(live_all, at_chaos * slots_dev, slots_dev, 0)
    live_here = jnp.pad(live_own.astype(F32), (0, slab * sp - slots_dev))
    live_here = lax.dynamic_slice_in_dim(live_here, at_slab * sp, sp, 0)
    live_here = jnp.broadcast_to(jnp.pad(live_here, (0, hs - sp))[:, None], (hs, ls))

    pack = jnp.asarray(plan.pack_table(), BF16)
    unpack = jnp.asarray(plan.unpack_table(), BF16)
    mtab = jnp.asarray(plan.modulus_table(), BF16)
    slopes, backs = (jnp.asarray(values, BF16) for values in (plan.slope_table(), plan.slope_table().T))
    grads, divs = (jnp.asarray(values, BF16) for values in (plan.gradient_table(), plan.divergence_table()))

    slots_pad = slab * sp

    def by_component(values):
        return jnp.pad(jnp.transpose(values, (1, 0, 2)), ((0, 0), (0, slots_pad - slots_dev), (0, 0)))

    def everyone(values):
        return lax.all_to_all(values, ("chaos", "slab"), 0, 0, tiled=True)

    def column(pieces):
        return [pieces[0]] + [
            lax.ppermute(pieces[step], "slab", [(z, (z + step) % slab) for z in range(slab)])
            for step in range(1, slab)
        ]

    smem = pl.BlockSpec(memory_space=pltpu.SMEM)
    vmem = pl.BlockSpec(memory_space=pltpu.VMEM)
    hbm = pl.BlockSpec(memory_space=pltpu.HBM)

    def call(kernel, name, in_specs, out_shape, scratch_shapes, grant=16 if n <= 64 else 60):
        return pl.pallas_call(
            kernel,
            out_shape=out_shape,
            in_specs=in_specs,
            out_specs=jax.tree.map(lambda _: vmem, out_shape),
            scratch_shapes=scratch_shapes,
            compiler_params=pltpu.CompilerParams(vmem_limit_bytes=grant * MIB),
            name=name,
        )

    def array(*shape):
        return jax.ShapeDtypeStruct(shape, F32)

    message, image = array(n, plan.rows_in, lanes), array(n, plan.rows_out, plan.lanes_out)
    grid_field, grid_more = array(NX, 3, hs, ls), array(NX + 1, 3, hs, ls)
    wide = pltpu.VMEM((NX * hs, plan.nyb * lanes), F32)
    narrow = pltpu.VMEM((NX * hs, plan.image_width), F32)
    field_scratch, more_scratch = pltpu.VMEM(grid_field.shape, F32), pltpu.VMEM(grid_more.shape, F32)

    mean_row = mean_modulus.reshape(1, PLANE)
    msg = call(
        functools.partial(start_kernel, plan),
        "start",
        [hbm, hbm, hbm, hbm],
        message,
        [
            narrow,
            wide,
            pltpu.VMEM((16, PLANE), F32),
            pltpu.VMEM((3, slots_pad, PLANE), F32),
            pltpu.VMEM((PLANE // 128, 128), F32),
            pltpu.VMEM((KL, PLANE), F32),
            pltpu.VMEM(pack.shape, BF16),
            pltpu.SemaphoreType.DMA((4,)),
        ],
        60,
    )(by_component(displacement), mean_modulus.reshape(PLANE // 128, 128), modes, pack)
    levels = jnp.asarray(level, jnp.int32)
    mix_scratch = [
        pltpu.VMEM((plan.positions, 3, 8, lanes), F32),
        pltpu.VMEM((plan.positions, 3, 8, lanes), F32),
        pltpu.VMEM((DEG * KL, 8, lanes), F32),
    ]

    arrived = everyone(msg)
    flat, parts = array(plan.rows_flat, PLANE), array(3, slots_pad, PLANE)
    load_flat = call(
        functools.partial(split_kernel, plan), "split", [vmem, vmem], (flat,) * slab, [pltpu.VMEM((slab, plan.rows_flat, PLANE), F32)]
    )(by_component(load), mean_row)
    load_flat, arrived = lax.optimization_barrier((load_flat, arrived))
    load_flat = column(load_flat)
    arrived, nodes = lax.optimization_barrier((arrived, nodes))
    first_image, mods = call(
        functools.partial(first_mix_kernel, plan, len(low), 3),
        "mix",
        [smem, smem, vmem, vmem, vmem, vmem, vmem],
        (image, array(FIELDS, 8, lanes)),
        mix_scratch + [pltpu.VMEM((n, plan.rows_in, lanes), F32)],
    )(nodes, levels, arrived.reshape(n * plan.rows_in, lanes), mtab, jnp.asarray(plan.regroup_table(), BF16), grads, divs)
    load_flat, first_image = lax.optimization_barrier((load_flat, first_image))
    load_s, mean_s = call(
        functools.partial(load_kernel, plan),
        "load",
        [vmem] * slab,
        (grid_field, array(NX, hs, ls)),
        [pltpu.VMEM((slab, plan.rows_flat, PLANE), F32)],
    )(*load_flat)
    msg, residual_s, update_s = call(
        functools.partial(middle_kernel, plan),
        "middle",
        [vmem] * 8,
        (message, grid_field, grid_more),
        [wide, narrow, field_scratch],
    )(everyone(first_image), load_s, live_here, mean_s, slopes, backs, unpack, pack)

    second_image = call(
        functools.partial(mix_kernel, plan, len(low), 2), "mix", [smem, smem, vmem, vmem, vmem, vmem], image, mix_scratch
    )(nodes, levels, everyone(msg), mods, grads, divs)
    around = pltpu.VMEM((slab, plan.rows_end, PLANE), F32)
    ending = call(
        functools.partial(end_kernel, plan),
        "end",
        [vmem] * 8,
        (array(plan.rows_end, PLANE),) * slab,
        [wide, narrow, field_scratch, more_scratch, field_scratch, around],
    )(everyone(second_image), residual_s, live_here, mean_s, slopes, backs, unpack, update_s)
    live_pad = jnp.pad(live_own.astype(F32), (0, slots_pad - slots_dev))
    outs = call(functools.partial(finish_kernel, plan), "finish", [vmem] * (2 + slab), (parts, parts), [around])(
        live_pad[:, None], by_component(displacement), *column(ending)
    )
    return tuple(jnp.transpose(values, (1, 0, 2))[:slots_dev] for values in outs)


def solution(mesh):
    in_specs = (P("chaos", None, "slab"), P("chaos", None, "slab"), P("slab"), P(None, "slab"), P())
    out_specs = (P("chaos", None, "slab"), P("chaos", None, "slab"))
    return jax.shard_map(
        per_device, mesh=mesh, in_specs=in_specs, out_specs=out_specs, check_vma=False
    )
```
